128 devices in a mesh: group: 2 (over core), dev: 64 (over y, z, x).
Axes of the slice: x: 4, y: 4, z: 4, core: 2. Of those that a mesh axis runs over, the one named last changes fastest.
Arguments:
- tokens: bfloat16 [16384, 1024], P(('group', 'dev')), may hold values from -6 to 6
- cotangent: bfloat16 [16384, 1024], P(('group', 'dev')), may hold values from -6 to 6
- expert_ids: int32 [16384, 2], P(('group', 'dev')), may hold values from 0 to 63, as said below
- slot_ids: int32 [16384, 2], P(('group', 'dev')), may hold values from 0 to 7, as said below
- w_qkv: bfloat16 [1024, 3072], replicated, may hold values from -0.1875 to 0.1875
- w_proj: bfloat16 [1024, 1024], replicated, may hold values from -0.1875 to 0.1875
- w_router: bfloat16 [1024, 64], replicated, may hold values from -0.1875 to 0.1875
- w_in: bfloat16 [64, 1024, 4096], P('dev', None, 'group'), may hold values from -0.1875 to 0.1875
- w_out: bfloat16 [64, 4096, 1024], P('dev', 'group'), may hold values from -0.09375 to 0.09375
Outputs:
- layer_out: bfloat16 [16384, 1024], P(('group', 'dev'))
- grad_tokens: bfloat16 [16384, 1024], P(('group', 'dev'))
- grad_qkv: float32 [1024, 3072], P(('group', 'dev'))
- grad_proj: float32 [1024, 1024], P(('group', 'dev'))
- grad_router: float32 [1024, 64], P(('group', 'dev'))
- grad_w_in: bfloat16 [64, 1024, 4096], P('dev', None, 'group')
- grad_w_out: bfloat16 [64, 4096, 1024], P('dev', 'group')
The draws below stay inside these ranges and needn't reach their ends.
Inputs may be any that keep to these rules, and one draw needn't show every extreme that they name: `expert_ids`: the two experts of a token differ. Among the tokens of one clip, each expert is named at most 8 times, and exactly 8 times by some expert of every clip. `slot_ids`: among the choices of one clip that name the same expert, the slots are distinct and below the number of such choices.
All inputs are finite; a program needn't handle non-finite values.
Results may differ from the reference program's by a relative error of at most 0.025.
Values may be sent and summed in bfloat16 or wider, within the bound.
A program may use at most 192 MiB of HBM per device.

```python
import jax
import jax.numpy as jnp
from jax import lax

D = 1024
HEADS = 16
FF = 4096
TOK_DEV = 128
EXPERTS = 64
CAP = 8
TOKENS = 16384


def routing_table(key):
    clip_count = TOKENS // TOK_DEV
    repeat = 2 * TOK_DEV // EXPERTS
    position = jnp.arange(2 * TOK_DEV, dtype=jnp.int32)
    first_end = EXPERTS * repeat // 2
    second_end = 3 * EXPERTS * repeat // 4
    half_repeat = repeat // 2
    base_expert = jnp.where(position < first_end, position // (2 * repeat), jnp.where(position < second_end, EXPERTS // 4 + (position - first_end) // repeat, EXPERTS // 2 + (position - second_end) // half_repeat))
    base_slot = jnp.where(position < first_end, position % (2 * repeat), jnp.where(position < second_end, (position - first_end) % repeat, (position - second_end) % half_repeat))

    def clip_table(clip_key):
        label_key, order_key = jax.random.split(clip_key)
        relabel = jax.random.permutation(label_key, EXPERTS).astype(jnp.int32)
        order = jax.random.permutation(order_key, TOK_DEV).astype(jnp.int32)
        labels = relabel[base_expert]
        experts_pair = jnp.stack([labels[order], labels[order + TOK_DEV]], axis=1)
        slots_pair = jnp.stack([base_slot[order], base_slot[order + TOK_DEV]], axis=1)
        return (experts_pair, slots_pair)
    experts_all, slots_all = jax.vmap(clip_table)(jax.random.split(key, clip_count))
    return (experts_all.reshape(TOKENS, 2).astype(jnp.int32), slots_all.reshape(TOKENS, 2).astype(jnp.int32))


def draw_expert_ids(key, part):
    return routing_table(key)[0]


def draw_slot_ids(key, part):
    return routing_table(key)[1]


def level_of(stream_key, shape, cuts, low, high):
    def one(axis_at, blocks):
        draws = jax.random.uniform(jax.random.fold_in(jax.random.fold_in(stream_key, 6), axis_at), (blocks,), jnp.float32, low / len(cuts), high / len(cuts))
        return jnp.repeat(jnp.exp(draws), shape[axis_at] // blocks).reshape((-1,) + (1,) * (len(shape) - axis_at - 1))

    factor_of = one(*cuts[0])
    for cut in cuts[1:]:
        factor_of = factor_of * one(*cut)
    return factor_of


def noise(stream_key, dims, scale, limit, cuts=(), kind=jnp.bfloat16):
    gain = level_of(stream_key, dims, cuts, -0.22, 0.18) if cuts else 1.0
    values = jax.random.normal(stream_key, dims, jnp.float32) * scale * gain
    return jnp.minimum(jnp.maximum(values, -limit), limit).astype(kind)


def setup_inputs(seed: int = 0) -> dict:
    key_of = jax.random.split(jax.random.key(seed), 10)
    tokens = noise(key_of[0], (TOKENS, D), 1.0, 6.0, ((0, 128),))
    cotangent = noise(key_of[1], (TOKENS, D), 1.0, 6.0, ((0, 128),))
    expert_ids = draw_expert_ids(jax.random.fold_in(key_of[9], 71), 0)
    slot_ids = draw_slot_ids(jax.random.fold_in(key_of[9], 71), 0)
    w_qkv = noise(key_of[4], (D, 3 * D), D ** -0.5, 0.1875)
    w_proj = noise(key_of[5], (D, D), D ** -0.5, 0.1875)
    w_router = noise(key_of[6], (D, EXPERTS), D ** -0.5, 0.1875)
    w_in = noise(key_of[7], (EXPERTS, D, FF), D ** -0.5, 0.1875, ((0, 64), (2, 2)))
    w_out = noise(key_of[8], (EXPERTS, FF, D), FF ** -0.5, 0.09375, ((0, 64), (1, 2)))
    return {"tokens": tokens, "cotangent": cotangent, "expert_ids": expert_ids, "slot_ids": slot_ids, "w_qkv": w_qkv, "w_proj": w_proj, "w_router": w_router, "w_in": w_in, "w_out": w_out}


def layer_norm(values):
    center = values - lax.optimization_barrier(jnp.mean(values, axis=-1, keepdims=True))
    spread = lax.optimization_barrier(jnp.mean(center * center, axis=-1, keepdims=True))
    return center * lax.rsqrt(spread + 1e-05)

def attention_block(clip_rows, w_qkv, w_proj):
    count = clip_rows.shape[0]
    width = clip_rows.shape[1]
    head_size = width // HEADS
    normed = layer_norm(clip_rows.astype(jnp.float32)).astype(jnp.bfloat16)
    qkv = jnp.dot(normed, w_qkv, preferred_element_type=jnp.float32).astype(jnp.bfloat16)
    query = qkv[:, :width].reshape(count, HEADS, head_size).astype(jnp.float32)
    keys = qkv[:, width:2 * width].reshape(count, HEADS, head_size).astype(jnp.float32)
    values = qkv[:, 2 * width:].reshape(count, HEADS, head_size).astype(jnp.float32)
    scores = jnp.einsum('qhd,khd->hqk', query, keys) / jnp.sqrt(jnp.float32(head_size))
    probs = jax.nn.softmax(scores, axis=-1).astype(jnp.bfloat16)
    attended = jnp.einsum('hqk,khd->qhd', probs.astype(jnp.float32), values).astype(jnp.bfloat16)
    attended = attended.reshape(count, width)
    return clip_rows.astype(jnp.float32) + jnp.dot(attended, w_proj, preferred_element_type=jnp.float32)

def gelu_exact(values):
    return jax.nn.gelu(values, approximate=False)

def reference(tokens, cotangent, expert_ids, slot_ids, w_qkv, w_proj, w_router, w_in, w_out):
    width = tokens.shape[1]
    clip_count = TOKENS // TOK_DEV
    clips = tokens.reshape(clip_count, TOK_DEV, width)
    resid = lax.map(lambda clip: attention_block(clip, w_qkv, w_proj).astype(jnp.bfloat16), clips)
    resid = resid.reshape(TOKENS, width)
    resid_f = resid.astype(jnp.float32)
    normed, norm_pullback = jax.vjp(layer_norm, resid_f)
    normed_b = normed.astype(jnp.bfloat16)
    logits = jnp.dot(normed_b, w_router, preferred_element_type=jnp.float32)
    choice_hot = (expert_ids[:, :, None] == jnp.arange(EXPERTS, dtype=jnp.int32)[None, None, :]).astype(jnp.float32)
    picked = lax.optimization_barrier(jnp.sum(logits[:, None, :] * choice_hot, axis=-1))
    mixing = jax.nn.softmax(picked, axis=-1)
    clip_index = (jnp.arange(TOKENS, dtype=jnp.int32) // TOK_DEV).astype(jnp.int32)
    target = ((expert_ids * clip_count + clip_index[:, None]) * CAP + slot_ids).astype(jnp.int32)
    total_slots = EXPERTS * clip_count * CAP
    token_index = jnp.broadcast_to(jnp.arange(TOKENS, dtype=jnp.int32)[:, None], (TOKENS, 2))
    owner = jnp.zeros((total_slots,), jnp.int32).at[target.reshape(-1)].set(token_index.reshape(-1))
    filled = jnp.zeros((total_slots,), jnp.bfloat16).at[target.reshape(-1)].set(jnp.ones((2 * TOKENS,), jnp.bfloat16))
    slot_rows = (normed_b[owner] * filled[:, None]).reshape(EXPERTS, clip_count * CAP, width)

    def expert_forward(operands):
        rows, first, second = operands
        pre = jnp.dot(rows, first, preferred_element_type=jnp.float32)
        hidden = gelu_exact(pre).astype(jnp.bfloat16)
        return jnp.dot(hidden, second, preferred_element_type=jnp.float32).astype(jnp.bfloat16)
    expert_out = lax.map(expert_forward, (slot_rows, w_in, w_out)).reshape(total_slots, width)
    outputs_pair = expert_out[target]
    layer_out = (resid_f + lax.optimization_barrier(jnp.sum(mixing[:, :, None] * outputs_pair.astype(jnp.float32), axis=1))).astype(jnp.bfloat16)
    grad = cotangent.astype(jnp.float32)
    d_pair = (mixing[:, :, None] * grad[:, None, :]).astype(jnp.bfloat16)
    d_mix = lax.optimization_barrier(jnp.sum(grad[:, None, :] * outputs_pair.astype(jnp.float32), axis=-1))
    d_picked = mixing * (d_mix - lax.optimization_barrier(jnp.sum(mixing * d_mix, axis=-1, keepdims=True)))
    d_logits = lax.optimization_barrier(jnp.sum(d_picked[:, :, None] * choice_hot, axis=1)).astype(jnp.bfloat16)
    grad_router = jnp.dot(normed_b.T, d_logits, preferred_element_type=jnp.float32)
    d_slots = jnp.zeros((total_slots, width), jnp.bfloat16).at[target.reshape(-1)].set(d_pair.reshape(2 * TOKENS, width))
    d_slots = d_slots.reshape(EXPERTS, clip_count * CAP, width)

    def expert_backward(operands):
        rows, grad_rows, first, second = operands
        pre = jnp.dot(rows, first, preferred_element_type=jnp.float32)
        active, gelu_pullback = jax.vjp(gelu_exact, pre)
        hidden = active.astype(jnp.bfloat16)
        d_hidden = jnp.dot(grad_rows, second.T, preferred_element_type=jnp.float32)
        d_pre = gelu_pullback(d_hidden)[0].astype(jnp.bfloat16)
        d_rows = jnp.dot(d_pre, first.T, preferred_element_type=jnp.float32).astype(jnp.bfloat16)
        grad_second = jnp.dot(hidden.T, grad_rows, preferred_element_type=jnp.float32).astype(jnp.bfloat16)
        grad_first = jnp.dot(rows.T, d_pre, preferred_element_type=jnp.float32).astype(jnp.bfloat16)
        return (d_rows, grad_first, grad_second)
    d_rows, grad_w_in, grad_w_out = lax.map(expert_backward, (slot_rows, d_slots, w_in, w_out))
    d_rows_pair = d_rows.reshape(total_slots, width)[target].astype(jnp.float32)
    d_normed = lax.optimization_barrier(jnp.sum(d_rows_pair, axis=1)) + jnp.dot(d_logits, w_router.T, preferred_element_type=jnp.float32)
    d_resid = grad + norm_pullback(d_normed)[0]

    def clip_backward(carry, operands):
        clip, d_clip = operands
        _, pullback = jax.vjp(attention_block, clip, w_qkv, w_proj)
        d_tokens, d_qkv, d_proj = pullback(d_clip)
        return ((carry[0] + d_qkv.astype(jnp.float32), carry[1] + d_proj.astype(jnp.float32)), d_tokens)
    start = (jnp.zeros(w_qkv.shape, jnp.float32), jnp.zeros(w_proj.shape, jnp.float32))
    sums, grad_tokens = lax.scan(clip_backward, start, (clips, d_resid.reshape(clip_count, TOK_DEV, width)))
    grad_tokens = grad_tokens.reshape(TOKENS, width)
    return (layer_out, grad_tokens, sums[0], sums[1], grad_router, grad_w_in, grad_w_out)
```

```python
import functools

import jax
import jax.numpy as jnp
from jax import lax
from jax.experimental import pallas as pl
from jax.experimental.pallas import tpu as pltpu
from jax.sharding import PartitionSpec as P

HEADS = 16
MESH = pl.DeviceIdType.MESH
BF16 = jnp.bfloat16
F32 = jnp.float32
SWAP = [(0, 1), (1, 0)]
VMEM = pl.BlockSpec(memory_space=pltpu.VMEM)


def peer_of(me, k):
    y = (me // 16 + k // 16) % 4
    z = (me // 4 + k // 4) % 4
    x = (me + k) % 4
    return y * 16 + z * 4 + x


def exchange_kernel(src, dst, send_sem, recv_sem, own_sem):
    g = lax.axis_index("group")
    me = lax.axis_index("dev")
    barrier = pltpu.get_barrier_semaphore()

    def greet(k, _):
        pl.semaphore_signal(barrier, inc=1, device_id=(g, peer_of(me, k)), device_id_type=MESH)
        return 0

    lax.fori_loop(1, 64, greet, 0)
    own = pltpu.make_async_copy(src.at[me], dst.at[me], own_sem)
    own.start()
    pl.semaphore_wait(barrier, 63)

    def copy(k):
        peer = peer_of(me, k)
        return pltpu.make_async_remote_copy(
            src_ref=src.at[peer],
            dst_ref=dst.at[me],
            send_sem=send_sem.at[k],
            recv_sem=recv_sem.at[k],
            device_id=(g, peer),
            device_id_type=MESH,
        )

    def start(k, _):
        copy(k).start()
        return 0

    lax.fori_loop(1, 64, start, 0)

    def finish(k, _):
        copy(k).wait()
        return 0

    lax.fori_loop(1, 64, finish, 0)
    own.wait()


def exchange(blocks, collective_id):
    return pl.pallas_call(
        exchange_kernel,
        out_shape=jax.ShapeDtypeStruct(blocks.shape, blocks.dtype),
        in_specs=[VMEM],
        out_specs=VMEM,
        scratch_shapes=[
            pltpu.SemaphoreType.DMA((64,)),
            pltpu.SemaphoreType.DMA((64,)),
            pltpu.SemaphoreType.DMA(()),
        ],
        compiler_params=pltpu.CompilerParams(
            collective_id=collective_id, has_side_effects=True, vmem_limit_bytes=24 * 2**20
        ),
    )(blocks)


ORDERS = ((16, 4, 1), (4, 1, 16), (1, 16, 4))


def along(me, stride, k):
    at = (me // stride) % 4
    return me - at * stride + ((at + k) % 4) * stride


def reduce_kernel(*refs):
    parts, outs = refs[0:3], refs[3:6]
    first, second, third = refs[6:9], refs[9:12], refs[12:15]
    mid, last = refs[15:18], refs[18:21]
    send_sem, recv_sem = refs[21], refs[22]
    g = lax.axis_index("group")
    me = lax.axis_index("dev")
    barrier = pltpu.get_barrier_semaphore()
    for stride in (16, 4, 1):
        for k in (1, 2, 3):
            pl.semaphore_signal(
                barrier, inc=1, device_id=(g, along(me, stride, k)), device_id_type=MESH
            )
    pl.semaphore_wait(barrier, 9)

    def copies(phase, p, src, dst):
        stride = ORDERS[p][phase]
        at = (me // stride) % 4
        return [
            pltpu.make_async_remote_copy(
                src_ref=src.at[(at + k) % 4],
                dst_ref=dst.at[k - 1],
                send_sem=send_sem.at[phase * 9 + p * 3 + k - 1],
                recv_sem=recv_sem.at[phase * 9 + p * 3 + k - 1],
                device_id=(g, along(me, stride, k)),
                device_id_type=MESH,
            )
            for k in (1, 2, 3)
        ]

    def place(phase, p):
        return (me // ORDERS[p][phase]) % 4

    started = []

    def launch(phase, p, src, dst):
        group = copies(phase, p, src, dst)
        for c in group:
            c.start()
        started.append(group)
        return group

    one = [launch(0, p, parts[p], first[p]) for p in range(3)]
    two = []
    for p in range(3):
        for c in one[p]:
            c.wait_recv()
        own = parts[p].at[place(0, p)]
        for q in range(4):
            rows = pl.ds(q * 32, 32)
            total = own[rows, :].astype(F32)
            for k in range(3):
                total = total + first[p][k, rows, :].astype(F32)
            mid[p][q] = total.astype(BF16)
        two.append(launch(1, p, mid[p], second[p]))
    three = []
    for p in range(3):
        for c in two[p]:
            c.wait_recv()
        total = mid[p][place(1, p)].astype(F32)
        for k in range(3):
            total = total + second[p][k].astype(F32)
        for q in range(4):
            last[p][q] = total[q * 8 : q * 8 + 8, :]
        three.append(launch(2, p, last[p], third[p]))
    for p in range(3):
        for c in three[p]:
            c.wait_recv()
        total = last[p][place(2, p)]
        for k in range(3):
            total = total + third[p][k]
        outs[p][...] = total
    for group in started:
        for c in group:
            c.wait_send()


def reduce_parts(parts):
    widths = [p.shape[2] for p in parts]
    scratch = []
    scratch += [pltpu.VMEM((3, 128, w), BF16) for w in widths]
    scratch += [pltpu.VMEM((3, 32, w), BF16) for w in widths]
    scratch += [pltpu.VMEM((3, 8, w), F32) for w in widths]
    scratch += [pltpu.VMEM((4, 32, w), BF16) for w in widths]
    scratch += [pltpu.VMEM((4, 8, w), F32) for w in widths]
    scratch += [pltpu.SemaphoreType.DMA((27,)), pltpu.SemaphoreType.DMA((27,))]
    return pl.pallas_call(
        reduce_kernel,
        out_shape=[jax.ShapeDtypeStruct((8, w), F32) for w in widths],
        in_specs=[VMEM] * 3,
        out_specs=[VMEM] * 3,
        scratch_shapes=scratch,
        compiler_params=pltpu.CompilerParams(
            collective_id=7, has_side_effects=True, vmem_limit_bytes=40 * 2**20
        ),
    )(*parts)


def layer_norm(values):
    center = values - jnp.mean(values, axis=-1, keepdims=True)
    spread = jnp.mean(center * center, axis=-1, keepdims=True)
    return center * lax.rsqrt(spread + 1e-05)


def dot(a, b):
    return jnp.dot(a, b, preferred_element_type=F32)


def dot_t(a, b):
    return lax.dot_general(a, b, (((1,), (1,)), ((), ())), preferred_element_type=F32)


def t_dot(a, b):
    return lax.dot_general(a, b, (((0,), (0,)), ((), ())), preferred_element_type=F32)


def attention(clip_rows, w_qkv, w_proj):
    count, width = clip_rows.shape
    head = width // HEADS
    rows32 = clip_rows.astype(F32)
    center = rows32 - jnp.mean(rows32, axis=-1, keepdims=True)
    rstd = lax.rsqrt(jnp.mean(center * center, axis=-1, keepdims=True) + 1e-05)
    normed = center * rstd
    normed_b = normed.astype(BF16)
    qkv = dot(normed_b, w_qkv).astype(BF16)
    q, k, v = (qkv[:, i * width : (i + 1) * width].reshape(count, HEADS, head) for i in range(3))
    scores = jnp.einsum("qhd,khd->hqk", q, k, preferred_element_type=F32) * (head**-0.5)
    probs = jax.nn.softmax(scores, axis=-1)
    probs_b = probs.astype(BF16)
    attended = jnp.einsum("hqk,khd->qhd", probs_b, v, preferred_element_type=F32).astype(BF16)
    attended = attended.reshape(count, width)
    resid = rows32 + dot(attended, w_proj)
    return resid, (normed, rstd, normed_b, q, k, v, probs, probs_b, attended)


def norm_backward(normed, rstd, d_normed):
    mean = jnp.mean(d_normed, axis=-1, keepdims=True)
    along_it = jnp.mean(d_normed * normed, axis=-1, keepdims=True)
    return rstd * (d_normed - mean - normed * along_it)


def shards(tokens, cotangent, expert_ids, slot_ids, w_qkv, w_proj, w_router, w_in, w_out):
    chips = lax.axis_size("dev")
    count, width = tokens.shape
    capacity = 4 * count // chips
    head = width // HEADS
    g = lax.axis_index("group")
    half = w_in.shape[2]
    other_in = lax.ppermute(w_in[0], "group", SWAP)
    other_out = lax.ppermute(w_out[0], "group", SWAP)

    resid32, saved = attention(tokens, w_qkv, w_proj)
    normed1, rstd1, normed1_b, q, k, v, probs, probs_b, attended = saved
    resid_f = resid32.astype(BF16).astype(F32)
    center = resid_f - jnp.mean(resid_f, axis=-1, keepdims=True)
    rstd2 = lax.rsqrt(jnp.mean(center * center, axis=-1, keepdims=True) + 1e-05)
    normed2 = center * rstd2
    normed2_b = normed2.astype(BF16)
    logits = dot(normed2_b, w_router)
    choice_hot = (
        expert_ids[:, :, None] == jnp.arange(chips, dtype=jnp.int32)[None, None, :]
    ).astype(F32)
    picked = jnp.sum(logits[:, None, :] * choice_hot, axis=-1)
    mixing = jax.nn.softmax(picked, axis=-1)
    grad = cotangent.astype(F32)

    flat_slot = expert_ids * capacity + slot_ids
    slot_range = jnp.arange(chips * capacity, dtype=jnp.int32)
    place = [(flat_slot[:, i, None] == slot_range[None, :]).astype(BF16) for i in range(2)]
    d_pair = [(mixing[:, i : i + 1] * grad).astype(BF16) for i in range(2)]
    rows_out = t_dot(place[0] + place[1], normed2_b).astype(BF16)
    grads_out = t_dot(
        jnp.concatenate(place, axis=0), jnp.concatenate(d_pair, axis=0)
    ).astype(BF16)
    blocks = jnp.concatenate(
        [rows_out.reshape(chips, capacity, width), grads_out.reshape(chips, capacity, width)], axis=1
    )
    arrived = exchange(blocks, 1)
    rows = arrived[:, :capacity].reshape(-1, width)
    d_rows = arrived[:, capacity:].reshape(-1, width)

    w_ins = [w_in[0], other_in]
    w_outs = [w_out[0], other_out]
    hidden, d_pre = [], []
    total_out, total_in = 0.0, 0.0
    for first, second in zip(w_ins, w_outs):
        pre = dot(rows, first)
        cdf = 0.5 * (1.0 + lax.erf(pre * (0.5**0.5)))
        pdf = jnp.exp(-0.5 * pre * pre) * (0.5 / jnp.pi) ** 0.5
        act = (pre * cdf).astype(BF16)
        slope = cdf + pre * pdf
        total_out = total_out + dot(act, second)
        d_one = (slope * dot_t(d_rows, second)).astype(BF16)
        total_in = total_in + dot_t(d_one, first)
        hidden.append(act)
        d_pre.append(d_one)
    back = jnp.concatenate(
        [
            total_out.astype(BF16).reshape(chips, capacity, width),
            total_in.astype(BF16).reshape(chips, capacity, width),
        ],
        axis=1,
    )
    returned = exchange(back, 2)

    there_x, there_d, there_h, there_p = (
        lax.ppermute(a, "group", SWAP) for a in (rows, d_rows, hidden[1], d_pre[1])
    )
    both = lambda a, b: jnp.concatenate([a, b], axis=0)
    grad_w_in = t_dot(both(rows, there_x), both(d_pre[0], there_p)).astype(BF16)
    grad_w_out = t_dot(both(hidden[0], there_h), both(d_rows, there_d)).astype(BF16)

    flat_out = returned[:, :capacity].reshape(-1, width)
    flat_in = returned[:, capacity:].reshape(-1, width)
    pair = [dot(p, flat_out) for p in place]
    layer_out = (resid_f + mixing[:, 0:1] * pair[0] + mixing[:, 1:2] * pair[1]).astype(BF16)
    d_mix = jnp.stack([jnp.sum(grad * a, axis=-1) for a in pair], axis=1)
    d_picked = mixing * (d_mix - jnp.sum(mixing * d_mix, axis=-1, keepdims=True))
    d_logits = jnp.sum(d_picked[:, :, None] * choice_hot, axis=1).astype(BF16)
    d_normed2 = dot(place[0] + place[1], flat_in) + dot_t(d_logits, w_router)
    d_resid = grad + norm_backward(normed2, rstd2, d_normed2)

    d_resid_b = d_resid.astype(BF16)
    d_att = dot_t(d_resid_b, w_proj).astype(BF16).reshape(count, HEADS, head)
    d_probs = jnp.einsum("qhd,khd->hqk", d_att, v, preferred_element_type=F32)
    d_v = jnp.einsum("hqk,qhd->khd", probs_b, d_att, preferred_element_type=F32)
    d_scores = probs * (d_probs - jnp.sum(probs * d_probs, axis=-1, keepdims=True))
    d_scores = (d_scores * (head**-0.5)).astype(BF16)
    d_q = jnp.einsum("hqk,khd->qhd", d_scores, k, preferred_element_type=F32)
    d_k = jnp.einsum("hqk,qhd->khd", d_scores, q, preferred_element_type=F32)
    d_qkv = jnp.concatenate([a.reshape(count, width) for a in (d_q, d_k, d_v)], axis=1).astype(BF16)
    d_normed1 = dot_t(d_qkv, w_qkv)
    grad_tokens = (d_resid + norm_backward(normed1, rstd1, d_normed1)).astype(BF16)

    rows_half = width // 2
    lhs = jnp.stack([normed1_b, attended, normed2_b], axis=0).reshape(3, count, 2, rows_half)
    mine = lax.dynamic_index_in_dim(lhs, g, axis=2, keepdims=False)
    theirs = lax.ppermute(
        lax.dynamic_index_in_dim(lhs, 1 - g, axis=2, keepdims=False), "group", SWAP
    )
    rhs = jnp.concatenate(
        [d_qkv, d_resid_b, d_logits, jnp.zeros((count, 64), BF16)], axis=1
    )
    rhs = both(rhs, lax.ppermute(rhs, "group", SWAP))
    lhs = jnp.concatenate([mine, theirs], axis=1)
    cube = lhs.reshape(3, 2 * count, 4, 4, 4, 8)

    def ordered(which, order):
        return cube[which].transpose((0,) + tuple(1 + a for a in order) + (4,)).reshape(
            2 * count, rows_half
        )

    cut = width + width // 2
    part0 = t_dot(lhs[0], rhs[:, :cut]).astype(BF16)
    part1 = t_dot(ordered(0, (1, 2, 0)), rhs[:, cut : 2 * cut]).astype(BF16)
    part2 = jnp.concatenate(
        [
            t_dot(ordered(1, (2, 0, 1)), rhs[:, 3 * width : 4 * width]),
            t_dot(ordered(2, (2, 0, 1)), rhs[:, 4 * width :]),
        ],
        axis=1,
    ).astype(BF16)
    sums = reduce_parts([a.reshape(4, 128, a.shape[1]) for a in (part0, part1, part2)])
    return (
        layer_out,
        grad_tokens,
        jnp.concatenate(sums[:2], axis=1),
        sums[2][:, :width],
        sums[2][:, width : width + chips],
        grad_w_in[None],
        grad_w_out[None],
    )


def solution(mesh):
    return jax.shard_map(
        shards,
        mesh=mesh,
        in_specs=(
            P(("group", "dev"), None),
            P(("group", "dev"), None),
            P(("group", "dev"), None),
            P(("group", "dev"), None),
            P(),
            P(),
            P(),
            P("dev", None, "group"),
            P("dev", "group", None),
        ),
        out_specs=(
            P(("group", "dev"), None),
            P(("group", "dev"), None),
            P(("group", "dev"), None),
            P(("group", "dev"), None),
            P(("group", "dev"), None),
            P("dev", None, "group"),
            P("dev", "group", None),
        ),
        check_vma=False,
    )
```

```python
import jax
import jax.numpy as jnp
from jax import lax
from jax.experimental import pallas as pl
from jax.experimental.pallas import tpu as pltpu
from jax.sharding import PartitionSpec as P

HEADS = 16
MESH = pl.DeviceIdType.MESH
BF16 = jnp.bfloat16
F32 = jnp.float32
SWAP = [(0, 1), (1, 0)]
VMEM = pl.BlockSpec(memory_space=pltpu.VMEM)
ANY = pl.BlockSpec(memory_space=pl.ANY)
CHUNK = 512


def peer_of(me, k):
    y = (me // 16 + k // 16) % 4
    z = (me // 4 + k // 4) % 4
    x = (me + k) % 4
    return y * 16 + z * 4 + x


def dot(a, b):
    return jnp.dot(a, b, preferred_element_type=F32)


def dot_t(a, b):
    return lax.dot_general(a, b, (((1,), (1,)), ((), ())), preferred_element_type=F32)


def t_dot(a, b):
    return lax.dot_general(a, b, (((0,), (0,)), ((), ())), preferred_element_type=F32)


def expert_kernel(*refs):
    x_in, g_in, m_in, w1_own, w2_own, w1_sib, w2_sib = refs[:7]
    ret_out, ret_in, grad_w1, grad_w2 = refs[7:11]
    w1, w2, xs, gs, xm, gm, hid, dp, acc, pack_out, pack_in = refs[11:22]
    xm_sib, gm_sib, hid_sib, dp_sib, x_turn, stage1, stage2 = refs[22:29]
    w_sem, send_out, recv_out, send_in, recv_in, own_sem, sib_send, sib_recv, grad_sem = refs[29:38]
    g = lax.axis_index("group")
    me = lax.axis_index("dev")
    barrier = pltpu.get_barrier_semaphore()

    def greet(k, _):
        pl.semaphore_signal(barrier, inc=1, device_id=(g, peer_of(me, k)), device_id_type=MESH)
        return 0

    lax.fori_loop(1, 64, greet, 0)
    pl.semaphore_signal(barrier, inc=1, device_id=(1 - g, me), device_id_type=MESH)

    def load(c, own):
        first, second = (w1_own, w2_own) if own else (w1_sib, w2_sib)
        at = pl.ds(pl.multiple_of((c % 4) * CHUNK, CHUNK), CHUNK)
        return (
            pltpu.make_async_copy(first.at[:, at], w1.at[c], w_sem.at[2 * c]),
            pltpu.make_async_copy(second.at[at, :], w2.at[c], w_sem.at[2 * c + 1]),
        )

    for c in range(8):
        for one in load(c, c >= 4):
            one.start()

    lane = lax.broadcasted_iota(jnp.int32, (8, 8, 128), 2)
    slot = lax.broadcasted_iota(jnp.int32, (8, 8, 128), 1)

    def unpack(i, _):
        chips = pl.ds(i * 8, 8)
        rows = pl.ds(pl.multiple_of(i * 64, 64), 64)
        spread = jnp.broadcast_to(m_in[chips], (8, 8, 128))
        mix = jnp.sum(jnp.where(lane == slot, spread, 0.0), axis=2, keepdims=True)
        for src, plain, mixed in ((x_in, xs, xm), (g_in, gs, gm)):
            block = src[chips].astype(F32)
            for h in range(2):
                piece = block[:, h * 8 : h * 8 + 8, :]
                columns = pl.ds(h * 512, 512)
                plain[rows, columns] = piece.reshape(64, 512).astype(BF16)
                mixed[rows, columns] = (piece * mix).reshape(64, 512).astype(BF16)
        return 0

    lax.fori_loop(0, 8, unpack, 0)
    pl.semaphore_wait(barrier, 64)

    def to_sibling(i, src, dst):
        c = pltpu.make_async_remote_copy(
            src_ref=src,
            dst_ref=dst,
            send_sem=sib_send.at[i],
            recv_sem=sib_recv.at[i],
            device_id=(1 - g, me),
            device_id_type=MESH,
        )
        c.start()
        return c

    swaps = [to_sibling(0, xm, xm_sib), to_sibling(1, gm, gm_sib)]

    def forward(c):
        for r in range(2):
            rows = pl.ds(r * 256, 256)
            pre = dot(xs[rows, :], w1[c])
            cdf = 0.5 * (1.0 + lax.erf(pre * (0.5**0.5)))
            pdf = jnp.exp(-0.5 * pre * pre) * 0.3989422804014327
            hid[c, rows, :] = (pre * cdf).astype(BF16)
            dp[c, rows, :] = (cdf + pre * pdf).astype(BF16)
        for r in range(2):
            rows = pl.ds(r * 256, 256)
            acc[rows, :] += dot(hid[c, rows, :], w2[c])

    def backward(c):
        for r in range(2):
            rows = pl.ds(r * 256, 256)
            d_hidden = dot_t(gs[rows, :], w2[c])
            dp[c, rows, :] = (dp[c, rows, :].astype(F32) * d_hidden).astype(BF16)
        for r in range(2):
            rows = pl.ds(r * 256, 256)
            acc[rows, :] += dot_t(dp[c, rows, :], w1[c])

    def pack_into(target):
        def one(i, _):
            value = acc[pl.ds(pl.multiple_of(i * 64, 64), 64), :].reshape(8, 8, 1024)
            both = jnp.concatenate([value[:, :, :512], value[:, :, 512:]], axis=1)
            target[pl.ds(i * 8, 8)] = both.astype(BF16)
            return 0

        lax.fori_loop(0, 8, one, 0)

    def home(k, src, dst, send_sem, recv_sem):
        peer = peer_of(me, k)
        return pltpu.make_async_remote_copy(
            src_ref=src.at[peer],
            dst_ref=dst.at[me],
            send_sem=send_sem.at[k],
            recv_sem=recv_sem.at[k],
            device_id=(g, peer),
            device_id_type=MESH,
        )

    def send_all(src, dst, send_sem, recv_sem, own):
        def one(k, _):
            home(k, src, dst, send_sem, recv_sem).start()
            return 0

        lax.fori_loop(1, 64, one, 0)
        mine = pltpu.make_async_copy(src.at[me], dst.at[me], own_sem.at[own])
        mine.start()
        return mine

    acc[...] = jnp.zeros_like(acc)
    def forward_loop(own):
        def one(c, _):
            for copy in load(c, own):
                copy.wait()
            forward(c)
            return 0

        lax.fori_loop(4 * own, 4 * own + 4, one, 0)

    def backward_loop(own):
        def one(c, _):
            backward(c)
            return 0

        lax.fori_loop(4 * own, 4 * own + 4, one, 0)

    forward_loop(0)
    swaps.append(to_sibling(2, hid.at[pl.ds(0, 4)], hid_sib))
    forward_loop(1)
    pack_into(pack_out)
    mine_out = send_all(pack_out, ret_out, send_out, recv_out, 0)
    acc[...] = jnp.zeros_like(acc)
    backward_loop(0)
    swaps.append(to_sibling(3, dp.at[pl.ds(0, 4)], dp_sib))
    backward_loop(1)
    pack_into(pack_in)
    mine_in = send_all(pack_in, ret_in, send_in, recv_in, 1)

    for s in swaps:
        s.wait_recv()
    for r in range(4):
        rows = pl.ds(r * 128, 128)
        x_turn[:, pl.ds(r * 128, 128)] = xm[rows, :].T
        x_turn[:, pl.ds(512 + r * 128, 128)] = xm_sib[rows, :].T

    def grad_copy(c, which):
        at = pl.ds(pl.multiple_of(c * CHUNK, CHUNK), CHUNK)
        source = stage1 if which == 0 else stage2
        target = grad_w1.at[:, at] if which == 0 else grad_w2.at[at, :]
        return pltpu.make_async_copy(source, target, grad_sem.at[which])

    def grads(c, _):
        @pl.when(c > 0)
        def _():
            grad_copy(c - 1, 0).wait()

        for r in range(4):
            rows = pl.ds(r * 256, 256)
            stage1[rows, :] = (
                dot(x_turn[rows, pl.ds(0, 512)], dp[4 + c])
                + dot(x_turn[rows, pl.ds(512, 512)], dp_sib[c])
            ).astype(BF16)
        grad_copy(c, 0).start()

        @pl.when(c > 0)
        def _():
            grad_copy(c - 1, 1).wait()

        for r in range(2):
            columns = pl.ds(r * 256, 256)
            stage2[columns, :] = (
                t_dot(hid[4 + c, :, columns], gm[...]) + t_dot(hid_sib[c, :, columns], gm_sib[...])
            ).astype(BF16)
        grad_copy(c, 1).start()
        return 0

    lax.fori_loop(0, 4, grads, 0)
    grad_copy(3, 0).wait()
    grad_copy(3, 1).wait()

    def finish(k, _):
        home(k, pack_out, ret_out, send_out, recv_out).wait()
        home(k, pack_in, ret_in, send_in, recv_in).wait()
        return 0

    lax.fori_loop(1, 64, finish, 0)
    mine_out.wait()
    mine_in.wait()
    for s in swaps:
        s.wait_send()


def run_experts(x_blocks, g_blocks, m_blocks, w1_own, w2_own, w1_sib, w2_sib):
    sem = pltpu.SemaphoreType.DMA
    return pl.pallas_call(
        expert_kernel,
        out_shape=[
            jax.ShapeDtypeStruct((64, 16, 512), BF16),
            jax.ShapeDtypeStruct((64, 16, 512), BF16),
            jax.ShapeDtypeStruct((1024, 2048), BF16),
            jax.ShapeDtypeStruct((2048, 1024), BF16),
        ],
        in_specs=[VMEM] * 3 + [ANY] * 4,
        out_specs=[VMEM] * 2 + [ANY] * 2,
        scratch_shapes=[
            pltpu.VMEM((8, 1024, CHUNK), BF16),
            pltpu.VMEM((8, CHUNK, 1024), BF16),
            pltpu.VMEM((512, 1024), BF16),
            pltpu.VMEM((512, 1024), BF16),
            pltpu.VMEM((512, 1024), BF16),
            pltpu.VMEM((512, 1024), BF16),
            pltpu.VMEM((8, 512, CHUNK), BF16),
            pltpu.VMEM((8, 512, CHUNK), BF16),
            pltpu.VMEM((512, 1024), F32),
            pltpu.VMEM((64, 16, 512), BF16),
            pltpu.VMEM((64, 16, 512), BF16),
            pltpu.VMEM((512, 1024), BF16),
            pltpu.VMEM((512, 1024), BF16),
            pltpu.VMEM((4, 512, CHUNK), BF16),
            pltpu.VMEM((4, 512, CHUNK), BF16),
            pltpu.VMEM((1024, 1024), BF16),
            pltpu.VMEM((1024, CHUNK), BF16),
            pltpu.VMEM((CHUNK, 1024), BF16),
            sem((16,)),
            sem((64,)),
            sem((64,)),
            sem((64,)),
            sem((64,)),
            sem((2,)),
            sem((4,)),
            sem((4,)),
            sem((2,)),
        ],
        compiler_params=pltpu.CompilerParams(
            collective_id=2, has_side_effects=True, vmem_limit_bytes=58 * 2**20
        ),
        name="experts",
    )(x_blocks, g_blocks, m_blocks, w1_own, w2_own, w1_sib, w2_sib)


def norm_parts(rows32):
    center = rows32 - jnp.mean(rows32, axis=-1, keepdims=True)
    rstd = lax.rsqrt(jnp.mean(center * center, axis=-1, keepdims=True) + 1e-05)
    return center * rstd, rstd


def norm_backward(normed, rstd, d_normed):
    mean = jnp.mean(d_normed, axis=-1, keepdims=True)
    along_it = jnp.mean(d_normed * normed, axis=-1, keepdims=True)
    return rstd * (d_normed - mean - normed * along_it)


def head_masks():
    low = lax.broadcasted_iota(jnp.int32, (128, 128), 1) < 64
    return low.astype(F32), 1.0 - low.astype(F32)


def two_heads(pair, masks):
    wide = pair.astype(F32)
    return jnp.concatenate([wide * masks[0], wide * masks[1]], axis=0).astype(BF16)


def softmax_pair(scores):
    out = []
    for h in range(2):
        one = scores[:, h * 128 : h * 128 + 128]
        e = jnp.exp(one - jnp.max(one, axis=-1, keepdims=True))
        out.append(e / jnp.sum(e, axis=-1, keepdims=True))
    return out


def attend_kernel(*refs):
    tokens, cot, ids, slots, ids_row, flat_row, w_qkv_in, w_proj_in, w_router = refs[:9]
    x_got, g_got, m_got, resid_out, qkv, att, mix_out = refs[9:16]
    w_qkv, w_proj, n2b, x_pack, g_pack, m_pack = refs[16:22]
    w_sem, send_sem, recv_sem, own_sem = refs[22:26]
    g = lax.axis_index("group")
    me = lax.axis_index("dev")
    barrier = pltpu.get_barrier_semaphore()

    def greet(k, _):
        pl.semaphore_signal(barrier, inc=1, device_id=(g, peer_of(me, k)), device_id_type=MESH)
        return 0

    lax.fori_loop(1, 64, greet, 0)
    loads = []
    for c in range(6):
        at = pl.ds(c * 512, 512)
        loads.append(pltpu.make_async_copy(w_qkv_in.at[:, at], w_qkv.at[:, at], w_sem.at[c]))
    loads.append(pltpu.make_async_copy(w_proj_in, w_proj, w_sem.at[6]))
    for c in loads:
        c.start()

    def dispatch(src, pack):
        for i in range(4):
            at = lax.broadcasted_iota(jnp.int32, (128, 128), 0) + i * 128
            hit = (at == flat_row[0:1, :]) | (at == flat_row[1:2, :])
            place = hit.astype(F32).astype(BF16)
            halves = [dot(place, src[:, h * 512 : h * 512 + 512]).reshape(16, 8, 512) for h in range(2)]
            pack[pl.ds(i * 16, 16)] = jnp.concatenate(halves, axis=1).astype(BF16)

    packs, gots = (x_pack, g_pack, m_pack), (x_got, g_got, m_got)

    def copy(i, k):
        peer = peer_of(me, k)
        return pltpu.make_async_remote_copy(
            src_ref=packs[i].at[peer],
            dst_ref=gots[i].at[me],
            send_sem=send_sem.at[i, k],
            recv_sem=recv_sem.at[i, k],
            device_id=(g, peer),
            device_id_type=MESH,
        )

    def send_all(i):
        def one(k, _):
            copy(i, k).start()
            return 0

        lax.fori_loop(1, 64, one, 0)
        own = pltpu.make_async_copy(packs[i].at[me], gots[i].at[me], own_sem.at[i])
        own.start()
        return own

    dispatch(cot, g_pack)
    pl.semaphore_wait(barrier, 63)
    owns = [send_all(1)]

    rows32 = tokens[...].astype(F32)
    normed, _ = norm_parts(rows32)
    normed_b = normed.astype(BF16)
    for c in range(6):
        loads[c].wait()
        at = pl.ds(c * 512, 512)
        qkv[:, at] = dot(normed_b, w_qkv[:, at]).astype(BF16)
    masks = head_masks()
    for p in range(8):
        q2, k2, v2 = (qkv[:, i * 1024 + p * 128 : i * 1024 + p * 128 + 128] for i in range(3))
        probs = softmax_pair(dot_t(q2, two_heads(k2, masks)) * 0.125)
        probs = jnp.concatenate(probs, axis=1).astype(BF16)
        att[:, p * 128 : p * 128 + 128] = dot(probs, two_heads(v2, masks)).astype(BF16)
    loads[6].wait()
    resid = (rows32 + dot(att[...], w_proj[...])).astype(BF16)
    resid_out[...] = resid
    normed2, _ = norm_parts(resid.astype(F32))
    n2b[...] = normed2.astype(BF16)
    dispatch(n2b, x_pack)
    owns.append(send_all(0))

    logits = dot(n2b[...], w_router[...])
    expert = lax.broadcasted_iota(jnp.int32, (128, 64), 1)
    picked = [
        jnp.sum(jnp.where(expert == ids[:, k : k + 1], logits, 0.0), axis=-1, keepdims=True)
        for k in range(2)
    ]
    top = jnp.maximum(picked[0], picked[1])
    e = [jnp.exp(a - top) for a in picked]
    lane = lax.broadcasted_iota(jnp.int32, (128, 128), 1)
    owner = lax.broadcasted_iota(jnp.int32, (64, 128), 0)
    table = jnp.zeros((64, 128), F32)
    for k in range(2):
        mix = e[k] / (e[0] + e[1])
        mix_out[:, k : k + 1] = mix
        spread = jnp.where(lane == slots[:, k : k + 1], mix, 0.0)
        high = spread.astype(BF16)
        low = (spread - high.astype(F32)).astype(BF16)
        hot = (owner == ids_row[k : k + 1, :]).astype(F32).astype(BF16)
        table = table + dot(hot, high) + dot(hot, low)
    m_pack[...] = table.reshape(64, 1, 128)
    owns.append(send_all(2))

    def finish(k, _):
        for i in range(3):
            copy(i, k).wait()
        return 0

    lax.fori_loop(1, 64, finish, 0)
    for c in owns:
        c.wait()


def run_attend(tokens, cot, ids, slots, ids_row, flat_row, w_qkv, w_proj, w_router):
    sem = pltpu.SemaphoreType.DMA
    shape = jax.ShapeDtypeStruct
    return pl.pallas_call(
        attend_kernel,
        out_shape=[
            shape((64, 16, 512), BF16),
            shape((64, 16, 512), BF16),
            shape((64, 1, 128), F32),
            shape((128, 1024), BF16),
            shape((128, 3072), BF16),
            shape((128, 1024), BF16),
            shape((128, 2), F32),
        ],
        in_specs=[VMEM] * 6 + [ANY] * 2 + [VMEM],
        out_specs=[VMEM] * 7,
        scratch_shapes=[
            pltpu.VMEM((1024, 3072), BF16),
            pltpu.VMEM((1024, 1024), BF16),
            pltpu.VMEM((128, 1024), BF16),
            pltpu.VMEM((64, 16, 512), BF16),
            pltpu.VMEM((64, 16, 512), BF16),
            pltpu.VMEM((64, 1, 128), F32),
            sem((7,)),
            sem((3, 64)),
            sem((3, 64)),
            sem((3,)),
        ],
        compiler_params=pltpu.CompilerParams(
            collective_id=1, has_side_effects=True, vmem_limit_bytes=40 * 2**20
        ),
        name="attend",
    )(tokens, cot, ids, slots, ids_row, flat_row, w_qkv, w_proj, w_router)


ORDERS = ((16, 4, 1), (4, 1, 16), (1, 16, 4))
EARLY, LATE = 384, 1024


def along(me, stride, k):
    at = (me // stride) % 4
    return me - at * stride + ((at + k) % 4) * stride


def natural_row(order, j):
    row = j % 8
    for at, stride in zip((128, 32, 8), ORDERS[order]):
        row = row + ((j // at) % 4) * (stride * 8)
    return row


def finish_kernel(*refs):
    ret_out, ret_in, tokens, cot, resid, qkv, att, mix, ids, flat, w_qkv_in, w_proj_in, w_router = refs[:13]
    layer_out, grad_tokens, sum_qkv, sum_proj, sum_router = refs[13:18]
    w_qkv, w_proj, rows, half_in, half_send, lhs, rhs, d_att = refs[18:26]
    parts, first, mid, second, last, third = (refs[26 + 2 * i : 28 + 2 * i] for i in range(6))
    w_sem, pair_send, pair_recv, send_sem, recv_sem = refs[38:43]
    g = lax.axis_index("group")
    me = lax.axis_index("dev")
    barrier = pltpu.get_barrier_semaphore()
    pl.semaphore_signal(barrier, inc=1, device_id=(1 - g, me), device_id_type=MESH)
    for stride in (16, 4, 1):
        for k in (1, 2, 3):
            pl.semaphore_signal(
                barrier, inc=1, device_id=(g, along(me, stride, k)), device_id_type=MESH
            )
    loads = [
        pltpu.make_async_copy(w_proj_in, w_proj, w_sem.at[0]),
        pltpu.make_async_copy(w_qkv_in, w_qkv, w_sem.at[1]),
    ]
    for c in loads:
        c.start()

    started = []

    def swap(i, src, dst):
        c = pltpu.make_async_remote_copy(
            src_ref=src,
            dst_ref=dst,
            send_sem=pair_send.at[i],
            recv_sem=pair_recv.at[i],
            device_id=(1 - g, me),
            device_id_type=MESH,
        )
        c.start()
        started.append(c)
        return c

    normed1, rstd1 = norm_parts(tokens[...].astype(F32))
    resid_f = resid[...].astype(F32)
    normed2, rstd2 = norm_parts(resid_f)
    half_in[0] = normed1.astype(BF16)
    half_in[1] = att[...]
    half_in[2] = normed2.astype(BF16)
    column = lax.broadcasted_iota(jnp.int32, (512, 512), 1)
    position = lax.broadcasted_iota(jnp.int32, (512, 512), 0)
    mine = pl.ds(pl.multiple_of(g * 512, 512), 512)
    theirs = pl.ds(pl.multiple_of((1 - g) * 512, 512), 512)
    for order in range(3):
        turn = (column == natural_row(order, position)).astype(F32).astype(BF16)
        for which in range(3):
            if which == 2 and order < 2:
                continue
            i = order * 2 + which
            lhs[i, :, 0:128] = dot_t(turn, half_in[which, :, mine]).astype(BF16)
            half_send[i] = dot_t(turn, half_in[which, :, theirs]).astype(BF16)
    pl.semaphore_wait(barrier, 10)
    lhs_swap = [swap(i, half_send.at[i], lhs.at[i, :, pl.ds(128, 128)]) for i in range(7)]

    def unpack(src):
        def one(i, _):
            block = src[pl.ds(i * 8, 8)].astype(F32)
            at = pl.ds(pl.multiple_of(i * 64, 64), 64)
            for h in range(2):
                piece = block[:, h * 8 : h * 8 + 8, :].reshape(64, 512)
                rows[at, pl.ds(h * 512, 512)] = piece.astype(BF16)
            return 0

        lax.fori_loop(0, 8, one, 0)

    slot = lax.broadcasted_iota(jnp.int32, (128, 512), 1)
    place = jnp.concatenate(
        [(slot == flat[:, k : k + 1]).astype(F32).astype(BF16) for k in range(2)], axis=0
    )
    grad = cot[...].astype(F32)
    mixing = [mix[:, k : k + 1] for k in range(2)]
    unpack(ret_out)
    pair = dot(place, rows[...])
    pair = [pair[:128], pair[128:]]
    layer_out[...] = (resid_f + mixing[0] * pair[0] + mixing[1] * pair[1]).astype(BF16)
    d_mix = [jnp.sum(grad * a, axis=-1, keepdims=True) for a in pair]
    centre = mixing[0] * d_mix[0] + mixing[1] * d_mix[1]
    expert = lax.broadcasted_iota(jnp.int32, (128, 128), 1)
    d_logits = sum(
        jnp.where(expert == ids[:, k : k + 1], mixing[k] * (d_mix[k] - centre), 0.0) for k in range(2)
    ).astype(BF16)
    unpack(ret_in)
    pair = dot(place, rows[...])
    d_normed2 = (
        mixing[0] * pair[:128] + mixing[1] * pair[128:] + dot_t(d_logits[:, :64], w_router[...])
    )
    d_resid = grad + norm_backward(normed2, rstd2, d_normed2)
    own_rows, sib_rows = pl.ds(0, 128), pl.ds(128, 128)
    rhs[own_rows, pl.ds(3072, 1024)] = d_resid.astype(BF16)
    rhs[own_rows, pl.ds(4096, 128)] = d_logits
    tail = pl.ds(3072, 1152)
    early_swap = swap(7, rhs.at[own_rows, tail], rhs.at[sib_rows, tail])
    loads[0].wait()
    d_att[...] = dot_t(rhs[own_rows, pl.ds(3072, 1024)], w_proj[...]).astype(BF16)

    def place_of(phase, order):
        return (me // ORDERS[order][phase]) % 4

    def launch(phase, late, order, src, dst):
        stride = ORDERS[order][phase]
        at = place_of(phase, order)
        group = []
        for k in (1, 2, 3):
            sem = ((phase * 2 + late) * 3 + order) * 3 + k - 1
            c = pltpu.make_async_remote_copy(
                src_ref=src.at[order, (at + k) % 4],
                dst_ref=dst.at[order, k - 1],
                send_sem=send_sem.at[sem],
                recv_sem=recv_sem.at[sem],
                device_id=(g, along(me, stride, k)),
                device_id_type=MESH,
            )
            c.start()
            group.append(c)
        started.extend(group)
        return group

    def sum_one(late, order, arriving):
        for c in arriving:
            c.wait_recv()
        at = place_of(0, order)
        for q in range(4):
            piece = pl.ds(q * 32, 32)
            total = parts[late][order, at, piece, :].astype(F32)
            for k in range(3):
                total = total + first[late][order, k, piece, :].astype(F32)
            mid[late][order, q] = total.astype(BF16)
        return launch(1, late, order, mid[late], second[late])

    def sum_two(late, order, arriving):
        for c in arriving:
            c.wait_recv()
        total = mid[late][order, place_of(1, order)].astype(F32)
        for k in range(3):
            total = total + second[late][order, k].astype(F32)
        for q in range(4):
            last[late][order, q] = total[q * 8 : q * 8 + 8, :]
        return launch(2, late, order, last[late], third[late])

    def sum_three(late, order, arriving):
        for c in arriving:
            c.wait_recv()
        total = last[late][order, place_of(2, order)]
        for k in range(3):
            total = total + third[late][order, k]
        return total

    for c in lhs_swap:
        c.wait_recv()
    early_swap.wait_recv()
    early = []
    for order in range(3):
        for r in range(4):
            for left, at, width in (
                (order * 2 + 1, 0, EARLY if order < 2 else 256),
                (6, 256, 128),
            ):
                if left == 6 and order < 2:
                    continue
                value = dot(
                    lhs[left, r * 128 : r * 128 + 128, :],
                    rhs[:, 3072 + order * EARLY + at : 3072 + order * EARLY + at + width],
                )
                parts[0][order, r, :, pl.ds(at, width)] = value.astype(BF16)
        early.append(launch(0, 0, order, parts[0], first[0]))

    masks = head_masks()
    for p in range(8):
        q2, k2, v2 = (qkv[:, i * 1024 + p * 128 : i * 1024 + p * 128 + 128] for i in range(3))
        d2 = d_att[:, p * 128 : p * 128 + 128]
        k_two, v_two = two_heads(k2, masks), two_heads(v2, masks)
        probs = softmax_pair(dot_t(q2, k_two) * 0.125)
        d_probs = dot_t(d2, v_two)
        d_scores = []
        for h in range(2):
            one = d_probs[:, h * 128 : h * 128 + 128]
            one = probs[h] * (one - jnp.sum(probs[h] * one, axis=-1, keepdims=True))
            d_scores.append(one * 0.125)
        d_scores = jnp.concatenate(d_scores, axis=1).astype(BF16)
        probs = jnp.concatenate(probs, axis=1).astype(BF16)
        d_k = t_dot(d_scores, q2)
        d_v = t_dot(probs, d2)
        rhs[own_rows, pl.ds(p * 128, 128)] = dot(d_scores, k_two).astype(BF16)
        rhs[own_rows, pl.ds(1024 + p * 128, 128)] = (
            d_k[:128] * masks[0] + d_k[128:] * masks[1]
        ).astype(BF16)
        rhs[own_rows, pl.ds(2048 + p * 128, 128)] = (
            d_v[:128] * masks[0] + d_v[128:] * masks[1]
        ).astype(BF16)
    late_swap = []
    for order in range(3):
        at = pl.ds(order * LATE, LATE)
        late_swap.append(swap(8 + order, rhs.at[own_rows, at], rhs.at[sib_rows, at]))
    early = [sum_one(0, order, early[order]) for order in range(3)]
    late = []
    for order in range(3):
        late_swap[order].wait_recv()
        for r in range(4):
            value = dot(
                lhs[order * 2, r * 128 : r * 128 + 128, :], rhs[:, order * LATE : order * LATE + LATE]
            )
            parts[1][order, r] = value.astype(BF16)
        late.append(launch(0, 1, order, parts[1], first[1]))
    early = [sum_two(0, order, early[order]) for order in range(3)]
    loads[1].wait()
    d_normed1 = dot_t(rhs[own_rows, pl.ds(0, 3072)], w_qkv[...])
    grad_tokens[...] = (d_resid + norm_backward(normed1, rstd1, d_normed1)).astype(BF16)
    late = [sum_one(1, order, late[order]) for order in range(3)]
    sum_proj[:, 0:384] = sum_three(0, 0, early[0])
    sum_proj[:, 384:768] = sum_three(0, 1, early[1])
    tail_sum = sum_three(0, 2, early[2])
    sum_proj[:, 768:1024] = tail_sum[:, :256]
    sum_router[...] = tail_sum[:, 256:320]
    late = [sum_two(1, order, late[order]) for order in range(3)]
    for order in range(3):
        sum_qkv[:, order * LATE : order * LATE + LATE] = sum_three(1, order, late[order])
    for c in started:
        c.wait_send()


def run_finish(*args):
    sem = pltpu.SemaphoreType.DMA
    shape = jax.ShapeDtypeStruct
    scratch = [
        pltpu.VMEM((1024, 3072), BF16),
        pltpu.VMEM((1024, 1024), BF16),
        pltpu.VMEM((512, 1024), BF16),
        pltpu.VMEM((3, 128, 1024), BF16),
        pltpu.VMEM((7, 512, 128), BF16),
        pltpu.VMEM((7, 512, 256), BF16),
        pltpu.VMEM((256, 4224), BF16),
        pltpu.VMEM((128, 1024), BF16),
    ]
    for lead, kind in (
        ((3, 4, 128), BF16),
        ((3, 3, 128), BF16),
        ((3, 4, 32), BF16),
        ((3, 3, 32), BF16),
        ((3, 4, 8), F32),
        ((3, 3, 8), F32),
    ):
        scratch += [pltpu.VMEM(lead + (width,), kind) for width in (EARLY, LATE)]
    scratch += [sem((2,)), sem((11,)), sem((11,)), sem((54,)), sem((54,))]
    return pl.pallas_call(
        finish_kernel,
        out_shape=[
            shape((128, 1024), BF16),
            shape((128, 1024), BF16),
            shape((8, 3072), F32),
            shape((8, 1024), F32),
            shape((8, 64), F32),
        ],
        in_specs=[VMEM] * 10 + [ANY] * 2 + [VMEM],
        out_specs=[VMEM] * 5,
        scratch_shapes=scratch,
        compiler_params=pltpu.CompilerParams(
            collective_id=3, has_side_effects=True, vmem_limit_bytes=48 * 2**20
        ),
        name="finish",
    )(*args)


def shards(tokens, cotangent, expert_ids, slot_ids, w_qkv, w_proj, w_router, w_in, w_out):
    other_in = lax.ppermute(w_in[0], "group", SWAP)
    other_out = lax.ppermute(w_out[0], "group", SWAP)
    flat = expert_ids * 8 + slot_ids
    x_blocks, g_blocks, m_blocks, resid, qkv, att, mix = run_attend(
        tokens, cotangent, expert_ids, slot_ids, expert_ids.T, flat.T, w_qkv, w_proj, w_router
    )
    returned_out, returned_in, grad_w_in, grad_w_out = run_experts(
        x_blocks, g_blocks, m_blocks, w_in[0], w_out[0], other_in, other_out
    )
    layer_out, grad_tokens, sum_qkv, sum_proj, sum_router = run_finish(
        returned_out, returned_in, tokens, cotangent, resid, qkv, att, mix, expert_ids, flat, w_qkv, w_proj, w_router
    )
    return (
        layer_out,
        grad_tokens,
        sum_qkv,
        sum_proj,
        sum_router,
        grad_w_in[None],
        grad_w_out[None],
    )


def solution(mesh):
    return jax.shard_map(
        shards,
        mesh=mesh,
        in_specs=(
            P(("group", "dev"), None),
            P(("group", "dev"), None),
            P(("group", "dev"), None),
            P(("group", "dev"), None),
            P(),
            P(),
            P(),
            P("dev", None, "group"),
            P("dev", "group", None),
        ),
        out_specs=(
            P(("group", "dev"), None),
            P(("group", "dev"), None),
            P(("group", "dev"), None),
            P(("group", "dev"), None),
            P(("group", "dev"), None),
            P("dev", None, "group"),
            P("dev", "group", None),
        ),
        check_vma=False,
    )
```

```python
import jax
import jax.numpy as jnp
from jax import lax
from jax.experimental import pallas as pl
from jax.experimental.pallas import tpu as pltpu
from jax.sharding import PartitionSpec as P

HEADS = 16
MESH = pl.DeviceIdType.MESH
BF16 = jnp.bfloat16
F32 = jnp.float32
VMEM = pl.BlockSpec(memory_space=pltpu.VMEM)
HBM = pl.BlockSpec(memory_space=pltpu.HBM)
CHUNK = 512


def peer_of(me, k):
    y = (me // 16 + k // 16) % 4
    z = (me // 4 + k // 4) % 4
    x = (me + k) % 4
    return y * 16 + z * 4 + x


def offset_of(j):
    r = j % 32
    y = r // 8
    z = (r // 2) % 4
    x = 2 * (r % 2) + (y + z + j // 32) % 2
    return y * 16 + z * 4 + x


def chip_before(me, k):
    y = (me // 16 + 4 - k // 16) % 4
    z = (me // 4 + 4 - (k // 4) % 4) % 4
    x = (me + 4 - k % 4) % 4
    return y * 16 + z * 4 + x


def dot(a, b):
    return jnp.dot(a, b, preferred_element_type=F32)


def dot_t(a, b):
    return lax.dot_general(a, b, (((1,), (1,)), ((), ())), preferred_element_type=F32)


def t_dot(a, b):
    return lax.dot_general(a, b, (((0,), (0,)), ((), ())), preferred_element_type=F32)


def norm_parts(rows32):
    center = rows32 - jnp.mean(rows32, axis=-1, keepdims=True)
    rstd = lax.rsqrt(jnp.mean(center * center, axis=-1, keepdims=True) + 1e-05)
    return center * rstd, rstd


def norm_backward(normed, rstd, d_normed):
    mean = jnp.mean(d_normed, axis=-1, keepdims=True)
    along_it = jnp.mean(d_normed * normed, axis=-1, keepdims=True)
    return rstd * (d_normed - mean - normed * along_it)


def head_masks():
    low = lax.broadcasted_iota(jnp.int32, (128, 128), 1) < 64
    return low.astype(F32), 1.0 - low.astype(F32)


def two_heads(pair, masks):
    wide = pair.astype(F32)
    return jnp.concatenate([wide * masks[0], wide * masks[1]], axis=0).astype(BF16)


def softmax_pair(scores):
    out = []
    for h in range(2):
        one = scores[:, h * 128 : h * 128 + 128]
        e = jnp.exp(one - jnp.max(one, axis=-1, keepdims=True))
        out.append(e / jnp.sum(e, axis=-1, keepdims=True))
    return out


def columns_of(row_ref):
    rows = row_ref[...].astype(F32)
    return [jnp.broadcast_to(rows[k : k + 1, :], (128, 128)).T.astype(jnp.int32) for k in range(2)]


def layer_kernel(*refs):
    tokens_in, cot_in, ids_in, slots_in, w_qkv_in, w_proj_in, w_router_in, w1_own, w2_own = refs[:9]
    ret_out, ret_in, resid_out, qkv_out, att_out, mix_out, grad_w1, grad_w2 = refs[9:17]
    tokens, cot, ids_row, slots_row, w_router, resid_buf, qkv, att, mix_buf = refs[17:26]
    w_qkv, w_proj, n2b, x_pack, g_pack, m_pack = refs[26:32]
    w1, w2, xs, gs, xm, gm, hid, dp, acc, pack_out, pack_in = refs[32:43]
    xm_sib, gm_sib, hid_sib, dp_sib, x_turn, stage1, stage2, x_buf, g_buf, m_buf = refs[43:53]
    in_sem, w_sem, push_send, push_recv, send_sem, recv_sem, home_send, home_recv = refs[53:61]
    own_sem, out_sem, sib_send, sib_recv, grad_sem = refs[61:66]
    g = lax.axis_index("group")
    me = lax.axis_index("dev")
    barrier = pltpu.get_barrier_semaphore()
    pl.semaphore_signal(barrier, inc=1, device_id=(1 - g, me), device_id_type=MESH)

    def greet(k, _):
        pl.semaphore_signal(barrier, inc=1, device_id=(g, peer_of(me, k)), device_id_type=MESH)
        return 0

    lax.fori_loop(1, 64, greet, 0)
    fetch = [
        pltpu.make_async_copy(src, dst, in_sem.at[7 + i])
        for i, (src, dst) in enumerate(
            (
                (ids_in, ids_row),
                (slots_in, slots_row),
                (cot_in, cot),
                (tokens_in, tokens),
                (w_router_in, w_router),
            )
        )
    ]
    loads = []
    for c in range(6):
        at = pl.ds(c * 512, 512)
        loads.append(pltpu.make_async_copy(w_qkv_in.at[:, at], w_qkv.at[:, at], in_sem.at[c]))
    loads.append(pltpu.make_async_copy(w_proj_in, w_proj, in_sem.at[6]))
    for c in fetch[:4] + loads + fetch[4:]:
        c.start()

    started = []

    def to_sibling(src, dst, send, recv):
        c = pltpu.make_async_remote_copy(
            src_ref=src,
            dst_ref=dst,
            send_sem=send,
            recv_sem=recv,
            device_id=(1 - g, me),
            device_id_type=MESH,
        )
        c.start()
        started.append(c)
        return c

    def weights(c):
        at = pl.ds(c * CHUNK, CHUNK)
        return w1_own.at[:, at], w2_own.at[at, :]

    def dispatch(src, pack):
        for i in range(4):
            at = lax.broadcasted_iota(jnp.int32, (128, 128), 0) + i * 128
            hit = (at == flat_row[0:1, :]) | (at == flat_row[1:2, :])
            place = hit.astype(F32).astype(BF16)
            halves = [dot(place, src[:, h * 512 : h * 512 + 512]).reshape(16, 8, 512) for h in range(2)]
            pack[pl.ds(i * 16, 16)] = jnp.concatenate(halves, axis=1).astype(BF16)

    packs, bufs = (x_pack, g_pack, m_pack), (x_buf, g_buf, m_buf)

    def out_copy(i, j):
        peer = peer_of(me, offset_of(j))
        return pltpu.make_async_remote_copy(
            src_ref=packs[i].at[peer],
            dst_ref=bufs[i].at[j],
            send_sem=send_sem.at[i, j],
            recv_sem=recv_sem.at[i, j],
            device_id=(g, peer),
            device_id_type=MESH,
        )

    def own_copy(i):
        return pltpu.make_async_copy(packs[i].at[me], bufs[i].at[0], own_sem.at[i])

    def over(low, high, action):
        def one(j, _):
            action(j)
            return 0

        lax.fori_loop(low, high, one, 0)

    def send_out(i, half):
        if half == 0:
            own_copy(i).start()
        over(1 + 31 * half, 32 + 32 * half, lambda j: out_copy(i, j).start())

    def take_in(i, half):
        if half == 0:
            own_copy(i).wait()
        over(1 + 31 * half, 32 + 32 * half, lambda j: out_copy(i, j).wait_recv())

    for c in fetch[:3]:
        c.wait()
    flat_row = ids_row[...] * 8 + slots_row[...]
    dispatch(cot, g_pack)
    pl.semaphore_wait(barrier, 64)
    send_out(1, 0)
    pushes = []
    for c in range(4):
        for i, (src, dst) in enumerate(zip(weights(c), (w1, w2))):
            sem = 2 * c + i
            pushes.append(to_sibling(src, dst.at[c], push_send.at[sem], push_recv.at[sem]))
    own_loads = []
    for c in range(4):
        for i, (src, dst) in enumerate(zip(weights(c), (w1, w2))):
            own_loads.append(pltpu.make_async_copy(src, dst.at[4 + c], w_sem.at[2 * c + i]))
            own_loads[-1].start()

    fetch[3].wait()
    rows32 = tokens[...].astype(F32)
    normed, _ = norm_parts(rows32)
    normed_b = normed.astype(BF16)
    for c in range(6):
        loads[c].wait()
        at = pl.ds(c * 512, 512)
        qkv[:, at] = dot(normed_b, w_qkv[:, at]).astype(BF16)
    masks = head_masks()
    for p in range(8):
        q2, k2, v2 = (qkv[:, i * 1024 + p * 128 : i * 1024 + p * 128 + 128] for i in range(3))
        probs = softmax_pair(dot_t(q2, two_heads(k2, masks)) * 0.125)
        probs = jnp.concatenate(probs, axis=1).astype(BF16)
        att[:, p * 128 : p * 128 + 128] = dot(probs, two_heads(v2, masks)).astype(BF16)
    loads[6].wait()
    resid = (rows32 + dot(att[...], w_proj[...])).astype(BF16)
    resid_buf[...] = resid
    normed2, _ = norm_parts(resid.astype(F32))
    n2b[...] = normed2.astype(BF16)
    dispatch(n2b, x_pack)
    send_out(0, 0)
    send_out(0, 1)

    leaving = [
        pltpu.make_async_copy(src, dst, out_sem.at[i])
        for i, (src, dst) in enumerate(((resid_buf, resid_out), (qkv, qkv_out), (att, att_out)))
    ]
    for c in leaving:
        c.start()
    fetch[4].wait()
    logits = dot_t(n2b[...], w_router[...])
    ids, slots = columns_of(ids_row), columns_of(slots_row)
    expert = lax.broadcasted_iota(jnp.int32, (128, 64), 1)
    picked = [
        jnp.sum(jnp.where(expert == ids[k][:, :64], logits, 0.0), axis=-1, keepdims=True)
        for k in range(2)
    ]
    top = jnp.maximum(picked[0], picked[1])
    e = [jnp.exp(a - top) for a in picked]
    lane = lax.broadcasted_iota(jnp.int32, (128, 128), 1)
    owner = lax.broadcasted_iota(jnp.int32, (64, 128), 0)
    table = jnp.zeros((64, 128), F32)
    for k in range(2):
        mix = e[k] / (e[0] + e[1])
        mix_buf[:, k * 128 : k * 128 + 128] = jnp.broadcast_to(mix, (128, 128))
        spread = jnp.where(lane == slots[k], mix, 0.0)
        high = spread.astype(BF16)
        low = (spread - high.astype(F32)).astype(BF16)
        hot = (owner == ids_row[k : k + 1, :]).astype(F32).astype(BF16)
        table = table + dot(hot, high) + dot(hot, low)
    m_pack[...] = table.reshape(64, 1, 128)
    send_out(2, 0)
    send_out(2, 1)
    send_out(1, 1)
    leaving.append(pltpu.make_async_copy(mix_buf, mix_out, out_sem.at[3]))
    leaving[3].start()

    def unpack(i, half, plain):
        def one(b):
            block = bufs[i][pl.ds(b * 8, 8)].astype(F32)
            at = pl.ds(pl.multiple_of(b * 64, 64), 64)
            for h in range(2):
                piece = block[:, h * 8 : h * 8 + 8, :].reshape(64, 512)
                plain[at, pl.ds(h * 512, 512)] = piece.astype(BF16)

        over(4 * half, 4 * half + 4, one)

    def scale(half):
        lanes = lax.broadcasted_iota(jnp.int32, (8, 8, 128), 2)
        sub = lax.broadcasted_iota(jnp.int32, (8, 8, 128), 1)

        def one(b):
            spread = jnp.broadcast_to(m_buf[pl.ds(b * 8, 8)], (8, 8, 128))
            mix = jnp.sum(jnp.where(lanes == sub, spread, 0.0), axis=2, keepdims=True).reshape(64, 1)
            at = pl.ds(pl.multiple_of(b * 64, 64), 64)
            for plain, mixed in ((xs, xm), (gs, gm)):
                mixed[at, :] = (plain[at, :].astype(F32) * mix).astype(BF16)

        over(4 * half, 4 * half + 4, one)

    def forward(half, group):
        rows = pl.ds(half * 256, 256)

        def one(i):
            for c in (2 * i, 2 * i + 1):
                if half == 0:
                    for n, w in enumerate((w1, w2)):
                        if group == 1:
                            src = weights(0)[n]
                            pltpu.make_async_copy(src, w.at[c], w_sem.at[2 * (c - 4) + n]).wait()
                        else:
                            pltpu.make_async_remote_copy(
                                src_ref=weights(0)[n],
                                dst_ref=w.at[c],
                                send_sem=push_send.at[2 * c + n],
                                recv_sem=push_recv.at[2 * c + n],
                                device_id=(1 - g, me),
                                device_id_type=MESH,
                            ).wait_recv()
                pre = dot(xs[rows, :], w1[c])
                cdf = 0.5 * (1.0 + lax.erf(pre * (0.5**0.5)))
                pdf = jnp.exp(-0.5 * pre * pre) * 0.3989422804014327
                hid[c, rows, :] = (pre * cdf).astype(BF16)
                dp[c, rows, :] = (cdf + pre * pdf).astype(BF16)
            acc[rows, :] += dot(hid[2 * i, rows, :], w2[2 * i]) + dot(hid[2 * i + 1, rows, :], w2[2 * i + 1])

        over(2 * group, 2 * group + 2, one)

    def backward(half, group):
        rows = pl.ds(half * 256, 256)

        def one(i):
            for c in (2 * i, 2 * i + 1):
                d_hidden = dot_t(gs[rows, :], w2[c])
                dp[c, rows, :] = (dp[c, rows, :].astype(F32) * d_hidden).astype(BF16)
            acc[rows, :] += dot_t(dp[2 * i, rows, :], w1[2 * i]) + dot_t(dp[2 * i + 1, rows, :], w1[2 * i + 1])

        over(2 * group, 2 * group + 2, one)

    def home(n, j):
        src, dst = ((pack_out, ret_out), (pack_in, ret_in))[n]
        return pltpu.make_async_remote_copy(
            src_ref=src.at[j],
            dst_ref=dst.at[me],
            send_sem=home_send.at[n, j],
            recv_sem=home_recv.at[n, j],
            device_id=(g, chip_before(me, offset_of(j))),
            device_id_type=MESH,
        )

    def own_home(n):
        src, dst = ((pack_out, ret_out), (pack_in, ret_in))[n]
        return pltpu.make_async_copy(src.at[0], dst.at[me], own_sem.at[3 + n])

    def send_home(n, half):
        target = (pack_out, pack_in)[n]

        def one(b):
            value = acc[pl.ds(pl.multiple_of(b * 64, 64), 64), :].reshape(8, 8, 1024)
            both = jnp.concatenate([value[:, :, :512], value[:, :, 512:]], axis=1)
            target[pl.ds(b * 8, 8)] = both.astype(BF16)

        over(4 * half, 4 * half + 4, one)
        if half == 0:
            own_home(n).start()
        over(1 + 31 * half, 32 + 32 * half, lambda j: home(n, j).start())

    def clear(half):
        rows = pl.ds(half * 256, 256)
        acc[rows, :] = jnp.zeros((256, 1024), F32)

    swaps = []

    def share(src, dst):
        n = len(swaps)
        swaps.append(to_sibling(src, dst, sib_send.at[n], sib_recv.at[n]))

    for half in range(2):
        rows = pl.ds(half * 256, 256)
        clear(half)
        take_in(0, half)
        unpack(0, half, xs)
        forward(half, 1)
        forward(half, 0)
        send_home(0, half)
        share(hid.at[pl.ds(0, 4), rows, :], hid_sib.at[:, rows, :])
    take_in(2, 0)
    take_in(2, 1)
    for half in range(2):
        rows = pl.ds(half * 256, 256)
        clear(half)
        take_in(1, half)
        unpack(1, half, gs)
        backward(half, 0)
        share(dp.at[pl.ds(0, 4), rows, :], dp_sib.at[:, rows, :])
        backward(half, 1)
        send_home(1, half)
        scale(half)
        share(xm.at[rows, :], xm_sib.at[rows, :])
        share(gm.at[rows, :], gm_sib.at[rows, :])

    def grad_copy(c, which):
        at = pl.ds(pl.multiple_of(c * CHUNK, CHUNK), CHUNK)
        source = stage1 if which == 0 else stage2
        target = grad_w1.at[:, at] if which == 0 else grad_w2.at[at, :]
        return pltpu.make_async_copy(source, target, grad_sem.at[which])

    for r in range(4):
        x_turn[:, pl.ds(r * 128, 128)] = xm[pl.ds(r * 128, 128), :].T
    for c in swaps:
        c.wait_recv()
    for r in range(4):
        x_turn[:, pl.ds(512 + r * 128, 128)] = xm_sib[pl.ds(r * 128, 128), :].T

    def grads(c):
        @pl.when(c > 0)
        def _():
            grad_copy(c - 1, 0).wait()

        for r in range(4):
            rows = pl.ds(r * 256, 256)
            stage1[rows, :] = (
                dot(x_turn[rows, pl.ds(0, 512)], dp[4 + c])
                + dot(x_turn[rows, pl.ds(512, 512)], dp_sib[c])
            ).astype(BF16)
        grad_copy(c, 0).start()

        @pl.when(c > 0)
        def _():
            grad_copy(c - 1, 1).wait()

        for r in range(2):
            columns = pl.ds(r * 256, 256)
            stage2[columns, :] = (
                t_dot(hid[4 + c, :, columns], gm[...]) + t_dot(hid_sib[c, :, columns], gm_sib[...])
            ).astype(BF16)
        grad_copy(c, 1).start()

    over(0, 4, grads)
    grad_copy(3, 0).wait()
    grad_copy(3, 1).wait()

    def finish(j):
        for i in range(3):
            out_copy(i, j).wait_send()
        for n in range(2):
            home(n, j).wait()

    over(1, 64, finish)
    for n in range(2):
        own_home(n).wait()
    for c in leaving:
        c.wait()
    for c in started:
        c.wait_send()


def run_layer(*args):
    sem = pltpu.SemaphoreType.DMA
    shape = jax.ShapeDtypeStruct
    return pl.pallas_call(
        layer_kernel,
        out_shape=[
            shape((64, 16, 512), BF16),
            shape((64, 16, 512), BF16),
            shape((128, 1024), BF16),
            shape((128, 3072), BF16),
            shape((128, 1024), BF16),
            shape((128, 256), F32),
            shape((1024, 2048), BF16),
            shape((2048, 1024), BF16),
        ],
        in_specs=[HBM] * 9,
        out_specs=[HBM] * 8,
        scratch_shapes=[
            pltpu.VMEM((128, 1024), BF16),
            pltpu.VMEM((128, 1024), BF16),
            pltpu.VMEM((2, 128), jnp.int32),
            pltpu.VMEM((2, 128), jnp.int32),
            pltpu.VMEM((64, 1024), BF16),
            pltpu.VMEM((128, 1024), BF16),
            pltpu.VMEM((128, 3072), BF16),
            pltpu.VMEM((128, 1024), BF16),
            pltpu.VMEM((128, 256), F32),
            pltpu.VMEM((1024, 3072), BF16),
            pltpu.VMEM((1024, 1024), BF16),
            pltpu.VMEM((128, 1024), BF16),
            pltpu.VMEM((64, 16, 512), BF16),
            pltpu.VMEM((64, 16, 512), BF16),
            pltpu.VMEM((64, 1, 128), F32),
            pltpu.VMEM((8, 1024, CHUNK), BF16),
            pltpu.VMEM((8, CHUNK, 1024), BF16),
            pltpu.VMEM((512, 1024), BF16),
            pltpu.VMEM((512, 1024), BF16),
            pltpu.VMEM((512, 1024), BF16),
            pltpu.VMEM((512, 1024), BF16),
            pltpu.VMEM((8, 512, CHUNK), BF16),
            pltpu.VMEM((8, 512, CHUNK), BF16),
            pltpu.VMEM((512, 1024), F32),
            pltpu.VMEM((64, 16, 512), BF16),
            pltpu.VMEM((64, 16, 512), BF16),
            pltpu.VMEM((512, 1024), BF16),
            pltpu.VMEM((512, 1024), BF16),
            pltpu.VMEM((4, 512, CHUNK), BF16),
            pltpu.VMEM((4, 512, CHUNK), BF16),
            pltpu.VMEM((1024, 1024), BF16),
            pltpu.VMEM((1024, CHUNK), BF16),
            pltpu.VMEM((CHUNK, 1024), BF16),
            pltpu.VMEM((64, 16, 512), BF16),
            pltpu.VMEM((64, 16, 512), BF16),
            pltpu.VMEM((64, 1, 128), F32),
            sem((12,)),
            sem((8,)),
            sem((8,)),
            sem((8,)),
            sem((3, 64)),
            sem((3, 64)),
            sem((2, 64)),
            sem((2, 64)),
            sem((5,)),
            sem((4,)),
            sem((8,)),
            sem((8,)),
            sem((2,)),
        ],
        compiler_params=pltpu.CompilerParams(
            collective_id=1, has_side_effects=True, vmem_limit_bytes=63 * 2**20
        ),
        name="layer",
    )(*args)


ORDERS = ((16, 4, 1), (4, 1, 16), (1, 16, 4))
EARLY, LATE = 384, 1024


def along(me, stride, k):
    at = (me // stride) % 4
    return me - at * stride + ((at + k) % 4) * stride


def natural_row(order, j):
    row = j % 8
    for at, stride in zip((128, 32, 8), ORDERS[order]):
        row = row + ((j // at) % 4) * (stride * 8)
    return row


def finish_kernel(*refs):
    layer_out, grad_tokens, sum_qkv, sum_proj, sum_router = refs[13:18]
    tokens, resid, att, ids_row, slots_row, ret_out, cot, mix, ret_in, w_router, w_proj, qkv, w_qkv = refs[18:31]
    rows, half_in, half_send, lhs, rhs, d_att = refs[31:37]
    parts, first, mid, second, last, third = (refs[37 + 2 * i : 39 + 2 * i] for i in range(6))
    w_sem, pair_send, pair_recv, send_sem, recv_sem = refs[49:54]
    g = lax.axis_index("group")
    me = lax.axis_index("dev")
    barrier = pltpu.get_barrier_semaphore()
    pl.semaphore_signal(barrier, inc=1, device_id=(1 - g, me), device_id_type=MESH)
    for stride in (16, 4, 1):
        for k in (1, 2, 3):
            pl.semaphore_signal(
                barrier, inc=1, device_id=(g, along(me, stride, k)), device_id_type=MESH
            )
    loads = [pltpu.make_async_copy(refs[i], refs[18 + i], w_sem.at[i]) for i in range(13)]
    for c in loads:
        c.start()

    def arrive(*which):
        for i in which:
            loads[i].wait()

    started = []

    def swap(i, src, dst):
        c = pltpu.make_async_remote_copy(
            src_ref=src,
            dst_ref=dst,
            send_sem=pair_send.at[i],
            recv_sem=pair_recv.at[i],
            device_id=(1 - g, me),
            device_id_type=MESH,
        )
        c.start()
        started.append(c)
        return c

    arrive(0, 1, 2)
    normed1, rstd1 = norm_parts(tokens[...].astype(F32))
    resid_f = resid[...].astype(F32)
    normed2, rstd2 = norm_parts(resid_f)
    half_in[0] = normed1.astype(BF16)
    half_in[1] = att[...]
    half_in[2] = normed2.astype(BF16)
    column = lax.broadcasted_iota(jnp.int32, (512, 512), 1)
    position = lax.broadcasted_iota(jnp.int32, (512, 512), 0)
    mine = pl.ds(pl.multiple_of(g * 512, 512), 512)
    theirs = pl.ds(pl.multiple_of((1 - g) * 512, 512), 512)
    for order in range(3):
        turn = (column == natural_row(order, position)).astype(F32).astype(BF16)
        for which in range(3):
            if which == 2 and order < 2:
                continue
            i = order * 2 + which
            lhs[i, :, 0:128] = dot_t(turn, half_in[which, :, mine]).astype(BF16)
            half_send[i] = dot_t(turn, half_in[which, :, theirs]).astype(BF16)
    pl.semaphore_wait(barrier, 10)
    lhs_swap = [swap(i, half_send.at[i], lhs.at[i, :, pl.ds(128, 128)]) for i in range(7)]

    def unpack(src):
        def one(i, _):
            block = src[pl.ds(i * 8, 8)].astype(F32)
            at = pl.ds(pl.multiple_of(i * 64, 64), 64)
            for h in range(2):
                piece = block[:, h * 8 : h * 8 + 8, :].reshape(64, 512)
                rows[at, pl.ds(h * 512, 512)] = piece.astype(BF16)
            return 0

        lax.fori_loop(0, 8, one, 0)

    arrive(3, 4, 5, 6, 7)
    slot = lax.broadcasted_iota(jnp.int32, (128, 128), 1)
    ids, slots = columns_of(ids_row), columns_of(slots_row)
    place = []
    for k in range(2):
        flat = ids[k] * 8 + slots[k]
        hits = [(slot + i * 128 == flat).astype(F32).astype(BF16) for i in range(4)]
        place.append(jnp.concatenate(hits, axis=1))
    place = jnp.concatenate(place, axis=0)
    grad = cot[...].astype(F32)
    mixing = [mix[:, k * 128 : k * 128 + 1] for k in range(2)]
    unpack(ret_out)
    pair = dot(place, rows[...])
    pair = [pair[:128], pair[128:]]
    layer_out[...] = (resid_f + mixing[0] * pair[0] + mixing[1] * pair[1]).astype(BF16)
    d_mix = [jnp.sum(grad * a, axis=-1, keepdims=True) for a in pair]
    centre = mixing[0] * d_mix[0] + mixing[1] * d_mix[1]
    expert = lax.broadcasted_iota(jnp.int32, (128, 128), 1)
    d_logits = sum(
        jnp.where(expert == ids[k], mixing[k] * (d_mix[k] - centre), 0.0) for k in range(2)
    ).astype(BF16)
    arrive(8, 9)
    unpack(ret_in)
    pair = dot(place, rows[...])
    d_normed2 = (
        mixing[0] * pair[:128] + mixing[1] * pair[128:] + dot(d_logits[:, :64], w_router[...])
    )
    d_resid = grad + norm_backward(normed2, rstd2, d_normed2)
    own_rows, sib_rows = pl.ds(0, 128), pl.ds(128, 128)
    rhs[own_rows, pl.ds(3072, 1024)] = d_resid.astype(BF16)
    rhs[own_rows, pl.ds(4096, 128)] = d_logits
    tail = pl.ds(3072, 1152)
    early_swap = swap(7, rhs.at[own_rows, tail], rhs.at[sib_rows, tail])
    arrive(10)
    d_att[...] = dot_t(rhs[own_rows, pl.ds(3072, 1024)], w_proj[...]).astype(BF16)

    def place_of(phase, order):
        return (me // ORDERS[order][phase]) % 4

    def launch(phase, late, order, src, dst):
        stride = ORDERS[order][phase]
        at = place_of(phase, order)
        group = []
        for k in (1, 2, 3):
            sem = ((phase * 2 + late) * 3 + order) * 3 + k - 1
            c = pltpu.make_async_remote_copy(
                src_ref=src.at[order, (at + k) % 4],
                dst_ref=dst.at[order, k - 1],
                send_sem=send_sem.at[sem],
                recv_sem=recv_sem.at[sem],
                device_id=(g, along(me, stride, k)),
                device_id_type=MESH,
            )
            c.start()
            group.append(c)
        started.extend(group)
        return group

    def sum_one(late, order, arriving):
        for c in arriving:
            c.wait_recv()
        at = place_of(0, order)
        for q in range(4):
            piece = pl.ds(q * 32, 32)
            total = parts[late][order, at, piece, :].astype(F32)
            for k in range(3):
                total = total + first[late][order, k, piece, :].astype(F32)
            mid[late][order, q] = total.astype(BF16)
        return launch(1, late, order, mid[late], second[late])

    def sum_two(late, order, arriving):
        for c in arriving:
            c.wait_recv()
        total = mid[late][order, place_of(1, order)].astype(F32)
        for k in range(3):
            total = total + second[late][order, k].astype(F32)
        for q in range(4):
            last[late][order, q] = total[q * 8 : q * 8 + 8, :]
        return launch(2, late, order, last[late], third[late])

    def sum_three(late, order, arriving):
        for c in arriving:
            c.wait_recv()
        total = last[late][order, place_of(2, order)]
        for k in range(3):
            total = total + third[late][order, k]
        return total

    for c in lhs_swap:
        c.wait_recv()
    early_swap.wait_recv()
    early = []
    for order in range(3):
        for r in range(4):
            for left, at, width in (
                (order * 2 + 1, 0, EARLY if order < 2 else 256),
                (6, 256, 128),
            ):
                if left == 6 and order < 2:
                    continue
                value = dot(
                    lhs[left, r * 128 : r * 128 + 128, :],
                    rhs[:, 3072 + order * EARLY + at : 3072 + order * EARLY + at + width],
                )
                parts[0][order, r, :, pl.ds(at, width)] = value.astype(BF16)
        early.append(launch(0, 0, order, parts[0], first[0]))

    arrive(11)
    masks = head_masks()
    for p in range(8):
        q2, k2, v2 = (qkv[:, i * 1024 + p * 128 : i * 1024 + p * 128 + 128] for i in range(3))
        d2 = d_att[:, p * 128 : p * 128 + 128]
        k_two, v_two = two_heads(k2, masks), two_heads(v2, masks)
        probs = softmax_pair(dot_t(q2, k_two) * 0.125)
        d_probs = dot_t(d2, v_two)
        d_scores = []
        for h in range(2):
            one = d_probs[:, h * 128 : h * 128 + 128]
            one = probs[h] * (one - jnp.sum(probs[h] * one, axis=-1, keepdims=True))
            d_scores.append(one * 0.125)
        d_scores = jnp.concatenate(d_scores, axis=1).astype(BF16)
        probs = jnp.concatenate(probs, axis=1).astype(BF16)
        d_k = t_dot(d_scores, q2)
        d_v = t_dot(probs, d2)
        rhs[own_rows, pl.ds(p * 128, 128)] = dot(d_scores, k_two).astype(BF16)
        rhs[own_rows, pl.ds(1024 + p * 128, 128)] = (
            d_k[:128] * masks[0] + d_k[128:] * masks[1]
        ).astype(BF16)
        rhs[own_rows, pl.ds(2048 + p * 128, 128)] = (
            d_v[:128] * masks[0] + d_v[128:] * masks[1]
        ).astype(BF16)
    late_swap = []
    for order in range(3):
        at = pl.ds(order * LATE, LATE)
        late_swap.append(swap(8 + order, rhs.at[own_rows, at], rhs.at[sib_rows, at]))
    early = [sum_one(0, order, early[order]) for order in range(3)]
    late = []
    for order in range(3):
        late_swap[order].wait_recv()
        for r in range(4):
            value = dot(
                lhs[order * 2, r * 128 : r * 128 + 128, :], rhs[:, order * LATE : order * LATE + LATE]
            )
            parts[1][order, r] = value.astype(BF16)
        late.append(launch(0, 1, order, parts[1], first[1]))
    early = [sum_two(0, order, early[order]) for order in range(3)]
    arrive(12)
    d_normed1 = dot_t(rhs[own_rows, pl.ds(0, 3072)], w_qkv[...])
    grad_tokens[...] = (d_resid + norm_backward(normed1, rstd1, d_normed1)).astype(BF16)
    late = [sum_one(1, order, late[order]) for order in range(3)]
    sum_proj[:, 0:384] = sum_three(0, 0, early[0])
    sum_proj[:, 384:768] = sum_three(0, 1, early[1])
    tail_sum = sum_three(0, 2, early[2])
    sum_proj[:, 768:1024] = tail_sum[:, :256]
    sum_router[...] = tail_sum[:, 256:320]
    late = [sum_two(1, order, late[order]) for order in range(3)]
    for order in range(3):
        sum_qkv[:, order * LATE : order * LATE + LATE] = sum_three(1, order, late[order])
    for c in started:
        c.wait_send()


def run_finish(*args):
    sem = pltpu.SemaphoreType.DMA
    shape = jax.ShapeDtypeStruct
    scratch = [pltpu.VMEM(a.shape, a.dtype) for a in args]
    scratch += [
        pltpu.VMEM((512, 1024), BF16),
        pltpu.VMEM((3, 128, 1024), BF16),
        pltpu.VMEM((7, 512, 128), BF16),
        pltpu.VMEM((7, 512, 256), BF16),
        pltpu.VMEM((256, 4224), BF16),
        pltpu.VMEM((128, 1024), BF16),
    ]
    for lead, kind in (
        ((3, 4, 128), BF16),
        ((3, 3, 128), BF16),
        ((3, 4, 32), BF16),
        ((3, 3, 32), BF16),
        ((3, 4, 8), F32),
        ((3, 3, 8), F32),
    ):
        scratch += [pltpu.VMEM(lead + (width,), kind) for width in (EARLY, LATE)]
    scratch += [sem((13,)), sem((11,)), sem((11,)), sem((54,)), sem((54,))]
    return pl.pallas_call(
        finish_kernel,
        out_shape=[
            shape((128, 1024), BF16),
            shape((128, 1024), BF16),
            shape((8, 3072), F32),
            shape((8, 1024), F32),
            shape((8, 64), F32),
        ],
        in_specs=[HBM] * 13,
        out_specs=[VMEM] * 5,
        scratch_shapes=scratch,
        compiler_params=pltpu.CompilerParams(
            collective_id=3, has_side_effects=True, vmem_limit_bytes=53 * 2**20
        ),
        name="finish",
    )(*args)


def store_kernel(*refs):
    srcs, dsts, sems = refs[:7], refs[7:14], refs[14]
    copies = [pltpu.make_async_copy(srcs[i], dsts[i], sems.at[i]) for i in range(5)]
    for i in (5, 6):
        rows = srcs[i].shape[0] // 8
        for j in range(8):
            at = pl.ds(j * rows, rows)
            sem = sems.at[5 + (i - 5) * 8 + j]
            copies.append(pltpu.make_async_copy(srcs[i].at[at, :], dsts[i].at[at, :], sem))
    for c in copies:
        c.start()
    for c in copies:
        c.wait()


def run_store(*arrays):
    return pl.pallas_call(
        store_kernel,
        out_shape=[jax.ShapeDtypeStruct(a.shape, a.dtype) for a in arrays],
        in_specs=[VMEM] * 5 + [VMEM] * 2,
        out_specs=[HBM] * 7,
        scratch_shapes=[pltpu.SemaphoreType.DMA((21,))],
        compiler_params=pltpu.CompilerParams(vmem_limit_bytes=12 * 2**20),
        name="store",
    )(*arrays)


def shards(tokens, cotangent, expert_ids, slot_ids, w_qkv, w_proj, w_router, w_in, w_out):
    ids, slots, router = expert_ids.T, slot_ids.T, w_router.T
    returned_out, returned_in, resid, qkv, att, mix, grad_w_in, grad_w_out = run_layer(
        tokens, cotangent, ids, slots, w_qkv, w_proj, router, w_in[0], w_out[0]
    )
    small = run_finish(
        tokens, resid, att, ids, slots, returned_out, cotangent, mix, returned_in, router, w_proj, qkv, w_qkv
    )
    layer_out, grad_tokens, sum_qkv, sum_proj, sum_router, grad_w_in, grad_w_out = run_store(
        *small, grad_w_in, grad_w_out
    )
    return (
        layer_out,
        grad_tokens,
        sum_qkv,
        sum_proj,
        sum_router,
        grad_w_in[None],
        grad_w_out[None],
    )


def solution(mesh):
    return jax.shard_map(
        shards,
        mesh=mesh,
        in_specs=(
            P(("group", "dev"), None),
            P(("group", "dev"), None),
            P(("group", "dev"), None),
            P(("group", "dev"), None),
            P(),
            P(),
            P(),
            P("dev", None, "group"),
            P("dev", "group", None),
        ),
        out_specs=(
            P(("group", "dev"), None),
            P(("group", "dev"), None),
            P(("group", "dev"), None),
            P(("group", "dev"), None),
            P(("group", "dev"), None),
            P("dev", None, "group"),
            P("dev", "group", None),
        ),
        check_vma=False,
    )
```

```python
import jax
import jax.numpy as jnp
from jax import lax
from jax.experimental import pallas as pl
from jax.experimental.pallas import tpu as pltpu
from jax.sharding import PartitionSpec as P

HEADS = 16
MESH = pl.DeviceIdType.MESH
BF16 = jnp.bfloat16
F32 = jnp.float32
VMEM = pl.BlockSpec(memory_space=pltpu.VMEM)
HBM = pl.BlockSpec(memory_space=pltpu.HBM)
CHUNK = 512


def peer_of(me, k):
    y = (me // 16 + k // 16) % 4
    z = (me // 4 + k // 4) % 4
    x = (me + k) % 4
    return y * 16 + z * 4 + x


def offset_of(j):
    r = j % 32
    y = r // 8
    z = (r // 2) % 4
    x = 2 * (r % 2) + (y + z + j // 32) % 2
    return y * 16 + z * 4 + x


def chip_before(me, k):
    y = (me // 16 + 4 - k // 16) % 4
    z = (me // 4 + 4 - (k // 4) % 4) % 4
    x = (me + 4 - k % 4) % 4
    return y * 16 + z * 4 + x


def dot(a, b):
    return jnp.dot(a, b, preferred_element_type=F32)


def dot_t(a, b):
    return lax.dot_general(a, b, (((1,), (1,)), ((), ())), preferred_element_type=F32)


def t_dot(a, b):
    return lax.dot_general(a, b, (((0,), (0,)), ((), ())), preferred_element_type=F32)


def norm_parts(rows32):
    center = rows32 - jnp.mean(rows32, axis=-1, keepdims=True)
    rstd = lax.rsqrt(jnp.mean(center * center, axis=-1, keepdims=True) + 1e-05)
    return center * rstd, rstd


def norm_backward(normed, rstd, d_normed):
    mean = jnp.mean(d_normed, axis=-1, keepdims=True)
    along_it = jnp.mean(d_normed * normed, axis=-1, keepdims=True)
    return rstd * (d_normed - mean - normed * along_it)


def head_masks():
    low = lax.broadcasted_iota(jnp.int32, (128, 128), 1) < 64
    return low.astype(F32), 1.0 - low.astype(F32)


def two_heads(pair, masks):
    wide = pair.astype(F32)
    return jnp.concatenate([wide * masks[0], wide * masks[1]], axis=0).astype(BF16)


def softmax_pair(scores):
    out = []
    for h in range(2):
        one = scores[:, h * 128 : h * 128 + 128]
        e = jnp.exp(one - jnp.max(one, axis=-1, keepdims=True))
        out.append(e / jnp.sum(e, axis=-1, keepdims=True))
    return out


def columns_of(row_ref):
    rows = row_ref[...].astype(F32)
    return [jnp.broadcast_to(rows[k : k + 1, :], (128, 128)).T.astype(jnp.int32) for k in range(2)]


def layer_kernel(*refs):
    tokens_in, cot_in, ids_in, slots_in, w_qkv_in, w_proj_in, w_router_in, w1_own, w2_own = refs[:9]
    ret_out, ret_in, resid_out, qkv_out, att_out, mix_out, grad_w1, grad_w2 = refs[9:17]
    tokens, cot, ids_row, slots_row, w_router, resid_buf, qkv, att, mix_buf = refs[17:26]
    w_qkv, w_proj, n2b, x_pack, g_pack, m_pack = refs[26:32]
    w1, w2, xs, gs, xm, gm, hid, dp, acc, pack_out, pack_in = refs[32:43]
    xm_sib, gm_sib, hid_sib, dp_sib, stage1, stage2, x_buf, g_buf, m_buf = refs[43:52]
    in_sem, w_sem, push_send, push_recv, send_sem, recv_sem, home_send, home_recv = refs[52:60]
    own_sem, out_sem, sib_send, sib_recv, grad_sem = refs[60:65]
    g = lax.axis_index("group")
    me = lax.axis_index("dev")
    barrier = pltpu.get_barrier_semaphore()
    pl.semaphore_signal(barrier, inc=1, device_id=(1 - g, me), device_id_type=MESH)

    def greet(k, _):
        pl.semaphore_signal(barrier, inc=1, device_id=(g, peer_of(me, k)), device_id_type=MESH)
        return 0

    lax.fori_loop(1, 64, greet, 0)
    fetch = [
        pltpu.make_async_copy(src, dst, in_sem.at[7 + i])
        for i, (src, dst) in enumerate(
            (
                (ids_in, ids_row),
                (slots_in, slots_row),
                (cot_in, cot),
                (tokens_in, tokens),
                (w_router_in, w_router),
            )
        )
    ]
    loads = []
    for c in range(6):
        at = pl.ds(c * 512, 512)
        loads.append(pltpu.make_async_copy(w_qkv_in.at[:, at], w_qkv.at[:, at], in_sem.at[c]))
    loads.append(pltpu.make_async_copy(w_proj_in, w_proj, in_sem.at[6]))
    for c in fetch[:4] + loads + fetch[4:]:
        c.start()

    started = []

    def to_sibling(src, dst, send, recv):
        c = pltpu.make_async_remote_copy(
            src_ref=src,
            dst_ref=dst,
            send_sem=send,
            recv_sem=recv,
            device_id=(1 - g, me),
            device_id_type=MESH,
        )
        c.start()
        started.append(c)
        return c

    def weights(c):
        at = pl.ds(c * CHUNK, CHUNK)
        return w1_own.at[:, at], w2_own.at[at, :]

    def dispatch(src, pack):
        for i in range(4):
            at = lax.broadcasted_iota(jnp.int32, (128, 128), 0) + i * 128
            hit = (at == flat_row[0:1, :]) | (at == flat_row[1:2, :])
            place = hit.astype(F32).astype(BF16)
            halves = [dot(place, src[:, h * 512 : h * 512 + 512]).reshape(16, 8, 512) for h in range(2)]
            pack[pl.ds(i * 16, 16)] = jnp.concatenate(halves, axis=1).astype(BF16)

    packs, bufs = (x_pack, g_pack, m_pack), (x_buf, g_buf, m_buf)

    def out_copy(i, j):
        peer = peer_of(me, offset_of(j))
        return pltpu.make_async_remote_copy(
            src_ref=packs[i].at[peer],
            dst_ref=bufs[i].at[j],
            send_sem=send_sem.at[i, j],
            recv_sem=recv_sem.at[i, j],
            device_id=(g, peer),
            device_id_type=MESH,
        )

    def own_copy(i):
        return pltpu.make_async_copy(packs[i].at[me], bufs[i].at[0], own_sem.at[i])

    def over(low, high, action):
        def one(j, _):
            action(j)
            return 0

        lax.fori_loop(low, high, one, 0)

    def send_out(i, half):
        if half == 0:
            own_copy(i).start()
        over(1 + 31 * half, 32 + 32 * half, lambda j: out_copy(i, j).start())

    def take_in(i, half):
        if half == 0:
            own_copy(i).wait()
        over(1 + 31 * half, 32 + 32 * half, lambda j: out_copy(i, j).wait_recv())

    for c in fetch[:3]:
        c.wait()
    flat_row = ids_row[...] * 8 + slots_row[...]
    dispatch(cot, g_pack)
    pl.semaphore_wait(barrier, 64)
    send_out(1, 0)
    pushes = []
    for c in range(4):
        for i, (src, dst) in enumerate(zip(weights(c), (w1, w2))):
            sem = 2 * c + i
            pushes.append(to_sibling(src, dst.at[c], push_send.at[sem], push_recv.at[sem]))
    own_loads = []
    for c in range(4):
        for i, (src, dst) in enumerate(zip(weights(c), (w1, w2))):
            own_loads.append(pltpu.make_async_copy(src, dst.at[4 + c], w_sem.at[2 * c + i]))
            own_loads[-1].start()

    fetch[3].wait()
    rows32 = tokens[...].astype(F32)
    normed, _ = norm_parts(rows32)
    normed_b = normed.astype(BF16)
    for c in range(6):
        loads[c].wait()
        at = pl.ds(c * 512, 512)
        qkv[:, at] = dot(normed_b, w_qkv[:, at]).astype(BF16)
    masks = head_masks()
    for p in range(8):
        q2, k2, v2 = (qkv[:, i * 1024 + p * 128 : i * 1024 + p * 128 + 128] for i in range(3))
        probs = softmax_pair(dot_t(q2, two_heads(k2, masks)) * 0.125)
        probs = jnp.concatenate(probs, axis=1).astype(BF16)
        att[:, p * 128 : p * 128 + 128] = dot(probs, two_heads(v2, masks)).astype(BF16)
    loads[6].wait()
    resid = (rows32 + dot(att[...], w_proj[...])).astype(BF16)
    resid_buf[...] = resid
    normed2, _ = norm_parts(resid.astype(F32))
    n2b[...] = normed2.astype(BF16)
    dispatch(n2b, x_pack)
    send_out(0, 0)
    send_out(0, 1)

    leaving = [
        pltpu.make_async_copy(src, dst, out_sem.at[i])
        for i, (src, dst) in enumerate(((resid_buf, resid_out), (qkv, qkv_out), (att, att_out)))
    ]
    for c in leaving:
        c.start()
    fetch[4].wait()
    logits = dot_t(n2b[...], w_router[...])
    ids, slots = columns_of(ids_row), columns_of(slots_row)
    expert = lax.broadcasted_iota(jnp.int32, (128, 64), 1)
    picked = [
        jnp.sum(jnp.where(expert == ids[k][:, :64], logits, 0.0), axis=-1, keepdims=True)
        for k in range(2)
    ]
    top = jnp.maximum(picked[0], picked[1])
    e = [jnp.exp(a - top) for a in picked]
    lane = lax.broadcasted_iota(jnp.int32, (128, 128), 1)
    owner = lax.broadcasted_iota(jnp.int32, (64, 128), 0)
    table = jnp.zeros((64, 128), F32)
    for k in range(2):
        mix = e[k] / (e[0] + e[1])
        mix_buf[:, k * 128 : k * 128 + 128] = jnp.broadcast_to(mix, (128, 128))
        spread = jnp.where(lane == slots[k], mix, 0.0)
        high = spread.astype(BF16)
        low = (spread - high.astype(F32)).astype(BF16)
        hot = (owner == ids_row[k : k + 1, :]).astype(F32).astype(BF16)
        table = table + dot(hot, high) + dot(hot, low)
    m_pack[...] = table.reshape(64, 1, 128)
    send_out(2, 0)
    send_out(2, 1)
    send_out(1, 1)
    leaving.append(pltpu.make_async_copy(mix_buf, mix_out, out_sem.at[3]))
    leaving[3].start()

    def unpack(i, half, plain):
        def one(b):
            block = bufs[i][pl.ds(b * 8, 8)].astype(F32)
            at = pl.ds(pl.multiple_of(b * 64, 64), 64)
            for h in range(2):
                piece = block[:, h * 8 : h * 8 + 8, :].reshape(64, 512)
                plain[at, pl.ds(h * 512, 512)] = piece.astype(BF16)

        over(4 * half, 4 * half + 4, one)

    def scale(half):
        lanes = lax.broadcasted_iota(jnp.int32, (8, 8, 128), 2)
        sub = lax.broadcasted_iota(jnp.int32, (8, 8, 128), 1)

        def one(b):
            spread = jnp.broadcast_to(m_buf[pl.ds(b * 8, 8)], (8, 8, 128))
            mix = jnp.sum(jnp.where(lanes == sub, spread, 0.0), axis=2, keepdims=True).reshape(64, 1)
            at = pl.ds(pl.multiple_of(b * 64, 64), 64)
            for plain, mixed in ((xs, xm), (gs, gm)):
                mixed[at, :] = (plain[at, :].astype(F32) * mix).astype(BF16)

        over(4 * half, 4 * half + 4, one)

    def await_weights(group):
        for c in range(4 * group, 4 * group + 4):
            for n in range(2):
                if group == 1:
                    own_loads[2 * (c - 4) + n].wait()
                else:
                    pushes[2 * c + n].wait_recv()

    def add_up(rows, terms, fresh):
        total = terms[0]
        for term in terms[1:]:
            total = total + term
        acc[rows, :] = total if fresh else acc[rows, :] + total

    def forward(half, chunks, fresh):
        rows = pl.ds(half * 256, 256)
        for c in chunks:
            pre = dot(xs[rows, :], w1[c])
            cdf = 0.5 * (1.0 + lax.erf(pre * (0.5**0.5)))
            pdf = jnp.exp(-0.5 * pre * pre) * 0.3989422804014327
            hid[c, rows, :] = (pre * cdf).astype(BF16)
            dp[c, rows, :] = (cdf + pre * pdf).astype(BF16)
        add_up(rows, [dot(hid[c, rows, :], w2[c]) for c in chunks], fresh)

    def backward(half, chunks, fresh):
        rows = pl.ds(half * 256, 256)
        for c in chunks:
            d_hidden = dot_t(gs[rows, :], w2[c])
            dp[c, rows, :] = (dp[c, rows, :].astype(F32) * d_hidden).astype(BF16)
        add_up(rows, [dot_t(dp[c, rows, :], w1[c]) for c in chunks], fresh)

    def home(n, j):
        src, dst = ((pack_out, ret_out), (pack_in, ret_in))[n]
        return pltpu.make_async_remote_copy(
            src_ref=src.at[j],
            dst_ref=dst.at[me],
            send_sem=home_send.at[n, j],
            recv_sem=home_recv.at[n, j],
            device_id=(g, chip_before(me, offset_of(j))),
            device_id_type=MESH,
        )

    def own_home(n):
        src, dst = ((pack_out, ret_out), (pack_in, ret_in))[n]
        return pltpu.make_async_copy(src.at[0], dst.at[me], own_sem.at[3 + n])

    def send_home(n, half):
        target = (pack_out, pack_in)[n]

        def one(b):
            value = acc[pl.ds(pl.multiple_of(b * 64, 64), 64), :].reshape(8, 8, 1024)
            both = jnp.concatenate([value[:, :, :512], value[:, :, 512:]], axis=1)
            target[pl.ds(b * 8, 8)] = both.astype(BF16)

        over(4 * half, 4 * half + 4, one)
        if half == 0:
            own_home(n).start()
        over(1 + 31 * half, 32 + 32 * half, lambda j: home(n, j).start())

    swaps = []

    def share(src, dst):
        n = len(swaps)
        swaps.append(to_sibling(src, dst, sib_send.at[n], sib_recv.at[n]))

    low, high, every = range(4), range(4, 8), range(8)
    for half in range(2):
        rows = pl.ds(half * 256, 256)
        take_in(0, half)
        unpack(0, half, xs)
        if half == 0:
            await_weights(1)
            forward(half, high, True)
            await_weights(0)
            forward(half, low, False)
        else:
            forward(half, every, True)
        send_home(0, half)
        share(hid.at[pl.ds(0, 4), rows, :], hid_sib.at[:, rows, :])
    take_in(2, 0)
    take_in(2, 1)
    for half in range(2):
        rows = pl.ds(half * 256, 256)
        take_in(1, half)
        unpack(1, half, gs)
        scale(half)
        share(xm.at[rows, :], xm_sib.at[rows, :])
        share(gm.at[rows, :], gm_sib.at[rows, :])
        if half == 0:
            backward(half, every, True)
            send_home(1, half)
            share(dp.at[pl.ds(0, 4), rows, :], dp_sib.at[:, rows, :])
        else:
            backward(half, low, True)
            share(dp.at[pl.ds(0, 4), rows, :], dp_sib.at[:, rows, :])
            backward(half, high, False)
            send_home(1, half)

    def grad_copy(c, which):
        at = pl.ds(pl.multiple_of(c * CHUNK, CHUNK), CHUNK)
        source = stage1 if which == 0 else stage2
        target = grad_w1.at[:, at] if which == 0 else grad_w2.at[at, :]
        return pltpu.make_async_copy(source, target, grad_sem.at[which])

    for c in swaps:
        c.wait_recv()

    def grads(c):
        @pl.when(c > 0)
        def _():
            grad_copy(c - 1, 0).wait()

        for r in range(2):
            rows = pl.ds(r * 512, 512)
            stage1[rows, :] = (
                t_dot(xm[:, rows], dp[4 + c]) + t_dot(xm_sib[:, rows], dp_sib[c])
            ).astype(BF16)
        grad_copy(c, 0).start()

        @pl.when(c > 0)
        def _():
            grad_copy(c - 1, 1).wait()

        for r in range(2):
            columns = pl.ds(r * 256, 256)
            stage2[columns, :] = (
                t_dot(hid[4 + c, :, columns], gm[...]) + t_dot(hid_sib[c, :, columns], gm_sib[...])
            ).astype(BF16)
        grad_copy(c, 1).start()

    over(0, 4, grads)
    grad_copy(3, 0).wait()
    grad_copy(3, 1).wait()

    def finish(j):
        for i in range(3):
            out_copy(i, j).wait_send()
        for n in range(2):
            home(n, j).wait()

    over(1, 64, finish)
    for n in range(2):
        own_home(n).wait()
    for c in leaving:
        c.wait()
    for c in started:
        c.wait_send()


def run_layer(*args):
    sem = pltpu.SemaphoreType.DMA
    shape = jax.ShapeDtypeStruct
    return pl.pallas_call(
        layer_kernel,
        out_shape=[
            shape((64, 16, 512), BF16),
            shape((64, 16, 512), BF16),
            shape((128, 1024), BF16),
            shape((128, 3072), BF16),
            shape((128, 1024), BF16),
            shape((128, 256), F32),
            shape((1024, 2048), BF16),
            shape((2048, 1024), BF16),
        ],
        in_specs=[HBM] * 9,
        out_specs=[HBM] * 8,
        scratch_shapes=[
            pltpu.VMEM((128, 1024), BF16),
            pltpu.VMEM((128, 1024), BF16),
            pltpu.VMEM((2, 128), jnp.int32),
            pltpu.VMEM((2, 128), jnp.int32),
            pltpu.VMEM((64, 1024), BF16),
            pltpu.VMEM((128, 1024), BF16),
            pltpu.VMEM((128, 3072), BF16),
            pltpu.VMEM((128, 1024), BF16),
            pltpu.VMEM((128, 256), F32),
            pltpu.VMEM((1024, 3072), BF16),
            pltpu.VMEM((1024, 1024), BF16),
            pltpu.VMEM((128, 1024), BF16),
            pltpu.VMEM((64, 16, 512), BF16),
            pltpu.VMEM((64, 16, 512), BF16),
            pltpu.VMEM((64, 1, 128), F32),
            pltpu.VMEM((8, 1024, CHUNK), BF16),
            pltpu.VMEM((8, CHUNK, 1024), BF16),
            pltpu.VMEM((512, 1024), BF16),
            pltpu.VMEM((512, 1024), BF16),
            pltpu.VMEM((512, 1024), BF16),
            pltpu.VMEM((512, 1024), BF16),
            pltpu.VMEM((8, 512, CHUNK), BF16),
            pltpu.VMEM((8, 512, CHUNK), BF16),
            pltpu.VMEM((512, 1024), F32),
            pltpu.VMEM((64, 16, 512), BF16),
            pltpu.VMEM((64, 16, 512), BF16),
            pltpu.VMEM((512, 1024), BF16),
            pltpu.VMEM((512, 1024), BF16),
            pltpu.VMEM((4, 512, CHUNK), BF16),
            pltpu.VMEM((4, 512, CHUNK), BF16),
            pltpu.VMEM((1024, CHUNK), BF16),
            pltpu.VMEM((CHUNK, 1024), BF16),
            pltpu.VMEM((64, 16, 512), BF16),
            pltpu.VMEM((64, 16, 512), BF16),
            pltpu.VMEM((64, 1, 128), F32),
            sem((12,)),
            sem((8,)),
            sem((8,)),
            sem((8,)),
            sem((3, 64)),
            sem((3, 64)),
            sem((2, 64)),
            sem((2, 64)),
            sem((5,)),
            sem((4,)),
            sem((8,)),
            sem((8,)),
            sem((2,)),
        ],
        compiler_params=pltpu.CompilerParams(
            collective_id=1, has_side_effects=True, vmem_limit_bytes=63 * 2**20
        ),
        name="layer",
    )(*args)


ORDERS = ((16, 4, 1), (4, 1, 16), (1, 16, 4))
EARLY, LATE = 384, 512


def along(me, stride, k):
    at = (me // stride) % 4
    return me - at * stride + ((at + k) % 4) * stride


def natural_row(order, j):
    row = j % 8
    for at, stride in zip((128, 32, 8), ORDERS[order]):
        row = row + ((j // at) % 4) * (stride * 8)
    return row


def finish_kernel(*refs):
    layer_out, grad_tokens, sum_qkv, sum_proj, sum_router = refs[13:18]
    tokens, resid, att, ids_row, slots_row, ret_out, cot, mix, ret_in, w_router, w_proj, qkv, w_qkv = refs[18:31]
    rows, half_in, half_send, lhs, rhs, d_att = refs[31:37]
    parts, first, mid, second, last, third = (refs[37 + 3 * i : 40 + 3 * i] for i in range(6))
    w_sem, pair_send, pair_recv, send_sem, recv_sem = refs[55:60]
    g = lax.axis_index("group")
    me = lax.axis_index("dev")
    barrier = pltpu.get_barrier_semaphore()
    pl.semaphore_signal(barrier, inc=1, device_id=(1 - g, me), device_id_type=MESH)
    for stride in (16, 4, 1):
        for k in (1, 2, 3):
            pl.semaphore_signal(
                barrier, inc=1, device_id=(g, along(me, stride, k)), device_id_type=MESH
            )
    loads = [pltpu.make_async_copy(refs[i], refs[18 + i], w_sem.at[i]) for i in range(13)]
    for c in loads:
        c.start()

    def arrive(*which):
        for i in which:
            loads[i].wait()

    started = []

    def swap(i, src, dst):
        c = pltpu.make_async_remote_copy(
            src_ref=src,
            dst_ref=dst,
            send_sem=pair_send.at[i],
            recv_sem=pair_recv.at[i],
            device_id=(1 - g, me),
            device_id_type=MESH,
        )
        c.start()
        started.append(c)
        return c

    arrive(0, 1, 2)
    normed1, rstd1 = norm_parts(tokens[...].astype(F32))
    resid_f = resid[...].astype(F32)
    normed2, rstd2 = norm_parts(resid_f)
    half_in[0] = normed1.astype(BF16)
    half_in[1] = att[...]
    half_in[2] = normed2.astype(BF16)
    column = lax.broadcasted_iota(jnp.int32, (512, 512), 1)
    position = lax.broadcasted_iota(jnp.int32, (512, 512), 0)
    mine = pl.ds(pl.multiple_of(g * 512, 512), 512)
    theirs = pl.ds(pl.multiple_of((1 - g) * 512, 512), 512)
    for order in range(3):
        turn = (column == natural_row(order, position)).astype(F32).astype(BF16)
        for which in range(3):
            if which == 2 and order < 2:
                continue
            i = order * 2 + which
            lhs[i, :, 0:128] = dot_t(turn, half_in[which, :, mine]).astype(BF16)
            half_send[i] = dot_t(turn, half_in[which, :, theirs]).astype(BF16)
    pl.semaphore_wait(barrier, 10)
    lhs_swap = [swap(i, half_send.at[i], lhs.at[i, :, pl.ds(128, 128)]) for i in range(7)]

    def unpack(src):
        def one(i, _):
            block = src[pl.ds(i * 8, 8)].astype(F32)
            at = pl.ds(pl.multiple_of(i * 64, 64), 64)
            for h in range(2):
                piece = block[:, h * 8 : h * 8 + 8, :].reshape(64, 512)
                rows[at, pl.ds(h * 512, 512)] = piece.astype(BF16)
            return 0

        lax.fori_loop(0, 8, one, 0)

    arrive(3, 4, 5, 6, 7)
    slot = lax.broadcasted_iota(jnp.int32, (128, 128), 1)
    ids, slots = columns_of(ids_row), columns_of(slots_row)
    place = []
    for k in range(2):
        flat = ids[k] * 8 + slots[k]
        hits = [(slot + i * 128 == flat).astype(F32).astype(BF16) for i in range(4)]
        place.append(jnp.concatenate(hits, axis=1))
    place = jnp.concatenate(place, axis=0)
    grad = cot[...].astype(F32)
    mixing = [mix[:, k * 128 : k * 128 + 1] for k in range(2)]
    unpack(ret_out)
    pair = dot(place, rows[...])
    pair = [pair[:128], pair[128:]]
    layer_out[...] = (resid_f + mixing[0] * pair[0] + mixing[1] * pair[1]).astype(BF16)
    d_mix = [jnp.sum(grad * a, axis=-1, keepdims=True) for a in pair]
    centre = mixing[0] * d_mix[0] + mixing[1] * d_mix[1]
    expert = lax.broadcasted_iota(jnp.int32, (128, 128), 1)
    d_logits = sum(
        jnp.where(expert == ids[k], mixing[k] * (d_mix[k] - centre), 0.0) for k in range(2)
    ).astype(BF16)
    arrive(8, 9)
    unpack(ret_in)
    pair = dot(place, rows[...])
    d_normed2 = (
        mixing[0] * pair[:128] + mixing[1] * pair[128:] + dot(d_logits[:, :64], w_router[...])
    )
    d_resid = grad + norm_backward(normed2, rstd2, d_normed2)
    own_rows, sib_rows = pl.ds(0, 128), pl.ds(128, 128)
    rhs[own_rows, pl.ds(3072, 1024)] = d_resid.astype(BF16)
    rhs[own_rows, pl.ds(4096, 128)] = d_logits
    tail = pl.ds(3072, 1152)
    early_swap = swap(7, rhs.at[own_rows, tail], rhs.at[sib_rows, tail])
    arrive(10)
    d_att[...] = dot_t(rhs[own_rows, pl.ds(3072, 1024)], w_proj[...]).astype(BF16)

    def place_of(phase, order):
        return (me // ORDERS[order][phase]) % 4

    def launch(phase, late, order, src, dst):
        stride = ORDERS[order][phase]
        at = place_of(phase, order)
        group = []
        for k in (1, 2, 3):
            sem = ((phase * 3 + late) * 3 + order) * 3 + k - 1
            c = pltpu.make_async_remote_copy(
                src_ref=src.at[order, (at + k) % 4],
                dst_ref=dst.at[order, k - 1],
                send_sem=send_sem.at[sem],
                recv_sem=recv_sem.at[sem],
                device_id=(g, along(me, stride, k)),
                device_id_type=MESH,
            )
            c.start()
            group.append(c)
        started.extend(group)
        return group

    def sum_one(late, order, arriving):
        for c in arriving:
            c.wait_recv()
        at = place_of(0, order)
        for q in range(4):
            piece = pl.ds(q * 32, 32)
            total = parts[late][order, at, piece, :].astype(F32)
            for k in range(3):
                total = total + first[late][order, k, piece, :].astype(F32)
            mid[late][order, q] = total.astype(BF16)
        return launch(1, late, order, mid[late], second[late])

    def sum_two(late, order, arriving):
        for c in arriving:
            c.wait_recv()
        total = mid[late][order, place_of(1, order)].astype(F32)
        for k in range(3):
            total = total + second[late][order, k].astype(F32)
        for q in range(4):
            last[late][order, q] = total[q * 8 : q * 8 + 8, :]
        return launch(2, late, order, last[late], third[late])

    def sum_three(late, order, arriving):
        for c in arriving:
            c.wait_recv()
        total = last[late][order, place_of(2, order)]
        for k in range(3):
            total = total + third[late][order, k]
        return total

    for c in lhs_swap:
        c.wait_recv()
    early_swap.wait_recv()
    early = []
    for order in range(3):
        for r in range(4):
            for left, at, width in (
                (order * 2 + 1, 0, EARLY if order < 2 else 256),
                (6, 256, 128),
            ):
                if left == 6 and order < 2:
                    continue
                value = dot(
                    lhs[left, r * 128 : r * 128 + 128, :],
                    rhs[:, 3072 + order * EARLY + at : 3072 + order * EARLY + at + width],
                )
                parts[0][order, r, :, pl.ds(at, width)] = value.astype(BF16)
        early.append(launch(0, 0, order, parts[0], first[0]))

    arrive(11)
    masks = head_masks()
    def heads(p):
        q2, k2, v2 = (qkv[:, i * 1024 + p * 128 : i * 1024 + p * 128 + 128] for i in range(3))
        d2 = d_att[:, p * 128 : p * 128 + 128]
        k_two, v_two = two_heads(k2, masks), two_heads(v2, masks)
        probs = softmax_pair(dot_t(q2, k_two) * 0.125)
        d_probs = dot_t(d2, v_two)
        d_scores = []
        for h in range(2):
            one = d_probs[:, h * 128 : h * 128 + 128]
            one = probs[h] * (one - jnp.sum(probs[h] * one, axis=-1, keepdims=True))
            d_scores.append(one * 0.125)
        d_scores = jnp.concatenate(d_scores, axis=1).astype(BF16)
        probs = jnp.concatenate(probs, axis=1).astype(BF16)
        d_k = t_dot(d_scores, q2)
        d_v = t_dot(probs, d2)
        rhs[own_rows, pl.ds(p * 128, 128)] = dot(d_scores, k_two).astype(BF16)
        rhs[own_rows, pl.ds(1024 + p * 128, 128)] = (
            d_k[:128] * masks[0] + d_k[128:] * masks[1]
        ).astype(BF16)
        rhs[own_rows, pl.ds(2048 + p * 128, 128)] = (
            d_v[:128] * masks[0] + d_v[128:] * masks[1]
        ).astype(BF16)

    def columns(stage, order):
        return pl.ds(order * 1024 + stage * LATE, LATE)

    def swap_late(stage):
        return [
            swap(
                8 + stage * 3 + order,
                rhs.at[own_rows, columns(stage, order)],
                rhs.at[sib_rows, columns(stage, order)],
            )
            for order in range(3)
        ]

    def launch_late(stage, arriving):
        out = []
        for order in range(3):
            arriving[order].wait_recv()
            for r in range(4):
                value = dot(lhs[order * 2, r * 128 : r * 128 + 128, :], rhs[:, columns(stage, order)])
                parts[1 + stage][order, r] = value.astype(BF16)
            out.append(launch(0, 1 + stage, order, parts[1 + stage], first[1 + stage]))
        return out

    for p in range(4):
        heads(p)
    late_swap = [swap_late(0)]
    for p in range(4, 6):
        heads(p)
    late = [launch_late(0, late_swap[0])]
    for p in range(6, 8):
        heads(p)
    late_swap.append(swap_late(1))
    early = [sum_one(0, order, early[order]) for order in range(3)]
    late.append(launch_late(1, late_swap[1]))
    arrive(12)
    d_normed1 = dot_t(rhs[own_rows, pl.ds(0, 3072)], w_qkv[...])
    grad_tokens[...] = (d_resid + norm_backward(normed1, rstd1, d_normed1)).astype(BF16)
    early = [sum_two(0, order, early[order]) for order in range(3)]
    late[0] = [sum_one(1, order, late[0][order]) for order in range(3)]
    late[1] = [sum_one(2, order, late[1][order]) for order in range(3)]
    sum_proj[:, 0:384] = sum_three(0, 0, early[0])
    sum_proj[:, 384:768] = sum_three(0, 1, early[1])
    tail_sum = sum_three(0, 2, early[2])
    sum_proj[:, 768:1024] = tail_sum[:, :256]
    sum_router[...] = tail_sum[:, 256:320]
    late[0] = [sum_two(1, order, late[0][order]) for order in range(3)]
    late[1] = [sum_two(2, order, late[1][order]) for order in range(3)]
    for stage in range(2):
        for order in range(3):
            sum_qkv[:, columns(stage, order)] = sum_three(1 + stage, order, late[stage][order])
    for c in started:
        c.wait_send()


def run_finish(*args):
    sem = pltpu.SemaphoreType.DMA
    shape = jax.ShapeDtypeStruct
    scratch = [pltpu.VMEM(a.shape, a.dtype) for a in args]
    scratch += [
        pltpu.VMEM((512, 1024), BF16),
        pltpu.VMEM((3, 128, 1024), BF16),
        pltpu.VMEM((7, 512, 128), BF16),
        pltpu.VMEM((7, 512, 256), BF16),
        pltpu.VMEM((256, 4224), BF16),
        pltpu.VMEM((128, 1024), BF16),
    ]
    for lead, kind in (
        ((3, 4, 128), BF16),
        ((3, 3, 128), BF16),
        ((3, 4, 32), BF16),
        ((3, 3, 32), BF16),
        ((3, 4, 8), F32),
        ((3, 3, 8), F32),
    ):
        scratch += [pltpu.VMEM(lead + (width,), kind) for width in (EARLY, LATE, LATE)]
    scratch += [sem((13,)), sem((14,)), sem((14,)), sem((81,)), sem((81,))]
    return pl.pallas_call(
        finish_kernel,
        out_shape=[
            shape((128, 1024), BF16),
            shape((128, 1024), BF16),
            shape((8, 3072), F32),
            shape((8, 1024), F32),
            shape((8, 64), F32),
        ],
        in_specs=[HBM] * 13,
        out_specs=[VMEM] * 5,
        scratch_shapes=scratch,
        compiler_params=pltpu.CompilerParams(
            collective_id=3, has_side_effects=True, vmem_limit_bytes=53 * 2**20
        ),
        name="finish",
    )(*args)


def store_kernel(*refs):
    srcs, dsts, sems = refs[:7], refs[7:14], refs[14]
    copies = [pltpu.make_async_copy(srcs[i], dsts[i], sems.at[i]) for i in range(5)]
    for i in (5, 6):
        rows = srcs[i].shape[0] // 8
        for j in range(8):
            at = pl.ds(j * rows, rows)
            sem = sems.at[5 + (i - 5) * 8 + j]
            copies.append(pltpu.make_async_copy(srcs[i].at[at, :], dsts[i].at[at, :], sem))
    for c in copies:
        c.start()
    for c in copies:
        c.wait()


def run_store(*arrays):
    return pl.pallas_call(
        store_kernel,
        out_shape=[jax.ShapeDtypeStruct(a.shape, a.dtype) for a in arrays],
        in_specs=[VMEM] * 5 + [VMEM] * 2,
        out_specs=[HBM] * 7,
        scratch_shapes=[pltpu.SemaphoreType.DMA((21,))],
        compiler_params=pltpu.CompilerParams(vmem_limit_bytes=12 * 2**20),
        name="store",
    )(*arrays)


def shards(tokens, cotangent, expert_ids, slot_ids, w_qkv, w_proj, w_router, w_in, w_out):
    ids, slots, router = expert_ids.T, slot_ids.T, w_router.T
    returned_out, returned_in, resid, qkv, att, mix, grad_w_in, grad_w_out = run_layer(
        tokens, cotangent, ids, slots, w_qkv, w_proj, router, w_in[0], w_out[0]
    )
    small = run_finish(
        tokens, resid, att, ids, slots, returned_out, cotangent, mix, returned_in, router, w_proj, qkv, w_qkv
    )
    layer_out, grad_tokens, sum_qkv, sum_proj, sum_router, grad_w_in, grad_w_out = run_store(
        *small, grad_w_in, grad_w_out
    )
    return (
        layer_out,
        grad_tokens,
        sum_qkv,
        sum_proj,
        sum_router,
        grad_w_in[None],
        grad_w_out[None],
    )


def solution(mesh):
    return jax.shard_map(
        shards,
        mesh=mesh,
        in_specs=(
            P(("group", "dev"), None),
            P(("group", "dev"), None),
            P(("group", "dev"), None),
            P(("group", "dev"), None),
            P(),
            P(),
            P(),
            P("dev", None, "group"),
            P("dev", "group", None),
        ),
        out_specs=(
            P(("group", "dev"), None),
            P(("group", "dev"), None),
            P(("group", "dev"), None),
            P(("group", "dev"), None),
            P(("group", "dev"), None),
            P("dev", None, "group"),
            P("dev", "group", None),
        ),
        check_vma=False,
    )
```

```python
import jax
import jax.numpy as jnp
from jax import lax
from jax.experimental import pallas as pl
from jax.experimental.pallas import tpu as pltpu
from jax.sharding import PartitionSpec as P

HEADS = 16
MESH = pl.DeviceIdType.MESH
BF16 = jnp.bfloat16
F32 = jnp.float32
VMEM = pl.BlockSpec(memory_space=pltpu.VMEM)
HBM = pl.BlockSpec(memory_space=pltpu.HBM)
CHUNK = 512


def peer_of(me, k):
    y = (me // 16 + k // 16) % 4
    z = (me // 4 + k // 4) % 4
    x = (me + k) % 4
    return y * 16 + z * 4 + x


def offset_of(j):
    r = j % 32
    y = r // 8
    z = (r // 2) % 4
    x = 2 * (r % 2) + (y + z + j // 32) % 2
    return y * 16 + z * 4 + x


def chip_before(me, k):
    y = (me // 16 + 4 - k // 16) % 4
    z = (me // 4 + 4 - (k // 4) % 4) % 4
    x = (me + 4 - k % 4) % 4
    return y * 16 + z * 4 + x


def dot(a, b):
    return jnp.dot(a, b, preferred_element_type=F32)


def dot_t(a, b):
    return lax.dot_general(a, b, (((1,), (1,)), ((), ())), preferred_element_type=F32)


def t_dot(a, b):
    return lax.dot_general(a, b, (((0,), (0,)), ((), ())), preferred_element_type=F32)


def norm_parts(rows32):
    center = rows32 - jnp.mean(rows32, axis=-1, keepdims=True)
    rstd = lax.rsqrt(jnp.mean(center * center, axis=-1, keepdims=True) + 1e-05)
    return center * rstd, rstd


def norm_backward(normed, rstd, d_normed):
    mean = jnp.mean(d_normed, axis=-1, keepdims=True)
    along_it = jnp.mean(d_normed * normed, axis=-1, keepdims=True)
    return rstd * (d_normed - mean - normed * along_it)


def head_masks():
    low = lax.broadcasted_iota(jnp.int32, (128, 128), 1) < 64
    return low.astype(F32), 1.0 - low.astype(F32)


def two_heads(pair, masks):
    wide = pair.astype(F32)
    return jnp.concatenate([wide * masks[0], wide * masks[1]], axis=0).astype(BF16)


def softmax_pair(scores):
    out = []
    for h in range(2):
        one = scores[:, h * 128 : h * 128 + 128]
        e = jnp.exp(one - jnp.max(one, axis=-1, keepdims=True))
        out.append(e / jnp.sum(e, axis=-1, keepdims=True))
    return out


def columns_of(row_ref):
    rows = row_ref[...].astype(F32)
    return [jnp.broadcast_to(rows[k : k + 1, :], (128, 128)).T.astype(jnp.int32) for k in range(2)]


def layer_kernel(*refs):
    tokens_in, cot_in, ids_in, slots_in, w_qkv_in, w_proj_in, w_router_in, w1_own, w2_own = refs[:9]
    ret_out, ret_in, resid_out, qkv_out, lhs_out, grad_w1, grad_w2 = refs[9:16]
    tokens, cot, ids_row, slots_row, w_router, resid_buf, qkv, att, lhs = refs[16:25]
    w_qkv, w_proj, n2b, x_pack, g_pack, m_pack = refs[25:31]
    w1, w2, xs, gs, xm, gm, hid, dp, acc, pack_out, pack_in = refs[31:42]
    xm_sib, gm_sib, hid_sib, dp_sib, stage1, stage2, x_buf, g_buf, m_buf = refs[42:51]
    half_in, half_send = refs[51:53]
    in_sem, w_sem, push_send, push_recv, send_sem, recv_sem, home_send, home_recv = refs[53:61]
    own_sem, out_sem, sib_send, sib_recv, grad_sem = refs[61:66]
    lhs_send, lhs_recv = refs[66:68]
    g = lax.axis_index("group")
    me = lax.axis_index("dev")
    barrier = pltpu.get_barrier_semaphore()
    pl.semaphore_signal(barrier, inc=1, device_id=(1 - g, me), device_id_type=MESH)

    def greet(k, _):
        pl.semaphore_signal(barrier, inc=1, device_id=(g, peer_of(me, k)), device_id_type=MESH)
        return 0

    lax.fori_loop(1, 64, greet, 0)
    fetch = [
        pltpu.make_async_copy(src, dst, in_sem.at[7 + i])
        for i, (src, dst) in enumerate(
            (
                (ids_in, ids_row),
                (slots_in, slots_row),
                (cot_in, cot),
                (tokens_in, tokens),
                (w_router_in, w_router),
            )
        )
    ]
    loads = []
    for c in range(6):
        at = pl.ds(c * 512, 512)
        loads.append(pltpu.make_async_copy(w_qkv_in.at[:, at], w_qkv.at[:, at], in_sem.at[c]))
    loads.append(pltpu.make_async_copy(w_proj_in, w_proj, in_sem.at[6]))
    for c in fetch[:4] + loads + fetch[4:]:
        c.start()

    started = []

    def to_sibling(src, dst, send, recv):
        c = pltpu.make_async_remote_copy(
            src_ref=src,
            dst_ref=dst,
            send_sem=send,
            recv_sem=recv,
            device_id=(1 - g, me),
            device_id_type=MESH,
        )
        c.start()
        started.append(c)
        return c

    def weights(c):
        at = pl.ds(c * CHUNK, CHUNK)
        return w1_own.at[:, at], w2_own.at[at, :]

    def dispatch(src, pack):
        for i in range(4):
            at = lax.broadcasted_iota(jnp.int32, (128, 128), 0) + i * 128
            hit = (at == flat_row[0:1, :]) | (at == flat_row[1:2, :])
            place = hit.astype(F32).astype(BF16)
            halves = [dot(place, src[:, h * 512 : h * 512 + 512]).reshape(16, 8, 512) for h in range(2)]
            pack[pl.ds(i * 16, 16)] = jnp.concatenate(halves, axis=1).astype(BF16)

    packs, bufs = (x_pack, g_pack, m_pack), (x_buf, g_buf, m_buf)

    def out_copy(i, j):
        peer = peer_of(me, offset_of(j))
        return pltpu.make_async_remote_copy(
            src_ref=packs[i].at[peer],
            dst_ref=bufs[i].at[j],
            send_sem=send_sem.at[i, j],
            recv_sem=recv_sem.at[i, j],
            device_id=(g, peer),
            device_id_type=MESH,
        )

    def own_copy(i):
        return pltpu.make_async_copy(packs[i].at[me], bufs[i].at[0], own_sem.at[i])

    def over(low, high, action):
        def one(j, _):
            action(j)
            return 0

        lax.fori_loop(low, high, one, 0)

    def send_out(i, half):
        if half == 0:
            own_copy(i).start()
        over(1 + 31 * half, 32 + 32 * half, lambda j: out_copy(i, j).start())

    def take_in(i, half):
        if half == 0:
            own_copy(i).wait()
        over(1 + 31 * half, 32 + 32 * half, lambda j: out_copy(i, j).wait_recv())

    for c in fetch[:3]:
        c.wait()
    flat_row = ids_row[...] * 8 + slots_row[...]
    dispatch(cot, g_pack)
    pl.semaphore_wait(barrier, 64)
    send_out(1, 0)
    pushes = []
    for c in range(4):
        for i, (src, dst) in enumerate(zip(weights(c), (w1, w2))):
            sem = 2 * c + i
            pushes.append(to_sibling(src, dst.at[c], push_send.at[sem], push_recv.at[sem]))
    own_loads = []
    for c in range(4):
        for i, (src, dst) in enumerate(zip(weights(c), (w1, w2))):
            own_loads.append(pltpu.make_async_copy(src, dst.at[4 + c], w_sem.at[2 * c + i]))
            own_loads[-1].start()

    fetch[3].wait()
    rows32 = tokens[...].astype(F32)
    normed, _ = norm_parts(rows32)
    normed_b = normed.astype(BF16)
    for c in range(6):
        loads[c].wait()
        at = pl.ds(c * 512, 512)
        qkv[:, at] = dot(normed_b, w_qkv[:, at]).astype(BF16)
    masks = head_masks()
    for p in range(8):
        q2, k2, v2 = (qkv[:, i * 1024 + p * 128 : i * 1024 + p * 128 + 128] for i in range(3))
        probs = softmax_pair(dot_t(q2, two_heads(k2, masks)) * 0.125)
        probs = jnp.concatenate(probs, axis=1).astype(BF16)
        att[:, p * 128 : p * 128 + 128] = dot(probs, two_heads(v2, masks)).astype(BF16)
    loads[6].wait()
    resid = (rows32 + dot(att[...], w_proj[...])).astype(BF16)
    resid_buf[...] = resid
    normed2, _ = norm_parts(resid.astype(F32))
    n2b[...] = normed2.astype(BF16)
    dispatch(n2b, x_pack)
    send_out(0, 0)
    send_out(0, 1)

    leaving = [
        pltpu.make_async_copy(src, dst, out_sem.at[i])
        for i, (src, dst) in enumerate(((resid_buf, resid_out), (qkv, qkv_out)))
    ]
    for c in leaving:
        c.start()
    fetch[4].wait()
    logits = dot_t(n2b[...], w_router[...])
    ids, slots = columns_of(ids_row), columns_of(slots_row)
    expert = lax.broadcasted_iota(jnp.int32, (128, 64), 1)
    picked = [
        jnp.sum(jnp.where(expert == ids[k][:, :64], logits, 0.0), axis=-1, keepdims=True)
        for k in range(2)
    ]
    top = jnp.maximum(picked[0], picked[1])
    e = [jnp.exp(a - top) for a in picked]
    lane = lax.broadcasted_iota(jnp.int32, (128, 128), 1)
    owner = lax.broadcasted_iota(jnp.int32, (64, 128), 0)
    table = jnp.zeros((64, 128), F32)
    for k in range(2):
        mix = e[k] / (e[0] + e[1])
        spread = jnp.where(lane == slots[k], mix, 0.0)
        high = spread.astype(BF16)
        low = (spread - high.astype(F32)).astype(BF16)
        hot = (owner == ids_row[k : k + 1, :]).astype(F32).astype(BF16)
        table = table + dot(hot, high) + dot(hot, low)
    m_pack[...] = table.reshape(64, 1, 128)
    send_out(2, 0)
    send_out(2, 1)
    send_out(1, 1)

    half_in[0] = normed_b
    half_in[1] = att[...]
    half_in[2] = n2b[...]
    column = lax.broadcasted_iota(jnp.int32, (512, 512), 1)
    position = lax.broadcasted_iota(jnp.int32, (512, 512), 0)
    mine = pl.ds(pl.multiple_of(g * 512, 512), 512)
    theirs = pl.ds(pl.multiple_of((1 - g) * 512, 512), 512)
    for order in range(3):
        turn = (column == natural_row(order, position)).astype(F32).astype(BF16)
        for which in range(3 if order == 2 else 2):
            i = order * 2 + which
            lhs[i, :, 0:128] = dot_t(turn, half_in[which, :, mine]).astype(BF16)
            half_send[i] = dot_t(turn, half_in[which, :, theirs]).astype(BF16)
    lhs_swap = [
        to_sibling(half_send.at[i], lhs.at[i, :, pl.ds(128, 128)], lhs_send.at[i], lhs_recv.at[i])
        for i in range(7)
    ]

    def unpack(i, half, plain):
        def one(b):
            block = bufs[i][pl.ds(b * 8, 8)].astype(F32)
            at = pl.ds(pl.multiple_of(b * 64, 64), 64)
            for h in range(2):
                piece = block[:, h * 8 : h * 8 + 8, :].reshape(64, 512)
                plain[at, pl.ds(h * 512, 512)] = piece.astype(BF16)

        over(4 * half, 4 * half + 4, one)

    def scale(half):
        lanes = lax.broadcasted_iota(jnp.int32, (8, 8, 128), 2)
        sub = lax.broadcasted_iota(jnp.int32, (8, 8, 128), 1)

        def one(b):
            spread = jnp.broadcast_to(m_buf[pl.ds(b * 8, 8)], (8, 8, 128))
            mix = jnp.sum(jnp.where(lanes == sub, spread, 0.0), axis=2, keepdims=True).reshape(64, 1)
            at = pl.ds(pl.multiple_of(b * 64, 64), 64)
            for plain, mixed in ((xs, xm), (gs, gm)):
                mixed[at, :] = (plain[at, :].astype(F32) * mix).astype(BF16)

        over(4 * half, 4 * half + 4, one)

    def await_weights(group):
        for c in range(4 * group, 4 * group + 4):
            for n in range(2):
                if group == 1:
                    own_loads[2 * (c - 4) + n].wait()
                else:
                    pushes[2 * c + n].wait_recv()

    def add_up(rows, terms, fresh):
        total = terms[0]
        for term in terms[1:]:
            total = total + term
        acc[rows, :] = total if fresh else acc[rows, :] + total

    def forward(half, chunks, fresh):
        rows = pl.ds(half * 256, 256)
        for c in chunks:
            pre = dot(xs[rows, :], w1[c])
            cdf = 0.5 * (1.0 + lax.erf(pre * (0.5**0.5)))
            pdf = jnp.exp(-0.5 * pre * pre) * 0.3989422804014327
            hid[c, rows, :] = (pre * cdf).astype(BF16)
            dp[c, rows, :] = (cdf + pre * pdf).astype(BF16)
        add_up(rows, [dot(hid[c, rows, :], w2[c]) for c in chunks], fresh)

    def backward(half, chunks, fresh):
        rows = pl.ds(half * 256, 256)
        for c in chunks:
            d_hidden = dot_t(gs[rows, :], w2[c])
            dp[c, rows, :] = (dp[c, rows, :].astype(F32) * d_hidden).astype(BF16)
        add_up(rows, [dot_t(dp[c, rows, :], w1[c]) for c in chunks], fresh)

    def home(n, j):
        src, dst = ((pack_out, ret_out), (pack_in, ret_in))[n]
        return pltpu.make_async_remote_copy(
            src_ref=src.at[j],
            dst_ref=dst.at[me],
            send_sem=home_send.at[n, j],
            recv_sem=home_recv.at[n, j],
            device_id=(g, chip_before(me, offset_of(j))),
            device_id_type=MESH,
        )

    def own_home(n):
        src, dst = ((pack_out, ret_out), (pack_in, ret_in))[n]
        return pltpu.make_async_copy(src.at[0], dst.at[me], own_sem.at[3 + n])

    def send_home(n, half):
        target = (pack_out, pack_in)[n]

        def one(b):
            value = acc[pl.ds(pl.multiple_of(b * 64, 64), 64), :].reshape(8, 8, 1024)
            both = jnp.concatenate([value[:, :, :512], value[:, :, 512:]], axis=1)
            target[pl.ds(b * 8, 8)] = both.astype(BF16)

        over(4 * half, 4 * half + 4, one)
        if half == 0:
            own_home(n).start()
        over(1 + 31 * half, 32 + 32 * half, lambda j: home(n, j).start())

    swaps = []

    def share(src, dst):
        n = len(swaps)
        swaps.append(to_sibling(src, dst, sib_send.at[n], sib_recv.at[n]))

    low, high, every = range(4), range(4, 8), range(8)
    for half in range(2):
        rows = pl.ds(half * 256, 256)
        take_in(0, half)
        unpack(0, half, xs)
        if half == 0:
            await_weights(1)
            forward(half, high, True)
            await_weights(0)
            forward(half, low, False)
        else:
            forward(half, every, True)
        send_home(0, half)
        share(hid.at[pl.ds(0, 4), rows, :], hid_sib.at[:, rows, :])
    for c in lhs_swap:
        c.wait_recv()
    leaving.append(pltpu.make_async_copy(lhs, lhs_out, out_sem.at[2]))
    leaving[2].start()
    take_in(2, 0)
    take_in(2, 1)
    for half in range(2):
        rows = pl.ds(half * 256, 256)
        take_in(1, half)
        unpack(1, half, gs)
        scale(half)
        share(xm.at[rows, :], xm_sib.at[rows, :])
        share(gm.at[rows, :], gm_sib.at[rows, :])
        if half == 0:
            backward(half, every, True)
            send_home(1, half)
            share(dp.at[pl.ds(0, 4), rows, :], dp_sib.at[:, rows, :])
        else:
            backward(half, low, True)
            share(dp.at[pl.ds(0, 4), rows, :], dp_sib.at[:, rows, :])
            backward(half, high, False)
            send_home(1, half)

    def grad_copy(c, which):
        at = pl.ds(pl.multiple_of(c * CHUNK, CHUNK), CHUNK)
        source = stage1 if which == 0 else stage2
        target = grad_w1.at[:, at] if which == 0 else grad_w2.at[at, :]
        return pltpu.make_async_copy(source, target, grad_sem.at[which])

    for c in swaps:
        c.wait_recv()

    def grads(c):
        @pl.when(c > 0)
        def _():
            grad_copy(c - 1, 0).wait()

        for r in range(2):
            rows = pl.ds(r * 512, 512)
            stage1[rows, :] = (
                t_dot(xm[:, rows], dp[4 + c]) + t_dot(xm_sib[:, rows], dp_sib[c])
            ).astype(BF16)
        grad_copy(c, 0).start()

        @pl.when(c > 0)
        def _():
            grad_copy(c - 1, 1).wait()

        for r in range(2):
            columns = pl.ds(r * 256, 256)
            stage2[columns, :] = (
                t_dot(hid[4 + c, :, columns], gm[...]) + t_dot(hid_sib[c, :, columns], gm_sib[...])
            ).astype(BF16)
        grad_copy(c, 1).start()

    over(0, 4, grads)
    grad_copy(3, 0).wait()
    grad_copy(3, 1).wait()

    def finish(j):
        for i in range(3):
            out_copy(i, j).wait_send()
        for n in range(2):
            home(n, j).wait()

    over(1, 64, finish)
    for n in range(2):
        own_home(n).wait()
    for c in leaving:
        c.wait()
    for c in started:
        c.wait_send()


def run_layer(*args):
    sem = pltpu.SemaphoreType.DMA
    shape = jax.ShapeDtypeStruct
    return pl.pallas_call(
        layer_kernel,
        out_shape=[
            shape((64, 16, 512), BF16),
            shape((64, 16, 512), BF16),
            shape((128, 1024), BF16),
            shape((128, 3072), BF16),
            shape((7, 512, 256), BF16),
            shape((1024, 2048), BF16),
            shape((2048, 1024), BF16),
        ],
        in_specs=[HBM] * 9,
        out_specs=[HBM] * 7,
        scratch_shapes=[
            pltpu.VMEM((128, 1024), BF16),
            pltpu.VMEM((128, 1024), BF16),
            pltpu.VMEM((2, 128), jnp.int32),
            pltpu.VMEM((2, 128), jnp.int32),
            pltpu.VMEM((64, 1024), BF16),
            pltpu.VMEM((128, 1024), BF16),
            pltpu.VMEM((128, 3072), BF16),
            pltpu.VMEM((128, 1024), BF16),
            pltpu.VMEM((7, 512, 256), BF16),
            pltpu.VMEM((1024, 3072), BF16),
            pltpu.VMEM((1024, 1024), BF16),
            pltpu.VMEM((128, 1024), BF16),
            pltpu.VMEM((64, 16, 512), BF16),
            pltpu.VMEM((64, 16, 512), BF16),
            pltpu.VMEM((64, 1, 128), F32),
            pltpu.VMEM((8, 1024, CHUNK), BF16),
            pltpu.VMEM((8, CHUNK, 1024), BF16),
            pltpu.VMEM((512, 1024), BF16),
            pltpu.VMEM((512, 1024), BF16),
            pltpu.VMEM((512, 1024), BF16),
            pltpu.VMEM((512, 1024), BF16),
            pltpu.VMEM((8, 512, CHUNK), BF16),
            pltpu.VMEM((8, 512, CHUNK), BF16),
            pltpu.VMEM((512, 1024), F32),
            pltpu.VMEM((64, 16, 512), BF16),
            pltpu.VMEM((64, 16, 512), BF16),
            pltpu.VMEM((512, 1024), BF16),
            pltpu.VMEM((512, 1024), BF16),
            pltpu.VMEM((4, 512, CHUNK), BF16),
            pltpu.VMEM((4, 512, CHUNK), BF16),
            pltpu.VMEM((1024, CHUNK), BF16),
            pltpu.VMEM((CHUNK, 1024), BF16),
            pltpu.VMEM((64, 16, 512), BF16),
            pltpu.VMEM((64, 16, 512), BF16),
            pltpu.VMEM((64, 1, 128), F32),
            pltpu.VMEM((3, 128, 1024), BF16),
            pltpu.VMEM((7, 512, 128), BF16),
            sem((12,)),
            sem((8,)),
            sem((8,)),
            sem((8,)),
            sem((3, 64)),
            sem((3, 64)),
            sem((2, 64)),
            sem((2, 64)),
            sem((5,)),
            sem((3,)),
            sem((8,)),
            sem((8,)),
            sem((2,)),
            sem((7,)),
            sem((7,)),
        ],
        compiler_params=pltpu.CompilerParams(
            collective_id=1, has_side_effects=True, vmem_limit_bytes=63 * 2**20
        ),
        name="layer",
    )(*args)


ORDERS = ((16, 4, 1), (4, 1, 16), (1, 16, 4))
EARLY, LATE = 384, 512


def along(me, stride, k):
    at = (me // stride) % 4
    return me - at * stride + ((at + k) % 4) * stride


def natural_row(order, j):
    row = j % 8
    for at, stride in zip((128, 32, 8), ORDERS[order]):
        row = row + ((j // at) % 4) * (stride * 8)
    return row


def finish_kernel(*refs):
    layer_out, grad_tokens, sum_qkv, sum_proj, sum_router = refs[12:17]
    tokens, resid, ids_row, slots_row, ret_out, cot, w_router, ret_in, lhs, w_proj, qkv, w_qkv = refs[17:29]
    rows, rhs, d_att = refs[29:32]
    parts, first, mid, second, last, third = (refs[32 + 3 * i : 35 + 3 * i] for i in range(6))
    w_sem, pair_send, pair_recv, send_sem, recv_sem = refs[50:55]
    g = lax.axis_index("group")
    me = lax.axis_index("dev")
    barrier = pltpu.get_barrier_semaphore()
    pl.semaphore_signal(barrier, inc=1, device_id=(1 - g, me), device_id_type=MESH)
    for stride in (16, 4, 1):
        for k in (1, 2, 3):
            pl.semaphore_signal(
                barrier, inc=1, device_id=(g, along(me, stride, k)), device_id_type=MESH
            )
    loads = [pltpu.make_async_copy(refs[i], refs[17 + i], w_sem.at[i]) for i in range(12)]
    for c in loads:
        c.start()

    def arrive(*which):
        for i in which:
            loads[i].wait()

    started = []

    def swap(i, src, dst):
        c = pltpu.make_async_remote_copy(
            src_ref=src,
            dst_ref=dst,
            send_sem=pair_send.at[i],
            recv_sem=pair_recv.at[i],
            device_id=(1 - g, me),
            device_id_type=MESH,
        )
        c.start()
        started.append(c)
        return c

    arrive(0, 1)
    normed1, rstd1 = norm_parts(tokens[...].astype(F32))
    resid_f = resid[...].astype(F32)
    normed2, rstd2 = norm_parts(resid_f)

    def unpack(src):
        def one(i, _):
            block = src[pl.ds(i * 8, 8)].astype(F32)
            at = pl.ds(pl.multiple_of(i * 64, 64), 64)
            for h in range(2):
                piece = block[:, h * 8 : h * 8 + 8, :].reshape(64, 512)
                rows[at, pl.ds(h * 512, 512)] = piece.astype(BF16)
            return 0

        lax.fori_loop(0, 8, one, 0)

    arrive(2, 3, 4, 5, 6)
    slot = lax.broadcasted_iota(jnp.int32, (128, 128), 1)
    ids, slots = columns_of(ids_row), columns_of(slots_row)
    place = []
    for k in range(2):
        flat = ids[k] * 8 + slots[k]
        hits = [(slot + i * 128 == flat).astype(F32).astype(BF16) for i in range(4)]
        place.append(jnp.concatenate(hits, axis=1))
    place = jnp.concatenate(place, axis=0)
    grad = cot[...].astype(F32)
    logits = dot_t(normed2.astype(BF16), w_router[...])
    picked = [
        jnp.sum(jnp.where(slot[:, :64] == ids[k][:, :64], logits, 0.0), axis=-1, keepdims=True)
        for k in range(2)
    ]
    top = jnp.maximum(picked[0], picked[1])
    e = [jnp.exp(a - top) for a in picked]
    mixing = [a / (e[0] + e[1]) for a in e]
    unpack(ret_out)
    pair = dot(place, rows[...])
    pair = [pair[:128], pair[128:]]
    layer_out[...] = (resid_f + mixing[0] * pair[0] + mixing[1] * pair[1]).astype(BF16)
    d_mix = [jnp.sum(grad * a, axis=-1, keepdims=True) for a in pair]
    centre = mixing[0] * d_mix[0] + mixing[1] * d_mix[1]
    expert = lax.broadcasted_iota(jnp.int32, (128, 128), 1)
    d_logits = sum(
        jnp.where(expert == ids[k], mixing[k] * (d_mix[k] - centre), 0.0) for k in range(2)
    ).astype(BF16)
    arrive(7)
    unpack(ret_in)
    pair = dot(place, rows[...])
    d_normed2 = (
        mixing[0] * pair[:128] + mixing[1] * pair[128:] + dot(d_logits[:, :64], w_router[...])
    )
    d_resid = grad + norm_backward(normed2, rstd2, d_normed2)
    own_rows, sib_rows = pl.ds(0, 128), pl.ds(128, 128)
    rhs[own_rows, pl.ds(3072, 1024)] = d_resid.astype(BF16)
    rhs[own_rows, pl.ds(4096, 128)] = d_logits
    tail = pl.ds(3072, 1152)
    pl.semaphore_wait(barrier, 10)
    early_swap = swap(7, rhs.at[own_rows, tail], rhs.at[sib_rows, tail])
    arrive(9)
    d_att[...] = dot_t(rhs[own_rows, pl.ds(3072, 1024)], w_proj[...]).astype(BF16)

    def place_of(phase, order):
        return (me // ORDERS[order][phase]) % 4

    def launch(phase, late, order, src, dst):
        stride = ORDERS[order][phase]
        at = place_of(phase, order)
        group = []
        for k in (1, 2, 3):
            sem = ((phase * 3 + late) * 3 + order) * 3 + k - 1
            c = pltpu.make_async_remote_copy(
                src_ref=src.at[order, (at + k) % 4],
                dst_ref=dst.at[order, k - 1],
                send_sem=send_sem.at[sem],
                recv_sem=recv_sem.at[sem],
                device_id=(g, along(me, stride, k)),
                device_id_type=MESH,
            )
            c.start()
            group.append(c)
        started.extend(group)
        return group

    def sum_one(late, order, arriving):
        for c in arriving:
            c.wait_recv()
        at = place_of(0, order)
        for q in range(4):
            piece = pl.ds(q * 32, 32)
            total = parts[late][order, at, piece, :].astype(F32)
            for k in range(3):
                total = total + first[late][order, k, piece, :].astype(F32)
            mid[late][order, q] = total.astype(BF16)
        return launch(1, late, order, mid[late], second[late])

    def sum_two(late, order, arriving):
        for c in arriving:
            c.wait_recv()
        total = mid[late][order, place_of(1, order)].astype(F32)
        for k in range(3):
            total = total + second[late][order, k].astype(F32)
        for q in range(4):
            last[late][order, q] = total[q * 8 : q * 8 + 8, :]
        return launch(2, late, order, last[late], third[late])

    def sum_three(late, order, arriving):
        for c in arriving:
            c.wait_recv()
        total = last[late][order, place_of(2, order)]
        for k in range(3):
            total = total + third[late][order, k]
        return total

    arrive(8)
    early_swap.wait_recv()
    early = []
    for order in range(3):
        for r in range(4):
            for left, at, width in (
                (order * 2 + 1, 0, EARLY if order < 2 else 256),
                (6, 256, 128),
            ):
                if left == 6 and order < 2:
                    continue
                value = dot(
                    lhs[left, r * 128 : r * 128 + 128, :],
                    rhs[:, 3072 + order * EARLY + at : 3072 + order * EARLY + at + width],
                )
                parts[0][order, r, :, pl.ds(at, width)] = value.astype(BF16)
        early.append(launch(0, 0, order, parts[0], first[0]))

    arrive(10)
    masks = head_masks()
    def heads(p):
        q2, k2, v2 = (qkv[:, i * 1024 + p * 128 : i * 1024 + p * 128 + 128] for i in range(3))
        d2 = d_att[:, p * 128 : p * 128 + 128]
        k_two, v_two = two_heads(k2, masks), two_heads(v2, masks)
        probs = softmax_pair(dot_t(q2, k_two) * 0.125)
        d_probs = dot_t(d2, v_two)
        d_scores = []
        for h in range(2):
            one = d_probs[:, h * 128 : h * 128 + 128]
            one = probs[h] * (one - jnp.sum(probs[h] * one, axis=-1, keepdims=True))
            d_scores.append(one * 0.125)
        d_scores = jnp.concatenate(d_scores, axis=1).astype(BF16)
        probs = jnp.concatenate(probs, axis=1).astype(BF16)
        d_k = t_dot(d_scores, q2)
        d_v = t_dot(probs, d2)
        rhs[own_rows, pl.ds(p * 128, 128)] = dot(d_scores, k_two).astype(BF16)
        rhs[own_rows, pl.ds(1024 + p * 128, 128)] = (
            d_k[:128] * masks[0] + d_k[128:] * masks[1]
        ).astype(BF16)
        rhs[own_rows, pl.ds(2048 + p * 128, 128)] = (
            d_v[:128] * masks[0] + d_v[128:] * masks[1]
        ).astype(BF16)

    def columns(stage, order):
        return pl.ds(order * 1024 + stage * LATE, LATE)

    def swap_late(stage):
        return [
            swap(
                8 + stage * 3 + order,
                rhs.at[own_rows, columns(stage, order)],
                rhs.at[sib_rows, columns(stage, order)],
            )
            for order in range(3)
        ]

    def launch_late(stage, arriving):
        out = []
        for order in range(3):
            arriving[order].wait_recv()
            for r in range(4):
                value = dot(lhs[order * 2, r * 128 : r * 128 + 128, :], rhs[:, columns(stage, order)])
                parts[1 + stage][order, r] = value.astype(BF16)
            out.append(launch(0, 1 + stage, order, parts[1 + stage], first[1 + stage]))
        return out

    for p in range(4):
        heads(p)
    late_swap = [swap_late(0)]
    for p in range(4, 6):
        heads(p)
    late = [launch_late(0, late_swap[0])]
    for p in range(6, 8):
        heads(p)
    late_swap.append(swap_late(1))
    early = [sum_one(0, order, early[order]) for order in range(3)]
    late.append(launch_late(1, late_swap[1]))
    arrive(11)
    d_normed1 = dot_t(rhs[own_rows, pl.ds(0, 3072)], w_qkv[...])
    grad_tokens[...] = (d_resid + norm_backward(normed1, rstd1, d_normed1)).astype(BF16)
    early = [sum_two(0, order, early[order]) for order in range(3)]
    late[0] = [sum_one(1, order, late[0][order]) for order in range(3)]
    late[1] = [sum_one(2, order, late[1][order]) for order in range(3)]
    sum_proj[:, 0:384] = sum_three(0, 0, early[0])
    sum_proj[:, 384:768] = sum_three(0, 1, early[1])
    tail_sum = sum_three(0, 2, early[2])
    sum_proj[:, 768:1024] = tail_sum[:, :256]
    sum_router[...] = tail_sum[:, 256:320]
    late[0] = [sum_two(1, order, late[0][order]) for order in range(3)]
    late[1] = [sum_two(2, order, late[1][order]) for order in range(3)]
    for stage in range(2):
        for order in range(3):
            sum_qkv[:, columns(stage, order)] = sum_three(1 + stage, order, late[stage][order])
    for c in started:
        c.wait_send()


def run_finish(*args):
    sem = pltpu.SemaphoreType.DMA
    shape = jax.ShapeDtypeStruct
    scratch = [pltpu.VMEM(a.shape, a.dtype) for a in args]
    scratch += [
        pltpu.VMEM((512, 1024), BF16),
        pltpu.VMEM((256, 4224), BF16),
        pltpu.VMEM((128, 1024), BF16),
    ]
    for lead, kind in (
        ((3, 4, 128), BF16),
        ((3, 3, 128), BF16),
        ((3, 4, 32), BF16),
        ((3, 3, 32), BF16),
        ((3, 4, 8), F32),
        ((3, 3, 8), F32),
    ):
        scratch += [pltpu.VMEM(lead + (width,), kind) for width in (EARLY, LATE, LATE)]
    scratch += [sem((12,)), sem((14,)), sem((14,)), sem((81,)), sem((81,))]
    return pl.pallas_call(
        finish_kernel,
        out_shape=[
            shape((128, 1024), BF16),
            shape((128, 1024), BF16),
            shape((8, 3072), F32),
            shape((8, 1024), F32),
            shape((8, 64), F32),
        ],
        in_specs=[HBM] * 12,
        out_specs=[VMEM] * 5,
        scratch_shapes=scratch,
        compiler_params=pltpu.CompilerParams(
            collective_id=3, has_side_effects=True, vmem_limit_bytes=53 * 2**20
        ),
        name="finish",
    )(*args)


def store_kernel(*refs):
    srcs, dsts, sems = refs[:7], refs[7:14], refs[14]
    copies = [pltpu.make_async_copy(srcs[i], dsts[i], sems.at[i]) for i in range(5)]
    for i in (5, 6):
        rows = srcs[i].shape[0] // 8
        for j in range(8):
            at = pl.ds(j * rows, rows)
            sem = sems.at[5 + (i - 5) * 8 + j]
            copies.append(pltpu.make_async_copy(srcs[i].at[at, :], dsts[i].at[at, :], sem))
    for c in copies:
        c.start()
    for c in copies:
        c.wait()


def run_store(*arrays):
    return pl.pallas_call(
        store_kernel,
        out_shape=[jax.ShapeDtypeStruct(a.shape, a.dtype) for a in arrays],
        in_specs=[VMEM] * 5 + [VMEM] * 2,
        out_specs=[HBM] * 7,
        scratch_shapes=[pltpu.SemaphoreType.DMA((21,))],
        compiler_params=pltpu.CompilerParams(vmem_limit_bytes=12 * 2**20),
        name="store",
    )(*arrays)


def shards(tokens, cotangent, expert_ids, slot_ids, w_qkv, w_proj, w_router, w_in, w_out):
    ids, slots, router = expert_ids.T, slot_ids.T, w_router.T
    returned_out, returned_in, resid, qkv, lhs, grad_w_in, grad_w_out = run_layer(
        tokens, cotangent, ids, slots, w_qkv, w_proj, router, w_in[0], w_out[0]
    )
    small = run_finish(
        tokens, resid, ids, slots, returned_out, cotangent, router, returned_in, lhs, w_proj, qkv, w_qkv
    )
    layer_out, grad_tokens, sum_qkv, sum_proj, sum_router, grad_w_in, grad_w_out = run_store(
        *small, grad_w_in, grad_w_out
    )
    return (
        layer_out,
        grad_tokens,
        sum_qkv,
        sum_proj,
        sum_router,
        grad_w_in[None],
        grad_w_out[None],
    )


def solution(mesh):
    return jax.shard_map(
        shards,
        mesh=mesh,
        in_specs=(
            P(("group", "dev"), None),
            P(("group", "dev"), None),
            P(("group", "dev"), None),
            P(("group", "dev"), None),
            P(),
            P(),
            P(),
            P("dev", None, "group"),
            P("dev", "group", None),
        ),
        out_specs=(
            P(("group", "dev"), None),
            P(("group", "dev"), None),
            P(("group", "dev"), None),
            P(("group", "dev"), None),
            P(("group", "dev"), None),
            P("dev", None, "group"),
            P("dev", "group", None),
        ),
        check_vma=False,
    )
```

```python
import jax
import jax.numpy as jnp
from jax import lax
from jax.experimental import pallas as pl
from jax.experimental.pallas import tpu as pltpu
from jax.sharding import PartitionSpec as P

HEADS = 16
MESH = pl.DeviceIdType.MESH
BF16 = jnp.bfloat16
F32 = jnp.float32
VMEM = pl.BlockSpec(memory_space=pltpu.VMEM)
HBM = pl.BlockSpec(memory_space=pltpu.HBM)
CHUNK = 512


def peer_of(me, k):
    y = (me // 16 + k // 16) % 4
    z = (me // 4 + k // 4) % 4
    x = (me + k) % 4
    return y * 16 + z * 4 + x


def offset_of(j):
    r = j % 32
    y = r // 8
    z = (r // 2) % 4
    x = 2 * (r % 2) + (y + z + j // 32) % 2
    return y * 16 + z * 4 + x


def chip_before(me, k):
    y = (me // 16 + 4 - k // 16) % 4
    z = (me // 4 + 4 - (k // 4) % 4) % 4
    x = (me + 4 - k % 4) % 4
    return y * 16 + z * 4 + x


def dot(a, b):
    return jnp.dot(a, b, preferred_element_type=F32)


def dot_t(a, b):
    return lax.dot_general(a, b, (((1,), (1,)), ((), ())), preferred_element_type=F32)


def t_dot(a, b):
    return lax.dot_general(a, b, (((0,), (0,)), ((), ())), preferred_element_type=F32)


def norm_parts(rows32):
    center = rows32 - jnp.mean(rows32, axis=-1, keepdims=True)
    rstd = lax.rsqrt(jnp.mean(center * center, axis=-1, keepdims=True) + 1e-05)
    return center * rstd, rstd


def norm_backward(normed, rstd, d_normed):
    mean = jnp.mean(d_normed, axis=-1, keepdims=True)
    along_it = jnp.mean(d_normed * normed, axis=-1, keepdims=True)
    return rstd * (d_normed - mean - normed * along_it)


def head_masks():
    low = lax.broadcasted_iota(jnp.int32, (128, 128), 1) < 64
    return low.astype(F32), 1.0 - low.astype(F32)


def two_heads(pair, masks):
    wide = pair.astype(F32)
    return jnp.concatenate([wide * masks[0], wide * masks[1]], axis=0).astype(BF16)


def softmax_pair(scores):
    out = []
    for h in range(2):
        one = scores[:, h * 128 : h * 128 + 128]
        e = jnp.exp(one - jnp.max(one, axis=-1, keepdims=True))
        out.append(e / jnp.sum(e, axis=-1, keepdims=True))
    return out


def columns_of(row_ref):
    rows = row_ref[...].astype(F32)
    return [jnp.broadcast_to(rows[k : k + 1, :], (128, 128)).T.astype(jnp.int32) for k in range(2)]


def layer_kernel(*refs):
    tokens_in, cot_in, ids_in, slots_in, w_qkv_in, w_proj_in, w_router_in, w1_own, w2_own = refs[:9]
    ret_out, ret_in, resid_out, qkv_out, lhs_out, grad_w1, grad_w2 = refs[9:16]
    tokens, cot, ids_row, slots_row, w_router, resid_buf, qkv, att, lhs = refs[16:25]
    w_qkv, w_proj, n2b, x_pack, g_pack, m_pack = refs[25:31]
    w1, w2, xs, gs, xm, gm, hid, dp, acc, pack_out, pack_in = refs[31:42]
    xm_sib, gm_sib, hid_sib, dp_sib, stage1, stage2, x_buf, g_buf, m_buf = refs[42:51]
    half_in, half_send = refs[51:53]
    in_sem, w_sem, push_send, push_recv, send_sem, recv_sem, home_send, home_recv = refs[53:61]
    own_sem, out_sem, sib_send, sib_recv, grad_sem = refs[61:66]
    lhs_send, lhs_recv = refs[66:68]
    g = lax.axis_index("group")
    me = lax.axis_index("dev")
    barrier = pltpu.get_barrier_semaphore()
    pl.semaphore_signal(barrier, inc=1, device_id=(1 - g, me), device_id_type=MESH)

    def greet(k, _):
        pl.semaphore_signal(barrier, inc=1, device_id=(g, peer_of(me, k)), device_id_type=MESH)
        return 0

    lax.fori_loop(1, 64, greet, 0)
    fetch = [
        pltpu.make_async_copy(src, dst, in_sem.at[7 + i])
        for i, (src, dst) in enumerate(
            (
                (ids_in, ids_row),
                (slots_in, slots_row),
                (cot_in, cot),
                (tokens_in, tokens),
                (w_router_in, w_router),
            )
        )
    ]
    loads = []
    for c in range(6):
        at = pl.ds(c * 512, 512)
        loads.append(pltpu.make_async_copy(w_qkv_in.at[:, at], w_qkv.at[:, at], in_sem.at[c]))
    loads.append(pltpu.make_async_copy(w_proj_in, w_proj, in_sem.at[6]))
    for c in fetch[:4] + loads + fetch[4:]:
        c.start()

    started = []

    def to_sibling(src, dst, send, recv):
        c = pltpu.make_async_remote_copy(
            src_ref=src,
            dst_ref=dst,
            send_sem=send,
            recv_sem=recv,
            device_id=(1 - g, me),
            device_id_type=MESH,
        )
        c.start()
        started.append(c)
        return c

    def weights(c):
        at = pl.ds(c * CHUNK, CHUNK)
        return w1_own.at[:, at], w2_own.at[at, :]

    def dispatch(src, pack):
        for i in range(4):
            at = lax.broadcasted_iota(jnp.int32, (128, 128), 0) + i * 128
            hit = (at == flat_row[0:1, :]) | (at == flat_row[1:2, :])
            place = hit.astype(F32).astype(BF16)
            halves = [dot(place, src[:, h * 512 : h * 512 + 512]).reshape(16, 8, 512) for h in range(2)]
            pack[pl.ds(i * 16, 16)] = jnp.concatenate(halves, axis=1).astype(BF16)

    packs, bufs = (x_pack, g_pack, m_pack), (x_buf, g_buf, m_buf)

    def out_copy(i, j):
        peer = peer_of(me, offset_of(j))
        return pltpu.make_async_remote_copy(
            src_ref=packs[i].at[peer],
            dst_ref=bufs[i].at[j],
            send_sem=send_sem.at[i, j],
            recv_sem=recv_sem.at[i, j],
            device_id=(g, peer),
            device_id_type=MESH,
        )

    def own_copy(i):
        return pltpu.make_async_copy(packs[i].at[me], bufs[i].at[0], own_sem.at[i])

    def over(low, high, action):
        def one(j, _):
            action(j)
            return 0

        lax.fori_loop(low, high, one, 0)

    def send_out(i, half):
        if half == 0:
            own_copy(i).start()
        over(1 + 31 * half, 32 + 32 * half, lambda j: out_copy(i, j).start())

    def take_in(i, half):
        if half == 0:
            own_copy(i).wait()
        over(1 + 31 * half, 32 + 32 * half, lambda j: out_copy(i, j).wait_recv())

    for c in fetch[:3]:
        c.wait()
    flat_row = ids_row[...] * 8 + slots_row[...]
    dispatch(cot, g_pack)
    pl.semaphore_wait(barrier, 64)
    send_out(1, 0)
    pushes = []
    for c in range(4):
        for i, (src, dst) in enumerate(zip(weights(c), (w1, w2))):
            sem = 2 * c + i
            pushes.append(to_sibling(src, dst.at[c], push_send.at[sem], push_recv.at[sem]))
    own_loads = []
    for c in range(4):
        for i, (src, dst) in enumerate(zip(weights(c), (w1, w2))):
            own_loads.append(pltpu.make_async_copy(src, dst.at[4 + c], w_sem.at[2 * c + i]))
            own_loads[-1].start()

    fetch[3].wait()
    rows32 = tokens[...].astype(F32)
    normed, _ = norm_parts(rows32)
    normed_b = normed.astype(BF16)
    for c in range(6):
        loads[c].wait()
        at = pl.ds(c * 512, 512)
        qkv[:, at] = dot(normed_b, w_qkv[:, at]).astype(BF16)
    masks = head_masks()
    for p in range(8):
        q2, k2, v2 = (qkv[:, i * 1024 + p * 128 : i * 1024 + p * 128 + 128] for i in range(3))
        probs = softmax_pair(dot_t(q2, two_heads(k2, masks)) * 0.125)
        probs = jnp.concatenate(probs, axis=1).astype(BF16)
        att[:, p * 128 : p * 128 + 128] = dot(probs, two_heads(v2, masks)).astype(BF16)
    loads[6].wait()
    resid = (rows32 + dot(att[...], w_proj[...])).astype(BF16)
    resid_buf[...] = resid
    normed2, _ = norm_parts(resid.astype(F32))
    n2b[...] = normed2.astype(BF16)
    dispatch(n2b, x_pack)
    send_out(0, 0)
    send_out(0, 1)

    leaving = [
        pltpu.make_async_copy(src, dst, out_sem.at[i])
        for i, (src, dst) in enumerate(((resid_buf, resid_out), (qkv, qkv_out)))
    ]
    for c in leaving:
        c.start()
    fetch[4].wait()
    logits = dot_t(n2b[...], w_router[...])
    ids, slots = columns_of(ids_row), columns_of(slots_row)
    expert = lax.broadcasted_iota(jnp.int32, (128, 64), 1)
    picked = [
        jnp.sum(jnp.where(expert == ids[k][:, :64], logits, 0.0), axis=-1, keepdims=True)
        for k in range(2)
    ]
    top = jnp.maximum(picked[0], picked[1])
    e = [jnp.exp(a - top) for a in picked]
    lane = lax.broadcasted_iota(jnp.int32, (128, 128), 1)
    owner = lax.broadcasted_iota(jnp.int32, (64, 128), 0)
    table = jnp.zeros((64, 128), F32)
    for k in range(2):
        mix = e[k] / (e[0] + e[1])
        spread = jnp.where(lane == slots[k], mix, 0.0)
        high = spread.astype(BF16)
        low = (spread - high.astype(F32)).astype(BF16)
        hot = (owner == ids_row[k : k + 1, :]).astype(F32).astype(BF16)
        table = table + dot(hot, high) + dot(hot, low)
    m_pack[...] = table.reshape(64, 1, 128)
    send_out(2, 0)
    send_out(2, 1)
    send_out(1, 1)

    half_in[0] = normed_b
    half_in[1] = att[...]
    half_in[2] = n2b[...]
    column = lax.broadcasted_iota(jnp.int32, (512, 512), 1)
    position = lax.broadcasted_iota(jnp.int32, (512, 512), 0)
    mine = pl.ds(pl.multiple_of(g * 512, 512), 512)
    theirs = pl.ds(pl.multiple_of((1 - g) * 512, 512), 512)
    for order in range(3):
        turn = (column == natural_row(order, position)).astype(F32).astype(BF16)
        for which in range(3 if order == 2 else 2):
            i = order * 2 + which
            lhs[i, :, 0:128] = dot_t(turn, half_in[which, :, mine]).astype(BF16)
            half_send[i] = dot_t(turn, half_in[which, :, theirs]).astype(BF16)
    lhs_swap = [
        to_sibling(half_send.at[i], lhs.at[i, :, pl.ds(128, 128)], lhs_send.at[i], lhs_recv.at[i])
        for i in range(7)
    ]

    def unpack(i, half, plain):
        def one(b):
            block = bufs[i][pl.ds(b * 8, 8)].astype(F32)
            at = pl.ds(pl.multiple_of(b * 64, 64), 64)
            for h in range(2):
                piece = block[:, h * 8 : h * 8 + 8, :].reshape(64, 512)
                plain[at, pl.ds(h * 512, 512)] = piece.astype(BF16)

        over(4 * half, 4 * half + 4, one)

    def scale(half):
        lanes = lax.broadcasted_iota(jnp.int32, (8, 8, 128), 2)
        sub = lax.broadcasted_iota(jnp.int32, (8, 8, 128), 1)

        def one(b):
            spread = jnp.broadcast_to(m_buf[pl.ds(b * 8, 8)], (8, 8, 128))
            mix = jnp.sum(jnp.where(lanes == sub, spread, 0.0), axis=2, keepdims=True).reshape(64, 1)
            at = pl.ds(pl.multiple_of(b * 64, 64), 64)
            for plain, mixed in ((xs, xm), (gs, gm)):
                mixed[at, :] = (plain[at, :].astype(F32) * mix).astype(BF16)

        over(4 * half, 4 * half + 4, one)

    def await_weights(group):
        for c in range(4 * group, 4 * group + 4):
            for n in range(2):
                if group == 1:
                    own_loads[2 * (c - 4) + n].wait()
                else:
                    pushes[2 * c + n].wait_recv()

    def add_up(rows, terms):
        total = terms[0]
        for term in terms[1:]:
            total = total + term
        acc[rows, :] += total

    def forward(half, chunks):
        rows = pl.ds(half * 256, 256)
        for c in chunks:
            pre = dot(xs[rows, :], w1[c])
            cdf = 0.5 * (1.0 + lax.erf(pre * (0.5**0.5)))
            pdf = jnp.exp(-0.5 * pre * pre) * 0.3989422804014327
            hid[c, rows, :] = (pre * cdf).astype(BF16)
            dp[c, rows, :] = (cdf + pre * pdf).astype(BF16)
        add_up(rows, [dot(hid[c, rows, :], w2[c]) for c in chunks])

    def backward(half, chunks):
        rows = pl.ds(half * 256, 256)
        for c in chunks:
            d_hidden = dot_t(gs[rows, :], w2[c])
            dp[c, rows, :] = (dp[c, rows, :].astype(F32) * d_hidden).astype(BF16)
        add_up(rows, [dot_t(dp[c, rows, :], w1[c]) for c in chunks])

    def home(n, j):
        src, dst = ((pack_out, ret_out), (pack_in, ret_in))[n]
        return pltpu.make_async_remote_copy(
            src_ref=src.at[j],
            dst_ref=dst.at[me],
            send_sem=home_send.at[n, j],
            recv_sem=home_recv.at[n, j],
            device_id=(g, chip_before(me, offset_of(j))),
            device_id_type=MESH,
        )

    def own_home(n):
        src, dst = ((pack_out, ret_out), (pack_in, ret_in))[n]
        return pltpu.make_async_copy(src.at[0], dst.at[me], own_sem.at[3 + n])

    def send_home(n, half):
        target = (pack_out, pack_in)[n]

        def one(b):
            value = acc[pl.ds(pl.multiple_of(b * 64, 64), 64), :].reshape(8, 8, 1024)
            both = jnp.concatenate([value[:, :, :512], value[:, :, 512:]], axis=1)
            target[pl.ds(b * 8, 8)] = both.astype(BF16)

        over(4 * half, 4 * half + 4, one)
        if half == 0:
            own_home(n).start()
        over(1 + 31 * half, 32 + 32 * half, lambda j: home(n, j).start())

    swaps = []

    def sharing(src, dst):
        n = len(swaps)
        c = pltpu.make_async_remote_copy(
            src_ref=src,
            dst_ref=dst,
            send_sem=sib_send.at[n],
            recv_sem=sib_recv.at[n],
            device_id=(1 - g, me),
            device_id_type=MESH,
        )
        swaps.append(c)
        started.append(c)
        return c

    def share(src, dst):
        sharing(src, dst).start()

    def passes(half, work, before, between):
        acc[pl.ds(half * 256, 256), :] = jnp.zeros((256, 1024), F32)

        def one(i):
            for n, action in enumerate(before):
                pl.when(i == n)(action)
            work(i)
            if between is not None:
                pl.when(i == 0)(between)

        over(0, 2, one)

    for half in range(2):
        rows = pl.ds(half * 256, 256)
        take_in(0, half)
        unpack(0, half, xs)
        waits = [lambda: await_weights(1), lambda: await_weights(0)] if half == 0 else []
        passes(half, lambda i: forward(half, [4 * (1 - i) + q for q in range(4)]), waits, None)
        send_home(0, half)
        share(hid.at[pl.ds(0, 4), rows, :], hid_sib.at[:, rows, :])
    for c in lhs_swap:
        c.wait_recv()
    leaving.append(pltpu.make_async_copy(lhs, lhs_out, out_sem.at[2]))
    leaving[2].start()
    take_in(2, 0)
    take_in(2, 1)
    for half in range(2):
        rows = pl.ds(half * 256, 256)
        take_in(1, half)
        unpack(1, half, gs)
        scale(half)
        share(xm.at[rows, :], xm_sib.at[rows, :])
        share(gm.at[rows, :], gm_sib.at[rows, :])
        shared = sharing(dp.at[pl.ds(0, 4), rows, :], dp_sib.at[:, rows, :])
        passes(half, lambda i: backward(half, [4 * i + q for q in range(4)]), [], shared.start)
        send_home(1, half)

    def grad_copy(c, which):
        at = pl.ds(pl.multiple_of(c * CHUNK, CHUNK), CHUNK)
        source = stage1 if which == 0 else stage2
        target = grad_w1.at[:, at] if which == 0 else grad_w2.at[at, :]
        return pltpu.make_async_copy(source, target, grad_sem.at[which])

    for c in swaps:
        c.wait_recv()

    def grads(c):
        @pl.when(c > 0)
        def _():
            grad_copy(c - 1, 0).wait()

        for r in range(2):
            rows = pl.ds(r * 512, 512)
            stage1[rows, :] = (
                t_dot(xm[:, rows], dp[4 + c]) + t_dot(xm_sib[:, rows], dp_sib[c])
            ).astype(BF16)
        grad_copy(c, 0).start()

        @pl.when(c > 0)
        def _():
            grad_copy(c - 1, 1).wait()

        for r in range(2):
            columns = pl.ds(r * 256, 256)
            stage2[columns, :] = (
                t_dot(hid[4 + c, :, columns], gm[...]) + t_dot(hid_sib[c, :, columns], gm_sib[...])
            ).astype(BF16)
        grad_copy(c, 1).start()

    over(0, 4, grads)
    grad_copy(3, 0).wait()
    grad_copy(3, 1).wait()

    def finish(j):
        for i in range(3):
            out_copy(i, j).wait_send()
        for n in range(2):
            home(n, j).wait()

    over(1, 64, finish)
    for n in range(2):
        own_home(n).wait()
    for c in leaving:
        c.wait()
    for c in started:
        c.wait_send()


def run_layer(*args):
    sem = pltpu.SemaphoreType.DMA
    shape = jax.ShapeDtypeStruct
    return pl.pallas_call(
        layer_kernel,
        out_shape=[
            shape((64, 16, 512), BF16),
            shape((64, 16, 512), BF16),
            shape((128, 1024), BF16),
            shape((128, 3072), BF16),
            shape((7, 512, 256), BF16),
            shape((1024, 2048), BF16),
            shape((2048, 1024), BF16),
        ],
        in_specs=[HBM] * 9,
        out_specs=[HBM] * 7,
        scratch_shapes=[
            pltpu.VMEM((128, 1024), BF16),
            pltpu.VMEM((128, 1024), BF16),
            pltpu.VMEM((2, 128), jnp.int32),
            pltpu.VMEM((2, 128), jnp.int32),
            pltpu.VMEM((64, 1024), BF16),
            pltpu.VMEM((128, 1024), BF16),
            pltpu.VMEM((128, 3072), BF16),
            pltpu.VMEM((128, 1024), BF16),
            pltpu.VMEM((7, 512, 256), BF16),
            pltpu.VMEM((1024, 3072), BF16),
            pltpu.VMEM((1024, 1024), BF16),
            pltpu.VMEM((128, 1024), BF16),
            pltpu.VMEM((64, 16, 512), BF16),
            pltpu.VMEM((64, 16, 512), BF16),
            pltpu.VMEM((64, 1, 128), F32),
            pltpu.VMEM((8, 1024, CHUNK), BF16),
            pltpu.VMEM((8, CHUNK, 1024), BF16),
            pltpu.VMEM((512, 1024), BF16),
            pltpu.VMEM((512, 1024), BF16),
            pltpu.VMEM((512, 1024), BF16),
            pltpu.VMEM((512, 1024), BF16),
            pltpu.VMEM((8, 512, CHUNK), BF16),
            pltpu.VMEM((8, 512, CHUNK), BF16),
            pltpu.VMEM((512, 1024), F32),
            pltpu.VMEM((64, 16, 512), BF16),
            pltpu.VMEM((64, 16, 512), BF16),
            pltpu.VMEM((512, 1024), BF16),
            pltpu.VMEM((512, 1024), BF16),
            pltpu.VMEM((4, 512, CHUNK), BF16),
            pltpu.VMEM((4, 512, CHUNK), BF16),
            pltpu.VMEM((1024, CHUNK), BF16),
            pltpu.VMEM((CHUNK, 1024), BF16),
            pltpu.VMEM((64, 16, 512), BF16),
            pltpu.VMEM((64, 16, 512), BF16),
            pltpu.VMEM((64, 1, 128), F32),
            pltpu.VMEM((3, 128, 1024), BF16),
            pltpu.VMEM((7, 512, 128), BF16),
            sem((12,)),
            sem((8,)),
            sem((8,)),
            sem((8,)),
            sem((3, 64)),
            sem((3, 64)),
            sem((2, 64)),
            sem((2, 64)),
            sem((5,)),
            sem((3,)),
            sem((8,)),
            sem((8,)),
            sem((2,)),
            sem((7,)),
            sem((7,)),
        ],
        compiler_params=pltpu.CompilerParams(
            collective_id=1, has_side_effects=True, vmem_limit_bytes=63 * 2**20
        ),
        name="layer",
    )(*args)


ORDERS = ((16, 4, 1), (4, 1, 16), (1, 16, 4))
EARLY, LATE = 384, 512


def along(me, stride, k):
    at = (me // stride) % 4
    return me - at * stride + ((at + k) % 4) * stride


def natural_row(order, j):
    row = j % 8
    for at, stride in zip((128, 32, 8), ORDERS[order]):
        row = row + ((j // at) % 4) * (stride * 8)
    return row


def finish_kernel(*refs):
    layer_out, grad_tokens, sum_qkv, sum_proj, sum_router = refs[12:17]
    tokens, resid, ids_row, slots_row, ret_out, cot, w_router, ret_in, lhs, w_proj, qkv, w_qkv = refs[17:29]
    rows, rhs, d_att = refs[29:32]
    parts, first, mid, second, last, third = (refs[32 + 3 * i : 35 + 3 * i] for i in range(6))
    w_sem, pair_send, pair_recv, send_sem, recv_sem = refs[50:55]
    g = lax.axis_index("group")
    me = lax.axis_index("dev")
    barrier = pltpu.get_barrier_semaphore()
    pl.semaphore_signal(barrier, inc=1, device_id=(1 - g, me), device_id_type=MESH)
    for stride in (16, 4, 1):
        for k in (1, 2, 3):
            pl.semaphore_signal(
                barrier, inc=1, device_id=(g, along(me, stride, k)), device_id_type=MESH
            )
    loads = [pltpu.make_async_copy(refs[i], refs[17 + i], w_sem.at[i]) for i in range(12)]
    for c in loads:
        c.start()

    def arrive(*which):
        for i in which:
            loads[i].wait()

    started = []

    def swap(i, src, dst):
        c = pltpu.make_async_remote_copy(
            src_ref=src,
            dst_ref=dst,
            send_sem=pair_send.at[i],
            recv_sem=pair_recv.at[i],
            device_id=(1 - g, me),
            device_id_type=MESH,
        )
        c.start()
        started.append(c)
        return c

    arrive(0, 1)
    normed1, rstd1 = norm_parts(tokens[...].astype(F32))
    resid_f = resid[...].astype(F32)
    normed2, rstd2 = norm_parts(resid_f)

    def unpack(src):
        def one(i, _):
            block = src[pl.ds(i * 8, 8)].astype(F32)
            at = pl.ds(pl.multiple_of(i * 64, 64), 64)
            for h in range(2):
                piece = block[:, h * 8 : h * 8 + 8, :].reshape(64, 512)
                rows[at, pl.ds(h * 512, 512)] = piece.astype(BF16)
            return 0

        lax.fori_loop(0, 8, one, 0)

    arrive(2, 3, 4, 5, 6)
    slot = lax.broadcasted_iota(jnp.int32, (128, 128), 1)
    ids, slots = columns_of(ids_row), columns_of(slots_row)
    place = []
    for k in range(2):
        flat = ids[k] * 8 + slots[k]
        hits = [(slot + i * 128 == flat).astype(F32).astype(BF16) for i in range(4)]
        place.append(jnp.concatenate(hits, axis=1))
    place = jnp.concatenate(place, axis=0)
    grad = cot[...].astype(F32)
    logits = dot_t(normed2.astype(BF16), w_router[...])
    picked = [
        jnp.sum(jnp.where(slot[:, :64] == ids[k][:, :64], logits, 0.0), axis=-1, keepdims=True)
        for k in range(2)
    ]
    top = jnp.maximum(picked[0], picked[1])
    e = [jnp.exp(a - top) for a in picked]
    mixing = [a / (e[0] + e[1]) for a in e]
    unpack(ret_out)
    pair = dot(place, rows[...])
    pair = [pair[:128], pair[128:]]
    layer_out[...] = (resid_f + mixing[0] * pair[0] + mixing[1] * pair[1]).astype(BF16)
    d_mix = [jnp.sum(grad * a, axis=-1, keepdims=True) for a in pair]
    centre = mixing[0] * d_mix[0] + mixing[1] * d_mix[1]
    expert = lax.broadcasted_iota(jnp.int32, (128, 128), 1)
    d_logits = sum(
        jnp.where(expert == ids[k], mixing[k] * (d_mix[k] - centre), 0.0) for k in range(2)
    ).astype(BF16)
    arrive(7)
    unpack(ret_in)
    pair = dot(place, rows[...])
    d_normed2 = (
        mixing[0] * pair[:128] + mixing[1] * pair[128:] + dot(d_logits[:, :64], w_router[...])
    )
    d_resid = grad + norm_backward(normed2, rstd2, d_normed2)
    own_rows, sib_rows = pl.ds(0, 128), pl.ds(128, 128)
    rhs[own_rows, pl.ds(3072, 1024)] = d_resid.astype(BF16)
    rhs[own_rows, pl.ds(4096, 128)] = d_logits
    tail = pl.ds(3072, 1152)
    pl.semaphore_wait(barrier, 10)
    early_swap = swap(7, rhs.at[own_rows, tail], rhs.at[sib_rows, tail])
    arrive(9)
    d_att[...] = dot_t(rhs[own_rows, pl.ds(3072, 1024)], w_proj[...]).astype(BF16)

    def place_of(phase, order):
        return (me // ORDERS[order][phase]) % 4

    def launch(phase, late, order, src, dst):
        stride = ORDERS[order][phase]
        at = place_of(phase, order)
        group = []
        for k in (1, 2, 3):
            sem = ((phase * 3 + late) * 3 + order) * 3 + k - 1
            c = pltpu.make_async_remote_copy(
                src_ref=src.at[order, (at + k) % 4],
                dst_ref=dst.at[order, k - 1],
                send_sem=send_sem.at[sem],
                recv_sem=recv_sem.at[sem],
                device_id=(g, along(me, stride, k)),
                device_id_type=MESH,
            )
            c.start()
            group.append(c)
        started.extend(group)
        return group

    def sum_one(late, order, arriving):
        for c in arriving:
            c.wait_recv()
        at = place_of(0, order)
        for q in range(4):
            piece = pl.ds(q * 32, 32)
            total = parts[late][order, at, piece, :].astype(F32)
            for k in range(3):
                total = total + first[late][order, k, piece, :].astype(F32)
            mid[late][order, q] = total.astype(BF16)
        return launch(1, late, order, mid[late], second[late])

    def sum_two(late, order, arriving):
        for c in arriving:
            c.wait_recv()
        total = mid[late][order, place_of(1, order)].astype(F32)
        for k in range(3):
            total = total + second[late][order, k].astype(F32)
        for q in range(4):
            last[late][order, q] = total[q * 8 : q * 8 + 8, :]
        return launch(2, late, order, last[late], third[late])

    def sum_three(late, order, arriving):
        for c in arriving:
            c.wait_recv()
        total = last[late][order, place_of(2, order)]
        for k in range(3):
            total = total + third[late][order, k]
        return total

    arrive(8)
    early_swap.wait_recv()
    early = []
    for order in range(3):
        for r in range(4):
            for left, at, width in (
                (order * 2 + 1, 0, EARLY if order < 2 else 256),
                (6, 256, 128),
            ):
                if left == 6 and order < 2:
                    continue
                value = dot(
                    lhs[left, r * 128 : r * 128 + 128, :],
                    rhs[:, 3072 + order * EARLY + at : 3072 + order * EARLY + at + width],
                )
                parts[0][order, r, :, pl.ds(at, width)] = value.astype(BF16)
        early.append(launch(0, 0, order, parts[0], first[0]))

    arrive(10)
    masks = head_masks()
    def heads(p):
        q2, k2, v2 = (qkv[:, i * 1024 + p * 128 : i * 1024 + p * 128 + 128] for i in range(3))
        d2 = d_att[:, p * 128 : p * 128 + 128]
        k_two, v_two = two_heads(k2, masks), two_heads(v2, masks)
        probs = softmax_pair(dot_t(q2, k_two) * 0.125)
        d_probs = dot_t(d2, v_two)
        d_scores = []
        for h in range(2):
            one = d_probs[:, h * 128 : h * 128 + 128]
            one = probs[h] * (one - jnp.sum(probs[h] * one, axis=-1, keepdims=True))
            d_scores.append(one * 0.125)
        d_scores = jnp.concatenate(d_scores, axis=1).astype(BF16)
        probs = jnp.concatenate(probs, axis=1).astype(BF16)
        d_k = t_dot(d_scores, q2)
        d_v = t_dot(probs, d2)
        rhs[own_rows, pl.ds(p * 128, 128)] = dot(d_scores, k_two).astype(BF16)
        rhs[own_rows, pl.ds(1024 + p * 128, 128)] = (
            d_k[:128] * masks[0] + d_k[128:] * masks[1]
        ).astype(BF16)
        rhs[own_rows, pl.ds(2048 + p * 128, 128)] = (
            d_v[:128] * masks[0] + d_v[128:] * masks[1]
        ).astype(BF16)

    def columns(stage, order):
        return pl.ds(order * 1024 + stage * LATE, LATE)

    def swap_late(stage):
        return [
            swap(
                8 + stage * 3 + order,
                rhs.at[own_rows, columns(stage, order)],
                rhs.at[sib_rows, columns(stage, order)],
            )
            for order in range(3)
        ]

    def launch_late(stage, arriving):
        out = []
        for order in range(3):
            arriving[order].wait_recv()
            for r in range(4):
                value = dot(lhs[order * 2, r * 128 : r * 128 + 128, :], rhs[:, columns(stage, order)])
                parts[1 + stage][order, r] = value.astype(BF16)
            out.append(launch(0, 1 + stage, order, parts[1 + stage], first[1 + stage]))
        return out

    for p in range(4):
        heads(p)
    late_swap = [swap_late(0)]
    for p in range(4, 6):
        heads(p)
    late = [launch_late(0, late_swap[0])]
    for p in range(6, 8):
        heads(p)
    late_swap.append(swap_late(1))
    early = [sum_one(0, order, early[order]) for order in range(3)]
    late.append(launch_late(1, late_swap[1]))
    arrive(11)
    d_normed1 = dot_t(rhs[own_rows, pl.ds(0, 3072)], w_qkv[...])
    grad_tokens[...] = (d_resid + norm_backward(normed1, rstd1, d_normed1)).astype(BF16)
    early = [sum_two(0, order, early[order]) for order in range(3)]
    late[0] = [sum_one(1, order, late[0][order]) for order in range(3)]
    late[1] = [sum_one(2, order, late[1][order]) for order in range(3)]
    sum_proj[:, 0:384] = sum_three(0, 0, early[0])
    sum_proj[:, 384:768] = sum_three(0, 1, early[1])
    tail_sum = sum_three(0, 2, early[2])
    sum_proj[:, 768:1024] = tail_sum[:, :256]
    sum_router[...] = tail_sum[:, 256:320]
    late[0] = [sum_two(1, order, late[0][order]) for order in range(3)]
    late[1] = [sum_two(2, order, late[1][order]) for order in range(3)]
    for stage in range(2):
        for order in range(3):
            sum_qkv[:, columns(stage, order)] = sum_three(1 + stage, order, late[stage][order])
    for c in started:
        c.wait_send()


def run_finish(*args):
    sem = pltpu.SemaphoreType.DMA
    shape = jax.ShapeDtypeStruct
    scratch = [pltpu.VMEM(a.shape, a.dtype) for a in args]
    scratch += [
        pltpu.VMEM((512, 1024), BF16),
        pltpu.VMEM((256, 4224), BF16),
        pltpu.VMEM((128, 1024), BF16),
    ]
    for lead, kind in (
        ((3, 4, 128), BF16),
        ((3, 3, 128), BF16),
        ((3, 4, 32), BF16),
        ((3, 3, 32), BF16),
        ((3, 4, 8), F32),
        ((3, 3, 8), F32),
    ):
        scratch += [pltpu.VMEM(lead + (width,), kind) for width in (EARLY, LATE, LATE)]
    scratch += [sem((12,)), sem((14,)), sem((14,)), sem((81,)), sem((81,))]
    return pl.pallas_call(
        finish_kernel,
        out_shape=[
            shape((128, 1024), BF16),
            shape((128, 1024), BF16),
            shape((8, 3072), F32),
            shape((8, 1024), F32),
            shape((8, 64), F32),
        ],
        in_specs=[HBM] * 12,
        out_specs=[VMEM] * 5,
        scratch_shapes=scratch,
        compiler_params=pltpu.CompilerParams(
            collective_id=3, has_side_effects=True, vmem_limit_bytes=53 * 2**20
        ),
        name="finish",
    )(*args)


def store_kernel(*refs):
    srcs, dsts, sems = refs[:7], refs[7:14], refs[14]
    copies = [pltpu.make_async_copy(srcs[i], dsts[i], sems.at[i]) for i in range(5)]
    for i in (5, 6):
        rows = srcs[i].shape[0] // 8
        for j in range(8):
            at = pl.ds(j * rows, rows)
            sem = sems.at[5 + (i - 5) * 8 + j]
            copies.append(pltpu.make_async_copy(srcs[i].at[at, :], dsts[i].at[at, :], sem))
    for c in copies:
        c.start()
    for c in copies:
        c.wait()


def run_store(*arrays):
    return pl.pallas_call(
        store_kernel,
        out_shape=[jax.ShapeDtypeStruct(a.shape, a.dtype) for a in arrays],
        in_specs=[VMEM] * 5 + [VMEM] * 2,
        out_specs=[HBM] * 7,
        scratch_shapes=[pltpu.SemaphoreType.DMA((21,))],
        compiler_params=pltpu.CompilerParams(vmem_limit_bytes=12 * 2**20),
        name="store",
    )(*arrays)


def shards(tokens, cotangent, expert_ids, slot_ids, w_qkv, w_proj, w_router, w_in, w_out):
    ids, slots, router = expert_ids.T, slot_ids.T, w_router.T
    returned_out, returned_in, resid, qkv, lhs, grad_w_in, grad_w_out = run_layer(
        tokens, cotangent, ids, slots, w_qkv, w_proj, router, w_in[0], w_out[0]
    )
    small = run_finish(
        tokens, resid, ids, slots, returned_out, cotangent, router, returned_in, lhs, w_proj, qkv, w_qkv
    )
    layer_out, grad_tokens, sum_qkv, sum_proj, sum_router, grad_w_in, grad_w_out = run_store(
        *small, grad_w_in, grad_w_out
    )
    return (
        layer_out,
        grad_tokens,
        sum_qkv,
        sum_proj,
        sum_router,
        grad_w_in[None],
        grad_w_out[None],
    )


def solution(mesh):
    return jax.shard_map(
        shards,
        mesh=mesh,
        in_specs=(
            P(("group", "dev"), None),
            P(("group", "dev"), None),
            P(("group", "dev"), None),
            P(("group", "dev"), None),
            P(),
            P(),
            P(),
            P("dev", None, "group"),
            P("dev", "group", None),
        ),
        out_specs=(
            P(("group", "dev"), None),
            P(("group", "dev"), None),
            P(("group", "dev"), None),
            P(("group", "dev"), None),
            P(("group", "dev"), None),
            P("dev", None, "group"),
            P("dev", "group", None),
        ),
        check_vma=False,
    )
```
